32 devices in a mesh: prompt: 4 (over y, x), resp: 8 (over z, core).
Axes of the slice: x: 2, y: 2, z: 4, core: 2. Of those that a mesh axis runs over, the one named last changes fastest.
Arguments:
- prompt_rows: bfloat16 [2048, 5120], P(('prompt', 'resp')), may hold values from -6 to 6
- key_weight: bfloat16 [5120, 512], replicated, may hold values from -0.078125 to 0.078125
- value_weight: bfloat16 [5120, 512], replicated, may hold values from -0.078125 to 0.078125
- queries: bfloat16 [4096, 2560], P(('prompt', 'resp')), may hold values from -180 to 180
- own_keys: bfloat16 [4096, 512], P(('prompt', 'resp')), may hold values from -6 to 6
- own_values: bfloat16 [4096, 512], P(('prompt', 'resp')), may hold values from -6 to 6
- out_grad: bfloat16 [4096, 2560], P(('prompt', 'resp')), may hold values from -24 to 24
- first_length: int32 [32], P(('prompt', 'resp')), may hold values from 16 to 112
- resp_prompt: int32 [32, 2], P(('prompt', 'resp')), may hold values from 0 to 3
Outputs:
- query_grad: bfloat16 [4096, 2560], P(('prompt', 'resp'))
- key_grad: bfloat16 [4096, 512], P(('prompt', 'resp'))
- value_grad: bfloat16 [4096, 512], P(('prompt', 'resp'))
- prompt_grad: bfloat16 [2048, 5120], P(('prompt', 'resp'))
The draws below stay inside these ranges and needn't reach their ends.
All inputs are finite; a program needn't handle non-finite values.
Results may differ from the reference program's by a relative error of at most 0.038.
Values may be sent and summed in bfloat16 or wider, within the bound.
No kernel may reach another device: no remote copies, remote signals or barrier semaphores. Data moves between devices by JAX's collectives and lax.ppermute only.
A program may use at most 192 MiB of HBM per device.

```python
import jax
import jax.numpy as jnp
from jax import lax

D = 5120
H = 20
KVH = 4
E = 128
PLEN = 512
ROWS_DEV = 128
PROMPTS = 4
TOKENS = 4096
PROMPT_TOKENS = 2048
N_PROMPT = 4
N_RESP = 8
DEVICES = 32


def own_base(key):
    return jnp.clip(jax.random.normal(jax.random.fold_in(key, 11), (TOKENS, KVH * E), jnp.float32), -6.0, 6.0)


def draw_own_keys(key, part):
    base = own_base(key)
    return base.astype(jnp.bfloat16)


def draw_queries(key, part):
    key = jax.random.fold_in(key, 5)
    noise = 2.5 * jnp.clip(jax.random.normal(key, (TOKENS, H * E), jnp.float32), -6.0, 6.0)
    return noise.astype(jnp.bfloat16)


def plant(drawn, own_key, smallest, largest):
    longest = drawn.shape.index(max(drawn.shape))
    spots = []
    for shift in (0, 1):
        where = [jax.random.randint(jax.random.fold_in(own_key, axis), (), 0, length) for axis, length in enumerate(drawn.shape)]
        where[longest] = (where[longest] + shift) % drawn.shape[longest]
        spots.append(tuple(where))
    return drawn.at[spots[0]].set(smallest).at[spots[1]].set(largest)


def block_levels(key, dims, cuts, low, high):
    loudness = 1.0
    for dim, shards_of in cuts:
        draws = jax.random.uniform(jax.random.fold_in(jax.random.fold_in(key, 6), dim), (shards_of,), jnp.float32, low / len(cuts), high / len(cuts))
        loudness = loudness * jnp.repeat(jnp.exp(draws), dims[dim] // shards_of).reshape((-1,) + (1,) * (len(dims) - 1 - dim))
    return loudness


def scatter_about(rng, extent, scale, reach, cuts=(), kind=jnp.bfloat16):
    array = jax.random.normal(rng, extent, jnp.float32) * scale
    if len(cuts) > 0:
        array = block_levels(rng, extent, cuts, -0.22, 0.18) * array
    return jnp.clip(array, min=-reach, max=reach).astype(kind)


def setup_inputs(seed: int = 0) -> dict:
    streams_of = jax.random.split(jax.random.key(seed), 10)
    return {
        "prompt_rows": scatter_about(streams_of[0], (PROMPT_TOKENS, D), 1.0, 6.0, ((0, 32),)),
        "key_weight": scatter_about(streams_of[1], (D, KVH * E), D ** -0.5, 0.078125),
        "value_weight": scatter_about(streams_of[2], (D, KVH * E), D ** -0.5, 0.078125),
        "queries": draw_queries(jax.random.fold_in(streams_of[9], 71), 0),
        "own_keys": draw_own_keys(jax.random.fold_in(streams_of[9], 71), 0),
        "own_values": scatter_about(streams_of[5], (TOKENS, KVH * E), 1.0, 6.0, ((0, 32),)),
        "out_grad": scatter_about(streams_of[6], (TOKENS, H * E), 4.0, 24.0, ((0, 32),)),
        "first_length": plant(jax.random.randint(streams_of[7], (N_PROMPT * N_RESP,), ROWS_DEV // 8, ROWS_DEV - ROWS_DEV // 8 + 1), jax.random.fold_in(streams_of[7], 1), ROWS_DEV // 8, (ROWS_DEV - ROWS_DEV // 8 + 1) - 1).astype(jnp.int32),
        "resp_prompt": plant(jax.random.randint(streams_of[8], (N_PROMPT * N_RESP, 2), 0, PROMPTS), jax.random.fold_in(streams_of[8], 1), 0, PROMPTS - 1).astype(jnp.int32),
    }


def block_scores(query_heads, key_block):
    keys = key_block.reshape(key_block.shape[0], query_heads.shape[1], E).astype(jnp.float32)
    return jnp.einsum("rkge,jke->kgrj", query_heads.astype(jnp.float32), keys, precision=lax.Precision.HIGHEST) * (E ** -0.5)


def value_products(grad_heads, value_block):
    values = value_block.reshape(value_block.shape[0], grad_heads.shape[1], E).astype(jnp.float32)
    return jnp.einsum("rkge,jke->kgrj", grad_heads.astype(jnp.float32), values, precision=lax.Precision.HIGHEST)


def attend(query_heads, grad_heads, blocks):
    row_max = None
    row_total = None
    for key_block, value_block, visible in blocks:
        scores = jnp.where(visible, block_scores(query_heads, key_block), -jnp.inf)
        block_max = jnp.max(scores, axis=-1)
        if row_max is None:
            row_max = block_max
            row_total = jnp.sum(jnp.exp(scores - row_max[..., None]), axis=-1)
        else:
            new_max = jnp.maximum(row_max, block_max)
            row_total = row_total * jnp.exp(row_max - new_max) + jnp.sum(jnp.exp(scores - new_max[..., None]), axis=-1)
            row_max = new_max

    def probabilities(key_block, visible):
        scores = block_scores(query_heads, key_block)
        return jnp.where(visible, jnp.exp(scores - row_max[..., None]) / row_total[..., None], 0.0)

    delta = jnp.zeros_like(row_max)
    for key_block, value_block, visible in blocks:
        probs_low = probabilities(key_block, visible).astype(jnp.bfloat16)
        delta = delta + jnp.sum(probs_low.astype(jnp.float32) * value_products(grad_heads, value_block), axis=-1)

    query_sum = jnp.zeros(query_heads.shape, jnp.float32)
    block_grads = []
    for key_block, value_block, visible in blocks:
        probs = probabilities(key_block, visible)
        probs_low = probs.astype(jnp.bfloat16).astype(jnp.float32)
        dscores = (probs * (value_products(grad_heads, value_block) - delta[..., None])).astype(jnp.bfloat16).astype(jnp.float32)
        keys = key_block.reshape(key_block.shape[0], query_heads.shape[1], E).astype(jnp.float32)
        query_sum = query_sum + jnp.einsum("kgrj,jke->rkge", dscores, keys, precision=lax.Precision.HIGHEST)
        key_part = jnp.einsum("kgrj,rkge->jke", dscores, query_heads.astype(jnp.float32), precision=lax.Precision.HIGHEST) * (E ** -0.5)
        value_part = jnp.einsum("kgrj,rkge->jke", probs_low, grad_heads.astype(jnp.float32), precision=lax.Precision.HIGHEST)
        block_grads.append((key_part.reshape(key_block.shape[0], -1), value_part.reshape(key_block.shape[0], -1)))
    return query_sum * (E ** -0.5), block_grads


def reference(prompt_rows, key_weight, value_weight, queries, own_keys, own_values, out_grad, first_length, resp_prompt):
    prefix_keys = jnp.dot(prompt_rows, key_weight, preferred_element_type=jnp.float32).astype(jnp.bfloat16)
    prefix_values = jnp.dot(prompt_rows, value_weight, preferred_element_type=jnp.float32).astype(jnp.bfloat16)
    group_size = H // KVH

    def device_step(carry, inputs):
        key_total, value_total = carry
        query_rows, key_rows, value_rows, grad_rows, boundary, prompt_pair = inputs
        row_count = query_rows.shape[0]
        query_heads = query_rows.reshape(row_count, KVH, group_size, E)
        grad_heads = grad_rows.reshape(row_count, KVH, group_size, E)
        position = jnp.arange(row_count, dtype=jnp.int32)
        second = position >= boundary
        own_mask = (second[:, None] == second[None, :]) & (position[None, :] <= position[:, None])
        blocks = [(key_rows, value_rows, own_mask)]
        for slot_index in range(2):
            offset = (prompt_pair[slot_index] * PLEN).astype(jnp.int32)
            seen = jnp.broadcast_to((second == (slot_index == 1))[:, None], (row_count, PLEN))
            blocks.append((lax.dynamic_slice_in_dim(prefix_keys, offset, PLEN, 0), lax.dynamic_slice_in_dim(prefix_values, offset, PLEN, 0), seen))
        query_sum, block_grads = attend(query_heads, grad_heads, blocks)
        for slot_index in range(2):
            offset = (prompt_pair[slot_index] * PLEN).astype(jnp.int32)
            key_total = lax.dynamic_update_slice_in_dim(key_total, lax.dynamic_slice_in_dim(key_total, offset, PLEN, 0) + block_grads[1 + slot_index][0], offset, 0)
            value_total = lax.dynamic_update_slice_in_dim(value_total, lax.dynamic_slice_in_dim(value_total, offset, PLEN, 0) + block_grads[1 + slot_index][1], offset, 0)
        results = (query_sum.reshape(row_count, -1).astype(jnp.bfloat16), block_grads[0][0].astype(jnp.bfloat16), block_grads[0][1].astype(jnp.bfloat16))
        return (key_total, value_total), results

    inputs = (queries.reshape(DEVICES, ROWS_DEV, -1), own_keys.reshape(DEVICES, ROWS_DEV, -1), own_values.reshape(DEVICES, ROWS_DEV, -1), out_grad.reshape(DEVICES, ROWS_DEV, -1), first_length, resp_prompt)
    empty = jnp.zeros((PROMPTS * PLEN, KVH * E), jnp.float32)
    (key_total, value_total), (query_grad, key_grad, value_grad) = lax.scan(device_step, (empty, empty), inputs)
    contract = (((1,), (1,)), ((), ()))
    prompt_grad = lax.dot_general(key_total.astype(jnp.bfloat16), key_weight, contract, preferred_element_type=jnp.float32)
    prompt_grad = prompt_grad + lax.dot_general(value_total.astype(jnp.bfloat16), value_weight, contract, preferred_element_type=jnp.float32)
    return (query_grad.reshape(TOKENS, -1), key_grad.reshape(TOKENS, -1), value_grad.reshape(TOKENS, -1), prompt_grad.astype(jnp.bfloat16))
```

```python
import functools
import math

import jax
import jax.numpy as jnp
from jax import lax
from jax.experimental import pallas as pl
from jax.experimental.pallas import tpu as pltpu
from jax.sharding import PartitionSpec as P

E = 128
PLEN = 512
SCALE = E ** (-0.5)
EXP2_SCALE = SCALE * math.log2(math.e)
HIDDEN = -1e30
BF16 = jnp.bfloat16
F32 = jnp.float32
VMEM_LIMIT = 40 * 1024 * 1024

ANY = pl.BlockSpec(memory_space=pl.ANY)
SMEM = pl.BlockSpec(memory_space=pltpu.SMEM)
VMEM = pl.BlockSpec(memory_space=pltpu.VMEM)


def params(**kwargs):
    return pltpu.CompilerParams(vmem_limit_bytes=VMEM_LIMIT, **kwargs)


def cost(flops, bytes_accessed, transcendentals=0):
    return pl.CostEstimate(
        flops=int(flops), bytes_accessed=int(bytes_accessed), transcendentals=int(transcendentals)
    )


def lanes(index, width):
    return pl.ds(pl.multiple_of(index * width, 128), width)


def dot(a, b, a_dim, b_dim):
    return lax.dot_general(a, b, (((a_dim,), (b_dim,)), ((), ())), preferred_element_type=F32)


def pack_kernel(n, place_ref, q_ref, g_ref, k_ref, v_ref, *rest):
    outs, sems = rest[:n], rest[n]
    copies = []
    for j in range(n):
        head = place_ref[0] ^ j
        start = 0
        for source in (q_ref, g_ref, k_ref, v_ref):
            width = source.shape[1] // n
            copies.append(
                pltpu.make_async_copy(
                    source.at[:, lanes(head, width)],
                    outs[j].at[:, start : start + width],
                    sems.at[len(copies)],
                )
            )
            start += width
    for copy in copies:
        copy.start()
    for copy in copies:
        copy.wait()


def pack(place, queries, out_grad, own_keys, own_values, n):
    rows = queries.shape[0]
    width = (2 * queries.shape[1] + 2 * own_keys.shape[1]) // n
    return pl.pallas_call(
        functools.partial(pack_kernel, n),
        out_shape=[jax.ShapeDtypeStruct((rows, width), BF16)] * n,
        in_specs=[SMEM, ANY, ANY, ANY, ANY],
        out_specs=[ANY] * n,
        scratch_shapes=[pltpu.SemaphoreType.DMA((4 * n,))],
        compiler_params=params(),
        cost_estimate=cost(0, 4 * n * rows * width),
        name="pack_rows",
    )(place, queries, out_grad, own_keys, own_values)


def unpack_kernel(n, place_ref, *rest):
    packets, (q_ref, k_ref, v_ref), sems = rest[:n], rest[n : n + 3], rest[n + 3]
    copies = []
    for j in range(n):
        head = place_ref[0] ^ j
        start = 0
        for target in (q_ref, k_ref, v_ref):
            width = target.shape[1] // n
            copies.append(
                pltpu.make_async_copy(
                    packets[j].at[:, start : start + width],
                    target.at[:, lanes(head, width)],
                    sems.at[len(copies)],
                )
            )
            start += width
    for copy in copies:
        copy.start()
    for copy in copies:
        copy.wait()


def unpack(place, packets, q_width, kv_width):
    n = len(packets)
    rows = packets[0].shape[0]
    return pl.pallas_call(
        functools.partial(unpack_kernel, n),
        out_shape=[
            jax.ShapeDtypeStruct((rows, width), BF16) for width in (q_width, kv_width, kv_width)
        ],
        in_specs=[SMEM] + [ANY] * n,
        out_specs=[ANY] * 3,
        scratch_shapes=[pltpu.SemaphoreType.DMA((3 * n,))],
        compiler_params=params(),
        cost_estimate=cost(0, 4 * rows * (q_width + 2 * kv_width)),
        name="unpack_rows",
    )(place, *packets)


def project_kernel(n, place_ref, x_ref, kw_ref, vw_ref, *rest):
    outs, key_sum, value_sum = rest[:n], rest[n], rest[n + 1]
    step = pl.program_id(0)
    keys = dot(x_ref[...], kw_ref[...], 1, 0)
    values = dot(x_ref[...], vw_ref[...], 1, 0)

    @pl.when(step == 0)
    def _():
        key_sum[...] = keys
        value_sum[...] = values

    @pl.when(step > 0)
    def _():
        key_sum[...] += keys
        value_sum[...] += values

    @pl.when(step == pl.num_programs(0) - 1)
    def _():
        width = key_sum.shape[1] // n
        for j in range(n):
            head = lanes(place_ref[0] ^ j, width)
            outs[j][:, :width] = key_sum[:, head].astype(BF16)
            outs[j][:, width:] = value_sum[:, head].astype(BF16)


def project(place, prompt_rows, key_weight, value_weight, n, chunk=1024):
    rows, depth = prompt_rows.shape
    width = key_weight.shape[1]
    weight_spec = pl.BlockSpec((chunk, width), lambda i: (i, 0))
    return pl.pallas_call(
        functools.partial(project_kernel, n),
        grid=(depth // chunk,),
        out_shape=[jax.ShapeDtypeStruct((rows, 2 * width // n), BF16)] * n,
        in_specs=[SMEM, pl.BlockSpec((rows, chunk), lambda i: (0, i)), weight_spec, weight_spec],
        out_specs=[pl.BlockSpec((rows, 2 * width // n), lambda i: (0, 0))] * n,
        scratch_shapes=[pltpu.VMEM((rows, width), F32)] * 2,
        compiler_params=params(),
        cost_estimate=cost(4 * rows * depth * width, 4 * depth * width + 2 * rows * depth),
        name="project_prefix",
    )(place, prompt_rows, key_weight, value_weight)


def attend_kernel(n, pieces, group, rows, place_ref, *rest):
    rest = list(rest)

    def take(count):
        taken = rest[:count]
        del rest[:count]
        return taken

    meta = take(n)
    packets = take(n)
    kv_in = take(pieces)
    grads_out = take(n)
    send_out = take(pieces // 2)
    keep_out = take(pieces // 2)
    packed, keys, values, key_acc, value_acc, grads, sems, out_sems = rest
    part = PLEN // pieces

    copies = []
    for m in range(pieces):
        for index, buffer in enumerate((keys, values)):
            copies.append(
                pltpu.make_async_copy(
                    kv_in[m].at[:, :, index * E : (index + 1) * E],
                    buffer.at[:, m * part : (m + 1) * part, :],
                    sems.at[len(copies)],
                )
            )
    for j in range(n):
        copies.append(
            pltpu.make_async_copy(packets[j], packed.at[j], sems.at[len(copies)])
        )
    for copy in copies:
        copy.start()
    key_acc[...] = jnp.zeros_like(key_acc)
    value_acc[...] = jnp.zeros_like(value_acc)
    for copy in copies:
        copy.wait()

    place = place_ref[0]
    total_rows = group * rows
    row_in_column = lax.broadcasted_iota(jnp.int32, (total_rows, E), 0) & (rows - 1)
    row_in_lane = lax.broadcasted_iota(jnp.int32, (rows, total_rows), 1) & (rows - 1)
    own_key = lax.broadcasted_iota(jnp.int32, (rows, total_rows), 0)
    lane_row = lax.broadcasted_iota(jnp.int32, (E, total_rows), 1) & (rows - 1)

    def pick(j, index):
        value = meta[0][index]
        for other in range(1, n):
            value = jnp.where(j == other, meta[other][index], value)
        return value

    def member(j, carry):
        boundary = pick(j, 0)
        first_at = pick(j, 1) ^ place
        second_at = pick(j, 2) ^ place
        heads = [packed[j, :, h * E : (h + 1) * E] for h in range(2 * group + 2)]
        query = jnp.concatenate(heads[:group], axis=0)
        grad = jnp.concatenate(heads[group : 2 * group], axis=0)
        own_k, own_v = heads[2 * group], heads[2 * group + 1]
        in_first = row_in_column < boundary

        def split(x):
            x = x.astype(F32)
            return jnp.concatenate(
                [jnp.where(in_first, x, 0.0), jnp.where(in_first, 0.0, x)], axis=1
            ).astype(BF16)

        query_pair = split(query)
        grad_pair = split(grad)
        key_pair = jnp.concatenate([keys[first_at], keys[second_at]], axis=1)
        value_pair = jnp.concatenate([values[first_at], values[second_at]], axis=1)

        scores = dot(key_pair, query_pair, 1, 1)
        visible = (own_key <= row_in_lane) & ((own_key >= boundary) == (row_in_lane >= boundary))
        own_scores = jnp.where(visible, dot(own_k, query, 1, 1), HIDDEN)
        top = jnp.maximum(
            jnp.max(scores, axis=0, keepdims=True), jnp.max(own_scores, axis=0, keepdims=True)
        )
        weight = jnp.exp2((scores - top) * EXP2_SCALE)
        own_weight = jnp.exp2((own_scores - top) * EXP2_SCALE)
        inverse = 1.0 / (
            jnp.sum(weight, axis=0, keepdims=True) + jnp.sum(own_weight, axis=0, keepdims=True)
        )
        probs = weight * inverse
        own_probs = own_weight * inverse
        probs_low = probs.astype(BF16)
        own_probs_low = own_probs.astype(BF16)
        dprobs = dot(value_pair, grad_pair, 1, 1)
        own_dprobs = dot(own_v, grad, 1, 1)
        delta = jnp.sum(probs_low.astype(F32) * dprobs, axis=0, keepdims=True) + jnp.sum(
            own_probs_low.astype(F32) * own_dprobs, axis=0, keepdims=True
        )
        dscores = (probs * (dprobs - delta)).astype(BF16)
        own_dscores = (own_probs * (own_dprobs - delta)).astype(BF16)

        key_part = dot(dscores, query_pair, 1, 0)
        value_part = dot(probs_low, grad_pair, 1, 0)
        key_acc[first_at] += key_part[:, :E]
        key_acc[second_at] += key_part[:, E:]
        value_acc[first_at] += value_part[:, :E]
        value_acc[second_at] += value_part[:, E:]

        query_both = dot(key_pair, dscores, 0, 0)
        query_part = jnp.where(lane_row < boundary, query_both[:E], query_both[E:])
        query_part = (query_part + dot(own_k, own_dscores, 0, 0)) * SCALE
        for h in range(group):
            grads[j, :, h * E : (h + 1) * E] = query_part[:, h * rows : (h + 1) * rows].T.astype(
                BF16
            )
        grads[j, :, group * E : (group + 1) * E] = (dot(own_dscores, query, 1, 0) * SCALE).astype(
            BF16
        )
        grads[j, :, (group + 1) * E :] = dot(own_probs_low, grad, 1, 0).astype(BF16)
        return carry

    lax.fori_loop(0, n, member, 0)

    out_copies = [
        pltpu.make_async_copy(grads.at[j], grads_out[j], out_sems.at[j]) for j in range(n)
    ]
    for copy in out_copies:
        copy.start()
    for m in range(pieces):
        target = keep_out[m // 2] if m % 2 == 0 else send_out[m // 2]
        span = slice(m * part, (m + 1) * part)
        target[:, :, :E] = (key_acc[:, span, :] * SCALE).astype(target.dtype)
        target[:, :, E:] = value_acc[:, span, :].astype(target.dtype)
    for copy in out_copies:
        copy.wait()


def attend(place, meta, packets, kv_in):
    n = len(packets)
    pieces = len(kv_in)
    rows, packet_width = packets[0].shape
    group = (packet_width // E - 2) // 2
    part = PLEN // pieces
    out_width = (group + 2) * E
    keys = PLEN + rows
    return pl.pallas_call(
        functools.partial(attend_kernel, n, pieces, group, rows),
        out_shape=[jax.ShapeDtypeStruct((rows, out_width), BF16)] * n
        + [jax.ShapeDtypeStruct((n, part, 2 * E), BF16)] * (pieces // 2)
        + [jax.ShapeDtypeStruct((n, part, 2 * E), F32)] * (pieces // 2),
        in_specs=[SMEM] * (1 + n) + [ANY] * (n + pieces),
        out_specs=[ANY] * n + [VMEM] * pieces,
        scratch_shapes=[
            pltpu.VMEM((n, rows, packet_width), BF16),
            pltpu.VMEM((n, PLEN, E), BF16),
            pltpu.VMEM((n, PLEN, E), BF16),
            pltpu.VMEM((n, PLEN, E), F32),
            pltpu.VMEM((n, PLEN, E), F32),
            pltpu.VMEM((n, rows, out_width), BF16),
            pltpu.SemaphoreType.DMA((2 * pieces + n,)),
            pltpu.SemaphoreType.DMA((n,)),
        ],
        compiler_params=params(),
        cost_estimate=cost(
            20 * n * group * rows * keys * E, 8 * 1024 * 1024, n * group * rows * keys
        ),
        name="attend_heads",
    )(place, *meta, *packets, *kv_in)


def total_kernel(n, keep_ref, *rest):
    parts, outs = rest[:-n], rest[-n:]
    for j in range(n):
        total = keep_ref[j]
        for part in parts:
            total = total + part[j].astype(F32)
        outs[j][...] = total.astype(BF16)


def total(keep, parts):
    n, rows, width = keep.shape
    return pl.pallas_call(
        functools.partial(total_kernel, n),
        out_shape=[jax.ShapeDtypeStruct((rows, width), BF16)] * n,
        in_specs=[VMEM] * (1 + len(parts)),
        out_specs=[VMEM] * n,
        compiler_params=params(),
        cost_estimate=cost(len(parts) * keep.size, (6 + 2 * len(parts)) * keep.size),
        name="total_prefix_grads",
    )(keep, *parts)


def prompt_kernel(n, place_ref, *rest):
    shares, (kw_ref, vw_ref, out_ref, key_grad, value_grad) = rest[:n], rest[n:]

    @pl.when(pl.program_id(0) == 0)
    def _():
        width = key_grad.shape[1] // n
        for j in range(n):
            head = lanes(place_ref[0] ^ j, width)
            key_grad[:, head] = shares[j][:, :width]
            value_grad[:, head] = shares[j][:, width:]

    out_ref[...] = (
        dot(key_grad[...], kw_ref[...], 1, 1) + dot(value_grad[...], vw_ref[...], 1, 1)
    ).astype(BF16)


def prompt_gradient(place, shares, key_weight, value_weight, chunk=1024):
    n = len(shares)
    rows = shares[0].shape[0]
    depth, width = key_weight.shape
    weight_spec = pl.BlockSpec((chunk, width), lambda i: (i, 0))
    return pl.pallas_call(
        functools.partial(prompt_kernel, n),
        grid=(depth // chunk,),
        out_shape=jax.ShapeDtypeStruct((rows, depth), BF16),
        in_specs=[SMEM]
        + [pl.BlockSpec(shares[0].shape, lambda i: (0, 0))] * n
        + [weight_spec, weight_spec],
        out_specs=pl.BlockSpec((rows, chunk), lambda i: (0, i)),
        scratch_shapes=[pltpu.VMEM((rows, width), BF16)] * 2,
        compiler_params=params(),
        cost_estimate=cost(4 * rows * depth * width, 4 * depth * width + 2 * rows * depth),
        name="prompt_gradient",
    )(place, *shares, key_weight, value_weight)


def per_device(
    n_prompt,
    n_resp,
    prompt_rows,
    key_weight,
    value_weight,
    queries,
    own_keys,
    own_values,
    out_grad,
    first_length,
    resp_prompt,
):
    def swap(x, axis, size, offset):
        return lax.ppermute(x, axis, [(i, i ^ offset) for i in range(size)])

    def swap_plane(items):
        return [items[0]] + [swap(items[j], "prompt", n_prompt, j) for j in range(1, n_prompt)]

    place = lax.axis_index("prompt").astype(jnp.int32).reshape(1)
    mine = jnp.concatenate([first_length, resp_prompt.reshape(-1)])
    meta = swap_plane([mine] * n_prompt)
    packets = swap_plane(pack(place, queries, out_grad, own_keys, own_values, n_prompt))

    plane_kv = swap_plane(project(place, prompt_rows, key_weight, value_weight, n_prompt))
    kv = jnp.stack(plane_kv)
    line_kv = [kv] + [swap(kv, "resp", n_resp, m) for m in range(2, n_resp, 2)]
    kv_in = []
    for piece in line_kv:
        kv_in += [piece, swap(piece, "resp", n_resp, 1)]

    outs = attend(place, meta, packets, kv_in)
    half = n_resp // 2
    grads, send, keep = outs[:n_prompt], outs[n_prompt : n_prompt + half], outs[n_prompt + half :]
    sent = [swap(piece, "resp", n_resp, 1) for piece in send]
    arrived = [sent[0]]
    for index in range(1, half):
        chip_sum = (keep[index] + sent[index].astype(F32)).astype(BF16)
        arrived.append(swap(chip_sum, "resp", n_resp, 2 * index))
    shares = swap_plane(total(keep[0], arrived))

    query_grad, key_grad, value_grad = unpack(
        place, swap_plane(grads), queries.shape[1], own_keys.shape[1]
    )
    prompt_grad = prompt_gradient(place, shares, key_weight, value_weight)
    return (query_grad, key_grad, value_grad, prompt_grad)


def solution(mesh):
    both = P(("prompt", "resp"), None)
    return jax.shard_map(
        functools.partial(per_device, mesh.shape["prompt"], mesh.shape["resp"]),
        mesh=mesh,
        in_specs=(both, P(), P(), both, both, both, both, P(("prompt", "resp")), both),
        out_specs=(both, both, both, both),
        check_vma=False,
    )
```

```python
import functools
import math

import jax
import jax.numpy as jnp
from jax import lax
from jax.experimental import pallas as pl
from jax.experimental.pallas import tpu as pltpu
from jax.sharding import PartitionSpec as P

E = 128
PLEN = 512
SCALE = E ** (-0.5)
EXP2_SCALE = SCALE * math.log2(math.e)
HIDDEN = -1e30
BF16 = jnp.bfloat16
F32 = jnp.float32
NOTE_ROWS = 16

ANY = pl.BlockSpec(memory_space=pl.ANY)
SMEM = pl.BlockSpec(memory_space=pltpu.SMEM)
VMEM = pl.BlockSpec(memory_space=pltpu.VMEM)


def params(mebibytes=40):
    return pltpu.CompilerParams(vmem_limit_bytes=mebibytes * 1024 * 1024)


def cost(flops, bytes_accessed, transcendentals=0):
    return pl.CostEstimate(
        flops=int(flops), bytes_accessed=int(bytes_accessed), transcendentals=int(transcendentals)
    )


def dot(a, b, a_dim, b_dim):
    return lax.dot_general(a, b, (((a_dim,), (b_dim,)), ((), ())), preferred_element_type=F32)


def pack_kernel(n, length_ref, prompts_ref, q_ref, g_ref, k_ref, v_ref, out_ref, notes, sems):
    rows = q_ref.shape[0]
    lane = lax.broadcasted_iota(jnp.int32, notes.shape, 1)
    note = jnp.where(
        lane < E, length_ref[0], jnp.where(lane < 2 * E, prompts_ref[0, 0], prompts_ref[0, 1])
    )
    notes[...] = note.astype(F32).astype(BF16)
    copies = []
    for member in range(n):
        start = 0
        for source in (q_ref, g_ref, k_ref, v_ref):
            width = source.shape[1] // n
            copies.append(
                pltpu.make_async_copy(
                    source.at[:, member * width : (member + 1) * width],
                    out_ref.at[member, 0:rows, start : start + width],
                    sems.at[len(copies)],
                )
            )
            start += width
        copies.append(
            pltpu.make_async_copy(
                notes, out_ref.at[member, rows : rows + NOTE_ROWS, :], sems.at[len(copies)]
            )
        )
    for copy in copies:
        copy.start()
    for copy in copies:
        copy.wait()


def pack(first_length, resp_prompt, queries, out_grad, own_keys, own_values, n):
    rows = queries.shape[0]
    width = (2 * queries.shape[1] + 2 * own_keys.shape[1]) // n
    return pl.pallas_call(
        functools.partial(pack_kernel, n),
        out_shape=jax.ShapeDtypeStruct((n, rows + NOTE_ROWS, width), BF16),
        in_specs=[SMEM, SMEM, ANY, ANY, ANY, ANY],
        out_specs=ANY,
        scratch_shapes=[
            pltpu.VMEM((NOTE_ROWS, width), BF16),
            pltpu.SemaphoreType.DMA((5 * n,)),
        ],
        compiler_params=params(),
        cost_estimate=cost(0, 4 * n * rows * width),
        name="pack_rows",
    )(first_length, resp_prompt, queries, out_grad, own_keys, own_values)


def unpack_kernel(n, packets, q_ref, k_ref, v_ref, sems):
    copies = []
    for member in range(n):
        start = 0
        for target in (q_ref, k_ref, v_ref):
            width = target.shape[1] // n
            copies.append(
                pltpu.make_async_copy(
                    packets.at[member, :, start : start + width],
                    target.at[:, member * width : (member + 1) * width],
                    sems.at[len(copies)],
                )
            )
            start += width
    for copy in copies:
        copy.start()
    for copy in copies:
        copy.wait()


def unpack(packets, q_width, kv_width):
    n, rows, _ = packets.shape
    return pl.pallas_call(
        functools.partial(unpack_kernel, n),
        out_shape=[
            jax.ShapeDtypeStruct((rows, width), BF16) for width in (q_width, kv_width, kv_width)
        ],
        in_specs=[ANY],
        out_specs=[ANY] * 3,
        scratch_shapes=[pltpu.SemaphoreType.DMA((3 * n,))],
        compiler_params=params(),
        cost_estimate=cost(0, 4 * rows * (q_width + 2 * kv_width)),
        name="unpack_rows",
    )(packets)


def project_kernel(n, x_ref, kw_ref, vw_ref, out_ref, key_sum, value_sum):
    step = pl.program_id(0)
    keys = dot(x_ref[...], kw_ref[...], 1, 0)
    values = dot(x_ref[...], vw_ref[...], 1, 0)

    @pl.when(step == 0)
    def _():
        key_sum[...] = keys
        value_sum[...] = values

    @pl.when(step > 0)
    def _():
        key_sum[...] += keys
        value_sum[...] += values

    @pl.when(step == pl.num_programs(0) - 1)
    def _():
        width = key_sum.shape[1] // n
        for member in range(n):
            head = slice(member * width, (member + 1) * width)
            out_ref[member, :, :width] = key_sum[:, head].astype(BF16)
            out_ref[member, :, width:] = value_sum[:, head].astype(BF16)


def project(prompt_rows, key_weight, value_weight, n, chunk=1024):
    rows, depth = prompt_rows.shape
    width = key_weight.shape[1]
    weight_spec = pl.BlockSpec((chunk, width), lambda i: (i, 0))
    out_shape = (n, rows, 2 * width // n)
    return pl.pallas_call(
        functools.partial(project_kernel, n),
        grid=(depth // chunk,),
        out_shape=jax.ShapeDtypeStruct(out_shape, BF16),
        in_specs=[pl.BlockSpec((rows, chunk), lambda i: (0, i)), weight_spec, weight_spec],
        out_specs=pl.BlockSpec(out_shape, lambda i: (0, 0, 0)),
        scratch_shapes=[pltpu.VMEM((rows, width), F32)] * 2,
        compiler_params=params(60),
        cost_estimate=cost(4 * rows * depth * width, 4 * depth * width + 2 * rows * depth),
        name="project_prefix",
    )(prompt_rows, key_weight, value_weight)


def attend_kernel(n, pieces, group, rows, packets, *rest):
    rest = list(rest)

    def take(count):
        taken = rest[:count]
        del rest[:count]
        return taken

    kv_in = take(pieces)
    (grads_out,) = take(1)
    send_out = take(pieces // 2)
    keep_out = take(pieces // 2)
    packed, keys, values, key_acc, value_acc, grads, sems, out_sem = rest
    part = PLEN // pieces

    copies = []
    for m in range(pieces):
        for index, buffer in enumerate((keys, values)):
            copies.append(
                pltpu.make_async_copy(
                    kv_in[m].at[:, :, index * E : (index + 1) * E],
                    buffer.at[:, m * part : (m + 1) * part, :],
                    sems.at[len(copies)],
                )
            )
    copies.append(pltpu.make_async_copy(packets, packed, sems.at[len(copies)]))
    for copy in copies:
        copy.start()
    key_acc[...] = jnp.zeros_like(key_acc)
    value_acc[...] = jnp.zeros_like(value_acc)
    for copy in copies:
        copy.wait()

    total_rows = group * rows
    row_in_column = lax.broadcasted_iota(jnp.int32, (total_rows, E), 0) & (rows - 1)
    row_in_lane = lax.broadcasted_iota(jnp.int32, (rows, total_rows), 1) & (rows - 1)
    own_key = lax.broadcasted_iota(jnp.int32, (rows, total_rows), 0)
    lane_row = lax.broadcasted_iota(jnp.int32, (E, total_rows), 1) & (rows - 1)

    def note(j, index):
        block = packed[j, rows : rows + NOTE_ROWS, index * E : (index + 1) * E]
        return jnp.max(block.astype(F32)).astype(jnp.int32)

    def member(j, carry):
        boundary, first_at, second_at = note(j, 0), note(j, 1), note(j, 2)
        heads = [packed[j, :rows, h * E : (h + 1) * E] for h in range(2 * group + 2)]
        query = jnp.concatenate(heads[:group], axis=0)
        grad = jnp.concatenate(heads[group : 2 * group], axis=0)
        own_k, own_v = heads[2 * group], heads[2 * group + 1]
        in_first = row_in_column < boundary

        def split(x):
            x = x.astype(F32)
            return jnp.concatenate(
                [jnp.where(in_first, x, 0.0), jnp.where(in_first, 0.0, x)], axis=1
            ).astype(BF16)

        query_pair = split(query)
        grad_pair = split(grad)
        key_pair = jnp.concatenate([keys[first_at], keys[second_at]], axis=1)
        value_pair = jnp.concatenate([values[first_at], values[second_at]], axis=1)

        scores = dot(key_pair, query_pair, 1, 1)
        visible = (own_key <= row_in_lane) & ((own_key >= boundary) == (row_in_lane >= boundary))
        own_scores = jnp.where(visible, dot(own_k, query, 1, 1), HIDDEN)
        top = jnp.maximum(
            jnp.max(scores, axis=0, keepdims=True), jnp.max(own_scores, axis=0, keepdims=True)
        )
        weight = jnp.exp2((scores - top) * EXP2_SCALE)
        own_weight = jnp.exp2((own_scores - top) * EXP2_SCALE)
        inverse = 1.0 / (
            jnp.sum(weight, axis=0, keepdims=True) + jnp.sum(own_weight, axis=0, keepdims=True)
        )
        probs = weight * inverse
        own_probs = own_weight * inverse
        probs_low = probs.astype(BF16)
        own_probs_low = own_probs.astype(BF16)
        dprobs = dot(value_pair, grad_pair, 1, 1)
        own_dprobs = dot(own_v, grad, 1, 1)
        delta = jnp.sum(probs_low.astype(F32) * dprobs, axis=0, keepdims=True) + jnp.sum(
            own_probs_low.astype(F32) * own_dprobs, axis=0, keepdims=True
        )
        dscores = (probs * (dprobs - delta)).astype(BF16)
        own_dscores = (own_probs * (own_dprobs - delta)).astype(BF16)

        key_part = dot(dscores, query_pair, 1, 0)
        value_part = dot(probs_low, grad_pair, 1, 0)
        key_acc[first_at] += key_part[:, :E]
        key_acc[second_at] += key_part[:, E:]
        value_acc[first_at] += value_part[:, :E]
        value_acc[second_at] += value_part[:, E:]

        query_both = dot(key_pair, dscores, 0, 0)
        query_part = jnp.where(lane_row < boundary, query_both[:E], query_both[E:])
        query_part = (query_part + dot(own_k, own_dscores, 0, 0)) * SCALE
        for h in range(group):
            grads[j, :, h * E : (h + 1) * E] = query_part[:, h * rows : (h + 1) * rows].T.astype(
                BF16
            )
        grads[j, :, group * E : (group + 1) * E] = (dot(own_dscores, query, 1, 0) * SCALE).astype(
            BF16
        )
        grads[j, :, (group + 1) * E :] = dot(own_probs_low, grad, 1, 0).astype(BF16)
        return carry

    lax.fori_loop(0, n, member, 0)

    out_copy = pltpu.make_async_copy(grads, grads_out, out_sem)
    out_copy.start()
    for m in range(pieces):
        target = keep_out[m // 2] if m % 2 == 0 else send_out[m // 2]
        span = slice(m * part, (m + 1) * part)
        target[:, :, :E] = (key_acc[:, span, :] * SCALE).astype(target.dtype)
        target[:, :, E:] = value_acc[:, span, :].astype(target.dtype)
    out_copy.wait()


def attend(packets, kv_in):
    n, noted_rows, packet_width = packets.shape
    rows = noted_rows - NOTE_ROWS
    pieces = len(kv_in)
    group = (packet_width // E - 2) // 2
    part = PLEN // pieces
    grads_shape = (n, rows, (group + 2) * E)
    keys = PLEN + rows
    return pl.pallas_call(
        functools.partial(attend_kernel, n, pieces, group, rows),
        out_shape=[jax.ShapeDtypeStruct(grads_shape, BF16)]
        + [jax.ShapeDtypeStruct((n, part, 2 * E), BF16)] * (pieces // 2)
        + [jax.ShapeDtypeStruct((n, part, 2 * E), F32)] * (pieces // 2),
        in_specs=[ANY] * (1 + pieces),
        out_specs=[ANY] + [VMEM] * pieces,
        scratch_shapes=[
            pltpu.VMEM(packets.shape, BF16),
            pltpu.VMEM((n, PLEN, E), BF16),
            pltpu.VMEM((n, PLEN, E), BF16),
            pltpu.VMEM((n, PLEN, E), F32),
            pltpu.VMEM((n, PLEN, E), F32),
            pltpu.VMEM(grads_shape, BF16),
            pltpu.SemaphoreType.DMA((2 * pieces + 1,)),
            pltpu.SemaphoreType.DMA,
        ],
        compiler_params=params(),
        cost_estimate=cost(
            20 * n * group * rows * keys * E, 8 * 1024 * 1024, n * group * rows * keys
        ),
        name="attend_heads",
    )(packets, *kv_in)


def total_kernel(keep_ref, *rest):
    parts, out_ref = rest[:-1], rest[-1]
    result = keep_ref[...]
    for part in parts:
        result = result + part[...].astype(F32)
    out_ref[...] = result.astype(BF16)


def total(keep, parts):
    return pl.pallas_call(
        total_kernel,
        out_shape=jax.ShapeDtypeStruct(keep.shape, BF16),
        in_specs=[VMEM] * (1 + len(parts)),
        out_specs=VMEM,
        compiler_params=params(),
        cost_estimate=cost(len(parts) * keep.size, (6 + 2 * len(parts)) * keep.size),
        name="total_prefix_grads",
    )(keep, *parts)


def prompt_kernel(n, shares, kw_ref, vw_ref, out_ref, key_grad, value_grad):
    @pl.when(pl.program_id(0) == 0)
    def _():
        width = key_grad.shape[1] // n
        for member in range(n):
            head = slice(member * width, (member + 1) * width)
            key_grad[:, head] = shares[member, :, :width]
            value_grad[:, head] = shares[member, :, width:]

    out_ref[...] = (
        dot(key_grad[...], kw_ref[...], 1, 1) + dot(value_grad[...], vw_ref[...], 1, 1)
    ).astype(BF16)


def prompt_gradient(shares, key_weight, value_weight, chunk=1024):
    n, rows, _ = shares.shape
    depth, width = key_weight.shape
    weight_spec = pl.BlockSpec((chunk, width), lambda i: (i, 0))
    return pl.pallas_call(
        functools.partial(prompt_kernel, n),
        grid=(depth // chunk,),
        out_shape=jax.ShapeDtypeStruct((rows, depth), BF16),
        in_specs=[pl.BlockSpec(shares.shape, lambda i: (0, 0, 0)), weight_spec, weight_spec],
        out_specs=pl.BlockSpec((rows, chunk), lambda i: (0, i)),
        scratch_shapes=[pltpu.VMEM((rows, width), BF16)] * 2,
        compiler_params=params(),
        cost_estimate=cost(4 * rows * depth * width, 4 * depth * width + 2 * rows * depth),
        name="prompt_gradient",
    )(shares, key_weight, value_weight)


def per_device(
    n_prompt,
    n_resp,
    prompt_rows,
    key_weight,
    value_weight,
    queries,
    own_keys,
    own_values,
    out_grad,
    first_length,
    resp_prompt,
):
    def swap(x, offset):
        return lax.ppermute(x, "resp", [(i, i ^ offset) for i in range(n_resp)])

    def transpose_plane(x):
        return lax.all_to_all(x, "prompt", 0, 0, tiled=True)

    packets = pack(first_length, resp_prompt, queries, out_grad, own_keys, own_values, n_prompt)
    packets, prompt_rows = lax.optimization_barrier((packets, prompt_rows))
    packets = transpose_plane(packets)

    kv = transpose_plane(project(prompt_rows, key_weight, value_weight, n_prompt))
    kv_in = []
    for m in range(0, n_resp, 2):
        piece = swap(kv, m) if m else kv
        kv_in += [piece, swap(piece, 1)]

    grads, *pieces = attend(packets, kv_in)
    half = n_resp // 2
    send, keep = pieces[:half], pieces[half:]
    sent = [swap(piece, 1) for piece in send]
    arrived = [sent[0]]
    for index in range(1, half):
        chip_sum = (keep[index] + sent[index].astype(F32)).astype(BF16)
        arrived.append(swap(chip_sum, 2 * index))
    shares = transpose_plane(total(keep[0], arrived))

    query_grad, key_grad, value_grad = unpack(
        transpose_plane(grads), queries.shape[1], own_keys.shape[1]
    )
    prompt_grad = prompt_gradient(shares, key_weight, value_weight)
    return (query_grad, key_grad, value_grad, prompt_grad)


def solution(mesh):
    both = P(("prompt", "resp"), None)
    return jax.shard_map(
        functools.partial(per_device, mesh.shape["prompt"], mesh.shape["resp"]),
        mesh=mesh,
        in_specs=(both, P(), P(), both, both, both, both, P(("prompt", "resp")), both),
        out_specs=(both, both, both, both),
        check_vma=False,
    )
```

```python
import functools
import math

import jax
import jax.numpy as jnp
from jax import lax
from jax.experimental import pallas as pl
from jax.experimental.pallas import tpu as pltpu
from jax.sharding import PartitionSpec as P

E = 128
PLEN = 512
SCALE = E ** (-0.5)
EXP2_SCALE = SCALE * math.log2(math.e)
HIDDEN = -1e30
BF16 = jnp.bfloat16
F32 = jnp.float32
NOTE_ROWS = 16
HEAD_BITS = (3, 1)
GATHER_BITS = (2, 4, 0)

ANY = pl.BlockSpec(memory_space=pl.ANY)
SMEM = pl.BlockSpec(memory_space=pltpu.SMEM)
VMEM = pl.BlockSpec(memory_space=pltpu.VMEM)


def params(mebibytes=40):
    return pltpu.CompilerParams(vmem_limit_bytes=mebibytes * 1024 * 1024)


def cost(flops, bytes_accessed, transcendentals=0):
    return pl.CostEstimate(
        flops=int(flops), bytes_accessed=int(bytes_accessed), transcendentals=int(transcendentals)
    )


def lanes(index, width):
    return pl.ds(pl.multiple_of(index * width, 128), width)


def dot(a, b, a_dim, b_dim):
    return lax.dot_general(a, b, (((a_dim,), (b_dim,)), ((), ())), preferred_element_type=F32)


def pack_kernel(n, place_ref, length_ref, prompts_ref, q_ref, g_ref, k_ref, v_ref, *rest):
    outs, notes, sems = rest[:n], rest[n], rest[n + 1]
    rows = q_ref.shape[0]
    copies = []
    for j in reversed(range(n)):
        start = 0
        for source in (q_ref, g_ref, k_ref, v_ref):
            width = source.shape[1] // n
            copies.append(
                pltpu.make_async_copy(
                    source.at[:, lanes(place_ref[0] ^ j, width)],
                    outs[j].at[0:rows, start : start + width],
                    sems.at[len(copies)],
                )
            )
            start += width
    for copy in copies:
        copy.start()
    lane = lax.broadcasted_iota(jnp.int32, notes.shape, 1)
    note = jnp.where(
        lane < E, length_ref[0], jnp.where(lane < 2 * E, prompts_ref[0, 0], prompts_ref[0, 1])
    )
    notes[...] = note.astype(F32).astype(BF16)
    for j in range(n):
        copy = pltpu.make_async_copy(
            notes, outs[j].at[rows : rows + NOTE_ROWS, :], sems.at[len(copies)]
        )
        copy.start()
        copies.append(copy)
    for copy in copies:
        copy.wait()


def pack(place, first_length, resp_prompt, queries, out_grad, own_keys, own_values, n):
    rows = queries.shape[0]
    width = (2 * queries.shape[1] + 2 * own_keys.shape[1]) // n
    return pl.pallas_call(
        functools.partial(pack_kernel, n),
        out_shape=[jax.ShapeDtypeStruct((rows + NOTE_ROWS, width), BF16)] * n,
        in_specs=[SMEM, SMEM, SMEM, ANY, ANY, ANY, ANY],
        out_specs=[ANY] * n,
        scratch_shapes=[
            pltpu.VMEM((NOTE_ROWS, width), BF16),
            pltpu.SemaphoreType.DMA((5 * n,)),
        ],
        compiler_params=params(60),
        cost_estimate=cost(0, 1024),
        name="pack_rows",
    )(place, first_length, resp_prompt, queries, out_grad, own_keys, own_values)


def unpack_kernel(n, place_ref, *rest):
    packets, targets, sems = rest[:n], rest[n : n + 3], rest[n + 3]
    copies = []
    for j in range(n):
        start = 0
        for target in targets:
            width = target.shape[1] // n
            copies.append(
                pltpu.make_async_copy(
                    packets[j].at[:, start : start + width],
                    target.at[:, lanes(place_ref[0] ^ j, width)],
                    sems.at[len(copies)],
                )
            )
            start += width
    for copy in copies:
        copy.start()
    for copy in copies:
        copy.wait()


def unpack(place, packets, q_width, kv_width):
    n = len(packets)
    rows = packets[0].shape[0]
    return pl.pallas_call(
        functools.partial(unpack_kernel, n),
        out_shape=[
            jax.ShapeDtypeStruct((rows, width), BF16) for width in (q_width, kv_width, kv_width)
        ],
        in_specs=[SMEM] + [ANY] * n,
        out_specs=[ANY] * 3,
        scratch_shapes=[pltpu.SemaphoreType.DMA((3 * n,))],
        compiler_params=params(),
        cost_estimate=cost(0, 4 * rows * (q_width + 2 * kv_width)),
        name="unpack_rows",
    )(place, *packets)


def project_kernel(n, steps, place_ref, x_ref, kw_ref, vw_ref, *rest):
    outs, (kw, vw, key_sum, value_sum, sems) = rest[:n], rest[n:]
    chunk = kw.shape[0] // steps
    copies = []
    for step in range(steps):
        span = slice(step * chunk, (step + 1) * chunk)
        for source, target in ((kw_ref, kw), (vw_ref, vw)):
            copies.append(
                pltpu.make_async_copy(
                    source.at[span, :], target.at[span, :], sems.at[len(copies)]
                )
            )
    for copy in copies:
        copy.start()
    keys = values = None
    for step in range(steps):
        span = slice(step * chunk, (step + 1) * chunk)
        copies[2 * step].wait()
        part = dot(x_ref[:, span], kw[span, :], 1, 0)
        keys = part if step == 0 else keys + part
        copies[2 * step + 1].wait()
        part = dot(x_ref[:, span], vw[span, :], 1, 0)
        values = part if step == 0 else values + part
    key_sum[...] = keys.astype(BF16)
    value_sum[...] = values.astype(BF16)
    width = key_sum.shape[1] // n
    for j in range(n):
        head = lanes(place_ref[0] ^ j, width)
        outs[j][:, :width] = key_sum[:, head]
        outs[j][:, width:] = value_sum[:, head]


def project(place, prompt_rows, key_weight, value_weight, n, steps=5):
    rows = prompt_rows.shape[0]
    width = key_weight.shape[1]
    return pl.pallas_call(
        functools.partial(project_kernel, n, steps),
        out_shape=[jax.ShapeDtypeStruct((rows, 2 * width // n), BF16)] * n,
        in_specs=[SMEM, VMEM, ANY, ANY],
        out_specs=[VMEM] * n,
        scratch_shapes=[pltpu.VMEM(key_weight.shape, BF16)] * 2
        + [pltpu.VMEM((rows, width), BF16)] * 2
        + [pltpu.SemaphoreType.DMA((2 * steps,))],
        compiler_params=params(60),
        cost_estimate=cost(0, 1024),
        name="project_prefix",
    )(place, prompt_rows, key_weight, value_weight)


def attend_kernel(slots, n, group, rows, place_ref, *rest):
    rest = list(rest)

    def take(count):
        taken = rest[:count]
        del rest[:count]
        return taken

    pieces = len(slots)
    packets = take(n)
    kv_in = take(pieces)
    grads_out = take(n)
    prefix_out = take(pieces)
    keys, values, key_acc, value_acc = rest
    part = kv_in[0].shape[1]

    for index in range(pieces):
        for j in range(n):
            prompt, slot = slots[index][j]
            span = slice(slot * part, (slot + 1) * part)
            keys[prompt, span, :] = kv_in[index][j, :, :E]
            values[prompt, span, :] = kv_in[index][j, :, E:]
    key_acc[...] = jnp.zeros_like(key_acc)
    value_acc[...] = jnp.zeros_like(value_acc)

    total_rows = group * rows
    row_in_column = lax.broadcasted_iota(jnp.int32, (total_rows, E), 0) & (rows - 1)
    row_in_lane = lax.broadcasted_iota(jnp.int32, (rows, total_rows), 1) & (rows - 1)
    own_key = lax.broadcasted_iota(jnp.int32, (rows, total_rows), 0)
    lane_row = lax.broadcasted_iota(jnp.int32, (E, total_rows), 1) & (rows - 1)

    for packet, grads in zip(packets, grads_out):

        def note(index):
            block = packet[rows : rows + NOTE_ROWS, index * E : (index + 1) * E]
            return jnp.max(block.astype(F32)).astype(jnp.int32)

        boundary, first_at, second_at = note(0), note(1) ^ place_ref[1], note(2) ^ place_ref[1]
        heads = [packet[:rows, h * E : (h + 1) * E] for h in range(2 * group + 2)]
        query = jnp.concatenate(heads[:group], axis=0)
        grad = jnp.concatenate(heads[group : 2 * group], axis=0)
        own_k, own_v = heads[2 * group], heads[2 * group + 1]
        in_first = row_in_column < boundary

        def split(x):
            x = x.astype(F32)
            return jnp.concatenate(
                [jnp.where(in_first, x, 0.0), jnp.where(in_first, 0.0, x)], axis=1
            ).astype(BF16)

        query_pair = split(query)
        grad_pair = split(grad)
        key_pair = jnp.concatenate([keys[first_at], keys[second_at]], axis=1)
        value_pair = jnp.concatenate([values[first_at], values[second_at]], axis=1)

        scores = dot(key_pair, query_pair, 1, 1)
        visible = (own_key <= row_in_lane) & ((own_key >= boundary) == (row_in_lane >= boundary))
        own_scores = jnp.where(visible, dot(own_k, query, 1, 1), HIDDEN)
        top = jnp.maximum(
            jnp.max(scores, axis=0, keepdims=True), jnp.max(own_scores, axis=0, keepdims=True)
        )
        weight = jnp.exp2((scores - top) * EXP2_SCALE)
        own_weight = jnp.exp2((own_scores - top) * EXP2_SCALE)
        inverse = 1.0 / (
            jnp.sum(weight, axis=0, keepdims=True) + jnp.sum(own_weight, axis=0, keepdims=True)
        )
        probs = weight * inverse
        own_probs = own_weight * inverse
        probs_low = probs.astype(BF16)
        own_probs_low = own_probs.astype(BF16)
        dprobs = dot(value_pair, grad_pair, 1, 1)
        own_dprobs = dot(own_v, grad, 1, 1)
        delta = jnp.sum(probs_low.astype(F32) * dprobs, axis=0, keepdims=True) + jnp.sum(
            own_probs_low.astype(F32) * own_dprobs, axis=0, keepdims=True
        )
        dscores = (probs * (dprobs - delta)).astype(BF16)
        own_dscores = (own_probs * (own_dprobs - delta)).astype(BF16)

        key_part = dot(dscores, query_pair, 1, 0)
        value_part = dot(probs_low, grad_pair, 1, 0)
        key_acc[first_at] += key_part[:, :E]
        key_acc[second_at] += key_part[:, E:]
        value_acc[first_at] += value_part[:, :E]
        value_acc[second_at] += value_part[:, E:]

        query_both = dot(key_pair, dscores, 0, 0)
        query_part = jnp.where(lane_row < boundary, query_both[:E], query_both[E:])
        query_part = (query_part + dot(own_k, own_dscores, 0, 0)) * SCALE
        for h in range(group):
            grads[:, h * E : (h + 1) * E] = query_part[:, h * rows : (h + 1) * rows].T.astype(BF16)
        grads[:, group * E : (group + 1) * E] = (dot(own_dscores, query, 1, 0) * SCALE).astype(BF16)
        grads[:, (group + 1) * E :] = dot(own_probs_low, grad, 1, 0).astype(BF16)

    for index in range(pieces):
        for j in range(n):
            prompt, slot = slots[index][j]
            span = slice(slot * part, (slot + 1) * part)
            target = prefix_out[index]
            target[j, :, :E] = (key_acc[prompt, span, :] * SCALE).astype(target.dtype)
            target[j, :, E:] = value_acc[prompt, span, :].astype(target.dtype)


def attend(place, packets, kv_in, slots, out_types, prompts):
    n = len(packets)
    noted_rows, packet_width = packets[0].shape
    rows = noted_rows - NOTE_ROWS
    group = (packet_width // E - 2) // 2
    keys = PLEN + rows
    return pl.pallas_call(
        functools.partial(attend_kernel, slots, n, group, rows),
        out_shape=[jax.ShapeDtypeStruct((rows, (group + 2) * E), BF16)] * n
        + [jax.ShapeDtypeStruct(kv_in[0].shape, kind) for kind in out_types],
        in_specs=[SMEM] + [VMEM] * (n + len(kv_in)),
        out_specs=[VMEM] * (n + len(kv_in)),
        scratch_shapes=[
            pltpu.VMEM((prompts, PLEN, E), BF16),
            pltpu.VMEM((prompts, PLEN, E), BF16),
            pltpu.VMEM((prompts, PLEN, E), F32),
            pltpu.VMEM((prompts, PLEN, E), F32),
        ],
        compiler_params=params(),
        cost_estimate=cost(
            20 * n * group * rows * keys * E, 8 * 1024 * 1024, n * group * rows * keys
        ),
        name="attend_head",
    )(place, *packets, *kv_in)


def total_kernel(n, keep_ref, *rest):
    parts, outs = rest[:-n], rest[-n:]
    for j in range(n):
        result = keep_ref[j]
        for part in parts:
            result = result + part[j].astype(F32)
        outs[j][...] = result.astype(BF16)


def total(keep, parts):
    n = keep.shape[0]
    return pl.pallas_call(
        functools.partial(total_kernel, n),
        out_shape=[jax.ShapeDtypeStruct(keep.shape[1:], BF16)] * n,
        in_specs=[VMEM] * (1 + len(parts)),
        out_specs=[VMEM] * n,
        compiler_params=params(),
        cost_estimate=cost(len(parts) * keep.size, (6 + 2 * len(parts)) * keep.size),
        name="total_prefix_grads",
    )(keep, *parts)


def prompt_kernel(n, place_ref, *rest):
    shares, (kw_ref, vw_ref, out_ref, key_grad, value_grad) = rest[:n], rest[n:]

    @pl.when(pl.program_id(0) == 0)
    def _():
        width = key_grad.shape[1] // n
        for j in range(n):
            head = lanes(place_ref[0] ^ j, width)
            key_grad[:, head] = shares[j][:, :width]
            value_grad[:, head] = shares[j][:, width:]

    out_ref[...] = (
        dot(key_grad[...], kw_ref[...], 1, 1) + dot(value_grad[...], vw_ref[...], 1, 1)
    ).astype(BF16)


def prompt_gradient(place, shares, key_weight, value_weight, chunk=1024):
    n = len(shares)
    rows = shares[0].shape[0]
    depth, width = key_weight.shape
    weight_spec = pl.BlockSpec((chunk, width), lambda i: (i, 0))
    return pl.pallas_call(
        functools.partial(prompt_kernel, n),
        grid=(depth // chunk,),
        out_shape=jax.ShapeDtypeStruct((rows, depth), BF16),
        in_specs=[SMEM]
        + [pl.BlockSpec(shares[0].shape, lambda i: (0, 0))] * n
        + [weight_spec, weight_spec],
        out_specs=pl.BlockSpec((rows, chunk), lambda i: (0, i)),
        scratch_shapes=[pltpu.VMEM((rows, width), BF16)] * 2,
        compiler_params=params(),
        cost_estimate=cost(4 * rows * depth * width, 4 * depth * width + 2 * rows * depth),
        name="prompt_gradient",
    )(place, *shares, key_weight, value_weight)


def spread(number, bits):
    return sum(((number >> i) & 1) << bit for i, bit in enumerate(bits))


def per_device(
    n_prompt,
    n_resp,
    prompt_rows,
    key_weight,
    value_weight,
    queries,
    own_keys,
    own_values,
    out_grad,
    first_length,
    resp_prompt,
):
    devices = n_prompt * n_resp
    heads = own_keys.shape[1] // E
    every_bit = range(devices.bit_length() - 1)
    rest_bits = [bit for bit in GATHER_BITS if bit in every_bit]
    rest_bits += [bit for bit in every_bit if bit not in rest_bits and bit not in HEAD_BITS]
    member = [spread(j, HEAD_BITS) for j in range(heads)]

    def swap(x, offset):
        return lax.ppermute(x, ("prompt", "resp"), [(i, i ^ offset) for i in range(devices)])

    def swap_group(items):
        return [items[0]] + [swap(items[j], member[j]) for j in range(1, heads)]

    prompt = lax.axis_index("prompt").astype(jnp.int32)
    device = prompt * n_resp + lax.axis_index("resp").astype(jnp.int32)
    head = sum(((device >> bit) & 1) << i for i, bit in enumerate(HEAD_BITS))
    place = jnp.stack([head, prompt])

    packed = pack(
        place, first_length, resp_prompt, queries, out_grad, own_keys, own_values, heads
    )
    packed, prompt_rows = lax.optimization_barrier((packed, prompt_rows))
    packets = swap_group(packed)

    projected = project(place, prompt_rows, key_weight, value_weight, heads)
    pieces = {0: jnp.stack(swap_group(projected))}
    for bit in rest_bits:
        for offset in list(pieces):
            pieces[offset | 1 << bit] = swap(pieces[offset], 1 << bit)
    offsets = list(pieces)

    filled = [0] * n_prompt
    slots = []
    for offset in offsets:
        places = []
        for j in range(heads):
            at = (offset ^ member[j]) // n_resp
            places.append((at, filled[at]))
            filled[at] += 1
        slots.append(tuple(places))

    first_out = 1 << rest_bits[-1]
    out_types = [BF16 if offset & first_out else F32 for offset in offsets]
    outs = attend(place, packets, [pieces[o] for o in offsets], tuple(slots), out_types, n_prompt)
    grads = outs[:heads]
    sums = dict(zip(offsets, outs[heads:]))
    arrived = {offset: [] for offset in offsets}
    for bit in reversed(rest_bits):
        for offset in reversed(offsets):
            if offset & 1 << bit:
                piece = sums.pop(offset)
                for part in arrived.pop(offset):
                    piece = piece + part.astype(F32)
                arrived[offset ^ 1 << bit].append(swap(piece.astype(BF16), 1 << bit))
        offsets = list(sums)
    shares = swap_group(total(sums[0], arrived[0]))

    query_grad, key_grad, value_grad = unpack(
        place, swap_group(grads), queries.shape[1], own_keys.shape[1]
    )
    prompt_grad = prompt_gradient(place, shares, key_weight, value_weight)
    return (query_grad, key_grad, value_grad, prompt_grad)


def solution(mesh):
    both = P(("prompt", "resp"), None)
    return jax.shard_map(
        functools.partial(per_device, mesh.shape["prompt"], mesh.shape["resp"]),
        mesh=mesh,
        in_specs=(both, P(), P(), both, both, both, both, P(("prompt", "resp")), both),
        out_specs=(both, both, both, both),
        check_vma=False,
    )
```

```python
import functools
import math

import jax
import jax.numpy as jnp
from jax import lax
from jax.experimental import pallas as pl
from jax.experimental.pallas import tpu as pltpu
from jax.sharding import PartitionSpec as P

E = 128
PLEN = 512
SCALE = E ** (-0.5)
EXP2_SCALE = SCALE * math.log2(math.e)
HIDDEN = -1e30
BF16 = jnp.bfloat16
F32 = jnp.float32
NOTE_ROWS = 16
HEAD_BITS = (3, 4)
GATHER_BITS = (2, 1, 0)

ANY = pl.BlockSpec(memory_space=pl.ANY)
SMEM = pl.BlockSpec(memory_space=pltpu.SMEM)
VMEM = pl.BlockSpec(memory_space=pltpu.VMEM)


def params(mebibytes=40):
    return pltpu.CompilerParams(vmem_limit_bytes=mebibytes * 1024 * 1024)


def cost(flops, bytes_accessed, transcendentals=0):
    return pl.CostEstimate(
        flops=int(flops), bytes_accessed=int(bytes_accessed), transcendentals=int(transcendentals)
    )


def lanes(index, width):
    return pl.ds(pl.multiple_of(index * width, 128), width)


def dot(a, b, a_dim, b_dim):
    return lax.dot_general(a, b, (((a_dim,), (b_dim,)), ((), ())), preferred_element_type=F32)


def open_kernel(n, steps, place_ref, length_ref, prompts_ref, x_ref, *rest):
    sources, (kw_ref, vw_ref), packets, heads = rest[:4], rest[4:6], rest[6 : 6 + n], rest[6 + n :]
    heads, (kw, vw, key_sum, value_sum, sems, row_sems) = heads[:n], heads[n:]
    chunk = kw.shape[0] // steps
    copies = []
    for step in range(steps):
        span = slice(step * chunk, (step + 1) * chunk)
        for source, target in ((kw_ref, kw), (vw_ref, vw)):
            copies.append(
                pltpu.make_async_copy(
                    source.at[span, :], target.at[span, :], sems.at[len(copies)]
                )
            )
    rows = sources[0].shape[0]
    row_copies = []
    for j in range(n):
        start = 0
        for source in sources:
            width = source.shape[1] // n
            row_copies.append(
                pltpu.make_async_copy(
                    source.at[:, lanes(place_ref[0] ^ j, width)],
                    packets[j].at[0:rows, start : start + width],
                    row_sems.at[len(row_copies)],
                )
            )
            start += width
    for copy in copies[:4] + row_copies + copies[4:]:
        copy.start()
    lane = lax.broadcasted_iota(jnp.int32, (NOTE_ROWS, packets[0].shape[1]), 1)
    note = jnp.where(
        lane < E, length_ref[0], jnp.where(lane < 2 * E, prompts_ref[0, 0], prompts_ref[0, 1])
    )
    note = note.astype(F32).astype(BF16)
    for j in range(n):
        packets[j][rows : rows + NOTE_ROWS, :] = note
    keys = values = None
    for step in range(steps):
        span = slice(step * chunk, (step + 1) * chunk)
        copies[2 * step].wait()
        part = dot(x_ref[:, span], kw[span, :], 1, 0)
        keys = part if step == 0 else keys + part
        copies[2 * step + 1].wait()
        part = dot(x_ref[:, span], vw[span, :], 1, 0)
        values = part if step == 0 else values + part
    key_sum[...] = keys.astype(BF16)
    value_sum[...] = values.astype(BF16)
    width = key_sum.shape[1] // n
    for j in range(n):
        head = lanes(place_ref[0] ^ j, width)
        heads[j][:, :width] = key_sum[:, head]
        heads[j][:, width:] = value_sum[:, head]
    for copy in row_copies:
        copy.wait()


def opening(place, first_length, resp_prompt, prompt_rows, rows_in, weights, n, steps=10):
    rows = rows_in[0].shape[0]
    packet = (rows + NOTE_ROWS, sum(x.shape[1] for x in rows_in) // n)
    prompt_count = prompt_rows.shape[0]
    width = weights[0].shape[1]
    outs = pl.pallas_call(
        functools.partial(open_kernel, n, steps),
        out_shape=[jax.ShapeDtypeStruct(packet, BF16)] * n
        + [jax.ShapeDtypeStruct((prompt_count, 2 * width // n), BF16)] * n,
        in_specs=[SMEM, SMEM, SMEM, VMEM] + [ANY] * 6,
        out_specs=[VMEM] * (2 * n),
        scratch_shapes=[pltpu.VMEM(weights[0].shape, BF16)] * 2
        + [pltpu.VMEM((prompt_count, width), BF16)] * 2
        + [pltpu.SemaphoreType.DMA((2 * steps,)), pltpu.SemaphoreType.DMA((4 * n,))],
        compiler_params=params(62),
        cost_estimate=cost(0, 1024),
        name="open",
    )(place, first_length, resp_prompt, prompt_rows, *rows_in, *weights)
    return outs[:n], outs[n:]


def unpack_kernel(n, place_ref, *rest):
    packets, targets = rest[:n], rest[n:]
    for j in range(n):
        start = 0
        for target in targets:
            width = target.shape[1] // n
            target[:, lanes(place_ref[0] ^ j, width)] = packets[j][:, start : start + width]
            start += width


def unpack(place, packets, q_width, kv_width):
    n = len(packets)
    rows = packets[0].shape[0]
    return pl.pallas_call(
        functools.partial(unpack_kernel, n),
        out_shape=[
            jax.ShapeDtypeStruct((rows, width), BF16) for width in (q_width, kv_width, kv_width)
        ],
        in_specs=[SMEM] + [VMEM] * n,
        out_specs=[VMEM] * 3,
        compiler_params=params(16),
        cost_estimate=cost(0, 4 * rows * (q_width + 2 * kv_width)),
        name="unpack_rows",
    )(place, *packets)


def attend_kernel(slots, n, group, rows, place_ref, *rest):
    rest = list(rest)

    def take(count):
        taken = rest[:count]
        del rest[:count]
        return taken

    pieces = len(slots)
    packets = take(n)
    kv_in = take(pieces)
    grads_out = take(n)
    prefix_out = take(pieces)
    keys, values, key_acc, value_acc = rest
    part = kv_in[0].shape[1]

    for index in range(pieces):
        for j in range(n):
            prompt, slot = slots[index][j]
            span = slice(slot * part, (slot + 1) * part)
            keys[prompt, span, :] = kv_in[index][j, :, :E]
            values[prompt, span, :] = kv_in[index][j, :, E:]
    key_acc[...] = jnp.zeros_like(key_acc)
    value_acc[...] = jnp.zeros_like(value_acc)

    total_rows = group * rows
    row_in_column = lax.broadcasted_iota(jnp.int32, (total_rows, E), 0) & (rows - 1)
    row_in_lane = lax.broadcasted_iota(jnp.int32, (rows, total_rows), 1) & (rows - 1)
    own_key = lax.broadcasted_iota(jnp.int32, (rows, total_rows), 0)
    lane_row = lax.broadcasted_iota(jnp.int32, (E, total_rows), 1) & (rows - 1)

    def products(packet):
        def note(index):
            block = packet[rows : rows + NOTE_ROWS, index * E : (index + 1) * E]
            return jnp.max(block.astype(F32)).astype(jnp.int32)

        boundary, first_at, second_at = note(0), note(1) ^ place_ref[1], note(2) ^ place_ref[1]
        heads = [packet[:rows, h * E : (h + 1) * E] for h in range(2 * group + 2)]
        query = jnp.concatenate(heads[:group], axis=0)
        grad = jnp.concatenate(heads[group : 2 * group], axis=0)
        own_k, own_v = heads[2 * group], heads[2 * group + 1]
        in_first = row_in_column < boundary

        def split(x):
            x = x.astype(F32)
            return jnp.concatenate(
                [jnp.where(in_first, x, 0.0), jnp.where(in_first, 0.0, x)], axis=1
            ).astype(BF16)

        query_pair = split(query)
        grad_pair = split(grad)
        key_pair = jnp.concatenate([keys[first_at], keys[second_at]], axis=1)
        value_pair = jnp.concatenate([values[first_at], values[second_at]], axis=1)

        visible = (own_key <= row_in_lane) & ((own_key >= boundary) == (row_in_lane >= boundary))
        return dict(
            boundary=boundary,
            first_at=first_at,
            second_at=second_at,
            query=query,
            grad=grad,
            own_k=own_k,
            query_pair=query_pair,
            grad_pair=grad_pair,
            key_pair=key_pair,
            scores=dot(key_pair, query_pair, 1, 1),
            own_scores=jnp.where(visible, dot(own_k, query, 1, 1), HIDDEN),
            dprobs=dot(value_pair, grad_pair, 1, 1),
            own_dprobs=dot(own_v, grad, 1, 1),
        )

    def soften(scores, own_scores, dprobs, own_dprobs, **_):
        top = jnp.maximum(
            jnp.max(scores, axis=0, keepdims=True), jnp.max(own_scores, axis=0, keepdims=True)
        )
        weight = jnp.exp2((scores - top) * EXP2_SCALE)
        own_weight = jnp.exp2((own_scores - top) * EXP2_SCALE)
        inverse = 1.0 / (
            jnp.sum(weight, axis=0, keepdims=True) + jnp.sum(own_weight, axis=0, keepdims=True)
        )
        probs = weight * inverse
        own_probs = own_weight * inverse
        probs_low = probs.astype(BF16)
        own_probs_low = own_probs.astype(BF16)
        delta = jnp.sum(probs_low.astype(F32) * dprobs, axis=0, keepdims=True) + jnp.sum(
            own_probs_low.astype(F32) * own_dprobs, axis=0, keepdims=True
        )
        return dict(
            probs_low=probs_low,
            own_probs_low=own_probs_low,
            dscores=(probs * (dprobs - delta)).astype(BF16),
            own_dscores=(own_probs * (own_dprobs - delta)).astype(BF16),
        )

    def gradients(
        grads, boundary, first_at, second_at, query, grad, own_k, query_pair, grad_pair, key_pair,
        probs_low, own_probs_low, dscores, own_dscores, **_
    ):
        key_part = dot(dscores, query_pair, 1, 0)
        value_part = dot(probs_low, grad_pair, 1, 0)
        key_acc[first_at] += key_part[:, :E]
        key_acc[second_at] += key_part[:, E:]
        value_acc[first_at] += value_part[:, :E]
        value_acc[second_at] += value_part[:, E:]

        query_both = dot(key_pair, dscores, 0, 0)
        query_part = jnp.where(lane_row < boundary, query_both[:E], query_both[E:])
        query_part = (query_part + dot(own_k, own_dscores, 0, 0)) * SCALE
        for h in range(group):
            grads[:, h * E : (h + 1) * E] = query_part[:, h * rows : (h + 1) * rows].T.astype(BF16)
        grads[:, group * E : (group + 1) * E] = (dot(own_dscores, query, 1, 0) * SCALE).astype(BF16)
        grads[:, (group + 1) * E :] = dot(own_probs_low, grad, 1, 0).astype(BF16)

    ahead = products(packets[0])
    for j in range(n):
        now = ahead
        if j + 1 < n:
            ahead = products(packets[j + 1])
        gradients(grads_out[j], **now, **soften(**now))

    for index in range(pieces):
        for j in range(n):
            prompt, slot = slots[index][j]
            span = slice(slot * part, (slot + 1) * part)
            target = prefix_out[index]
            target[j, :, :E] = (key_acc[prompt, span, :] * SCALE).astype(target.dtype)
            target[j, :, E:] = value_acc[prompt, span, :].astype(target.dtype)


def attend(place, packets, kv_in, slots, out_types, prompts):
    n = len(packets)
    noted_rows, packet_width = packets[0].shape
    rows = noted_rows - NOTE_ROWS
    group = (packet_width // E - 2) // 2
    keys = PLEN + rows
    return pl.pallas_call(
        functools.partial(attend_kernel, slots, n, group, rows),
        out_shape=[jax.ShapeDtypeStruct((rows, (group + 2) * E), BF16)] * n
        + [jax.ShapeDtypeStruct(kv_in[0].shape, kind) for kind in out_types],
        in_specs=[SMEM] + [VMEM] * (n + len(kv_in)),
        out_specs=[VMEM] * (n + len(kv_in)),
        scratch_shapes=[
            pltpu.VMEM((prompts, PLEN, E), BF16),
            pltpu.VMEM((prompts, PLEN, E), BF16),
            pltpu.VMEM((prompts, PLEN, E), F32),
            pltpu.VMEM((prompts, PLEN, E), F32),
        ],
        compiler_params=params(),
        cost_estimate=cost(
            20 * n * group * rows * keys * E, 8 * 1024 * 1024, n * group * rows * keys
        ),
        name="attend_head",
    )(place, *packets, *kv_in)


def total_kernel(n, keep_ref, *rest):
    parts, outs = rest[:-n], rest[-n:]
    for j in range(n):
        result = keep_ref[j]
        for part in parts:
            result = result + part[j].astype(F32)
        outs[j][...] = result.astype(BF16)


def total(keep, parts):
    n = keep.shape[0]
    return pl.pallas_call(
        functools.partial(total_kernel, n),
        out_shape=[jax.ShapeDtypeStruct(keep.shape[1:], BF16)] * n,
        in_specs=[VMEM] * (1 + len(parts)),
        out_specs=[VMEM] * n,
        compiler_params=params(),
        cost_estimate=cost(len(parts) * keep.size, (6 + 2 * len(parts)) * keep.size),
        name="total_prefix_grads",
    )(keep, *parts)


def prompt_kernel(n, place_ref, *rest):
    shares, (kw_ref, vw_ref, out_ref, key_grad, value_grad) = rest[:n], rest[n:]

    @pl.when(pl.program_id(0) == 0)
    def _():
        width = key_grad.shape[1] // n
        for j in range(n):
            head = lanes(place_ref[0] ^ j, width)
            key_grad[:, head] = shares[j][:, :width]
            value_grad[:, head] = shares[j][:, width:]

    out_ref[...] = (
        dot(key_grad[...], kw_ref[...], 1, 1) + dot(value_grad[...], vw_ref[...], 1, 1)
    ).astype(BF16)


def prompt_gradient(place, shares, key_weight, value_weight, chunk=1024):
    n = len(shares)
    rows = shares[0].shape[0]
    depth, width = key_weight.shape
    weight_spec = pl.BlockSpec((chunk, width), lambda i: (i, 0))
    return pl.pallas_call(
        functools.partial(prompt_kernel, n),
        grid=(depth // chunk,),
        out_shape=jax.ShapeDtypeStruct((rows, depth), BF16),
        in_specs=[SMEM]
        + [pl.BlockSpec(shares[0].shape, lambda i: (0, 0))] * n
        + [weight_spec, weight_spec],
        out_specs=pl.BlockSpec((rows, chunk), lambda i: (0, i)),
        scratch_shapes=[pltpu.VMEM((rows, width), BF16)] * 2,
        compiler_params=params(),
        cost_estimate=cost(4 * rows * depth * width, 4 * depth * width + 2 * rows * depth),
        name="prompt_gradient",
    )(place, *shares, key_weight, value_weight)


def spread(number, bits):
    return sum(((number >> i) & 1) << bit for i, bit in enumerate(bits))


def per_device(
    n_prompt,
    n_resp,
    prompt_rows,
    key_weight,
    value_weight,
    queries,
    own_keys,
    own_values,
    out_grad,
    first_length,
    resp_prompt,
):
    devices = n_prompt * n_resp
    heads = own_keys.shape[1] // E
    every_bit = range(devices.bit_length() - 1)
    rest_bits = [bit for bit in GATHER_BITS if bit in every_bit]
    rest_bits += [bit for bit in every_bit if bit not in rest_bits and bit not in HEAD_BITS]
    member = [spread(j, HEAD_BITS) for j in range(heads)]

    def swap(x, offset):
        return lax.ppermute(x, ("prompt", "resp"), [(i, i ^ offset) for i in range(devices)])

    def swap_group(items):
        return [items[0]] + [swap(items[j], member[j]) for j in range(1, heads)]

    prompt = lax.axis_index("prompt").astype(jnp.int32)
    device = prompt * n_resp + lax.axis_index("resp").astype(jnp.int32)
    head = sum(((device >> bit) & 1) << i for i, bit in enumerate(HEAD_BITS))
    place = jnp.stack([head, prompt])

    packed, projected = opening(
        place,
        first_length,
        resp_prompt,
        prompt_rows,
        (queries, out_grad, own_keys, own_values),
        (key_weight, value_weight),
        heads,
    )
    packets = swap_group(packed)
    pieces = {0: jnp.stack(swap_group(projected))}
    for bit in rest_bits:
        for offset in list(pieces):
            piece = pieces[offset]
            if bit == rest_bits[-1] and offset == max(pieces):
                piece, packets = lax.optimization_barrier((piece, packets))
            pieces[offset | 1 << bit] = swap(piece, 1 << bit)
    offsets = list(pieces)

    filled = [0] * n_prompt
    slots = []
    for offset in offsets:
        places = []
        for j in range(heads):
            at = (offset ^ member[j]) // n_resp
            places.append((at, filled[at]))
            filled[at] += 1
        slots.append(tuple(places))

    first_out = 1 << rest_bits[-1]
    out_types = [BF16 if offset & first_out else F32 for offset in offsets]
    outs = attend(place, packets, [pieces[o] for o in offsets], tuple(slots), out_types, n_prompt)
    grads = outs[:heads]
    sums = dict(zip(offsets, outs[heads:]))
    arrived = {offset: [] for offset in offsets}
    for bit in reversed(rest_bits):
        for offset in reversed(offsets):
            if offset & 1 << bit:
                piece = sums.pop(offset)
                for part in arrived.pop(offset):
                    piece = piece + part.astype(F32)
                if arrived[0] and bit == rest_bits[-2] and offset == max(offsets):
                    piece, grads = lax.optimization_barrier((piece, grads))
                arrived[offset ^ 1 << bit].append(swap(piece.astype(BF16), 1 << bit))
        offsets = list(sums)
    shares = swap_group(total(sums[0], arrived[0]))

    query_grad, key_grad, value_grad = unpack(
        place, swap_group(grads), queries.shape[1], own_keys.shape[1]
    )
    prompt_grad = prompt_gradient(place, shares, key_weight, value_weight)
    return (query_grad, key_grad, value_grad, prompt_grad)


def solution(mesh):
    both = P(("prompt", "resp"), None)
    return jax.shard_map(
        functools.partial(per_device, mesh.shape["prompt"], mesh.shape["resp"]),
        mesh=mesh,
        in_specs=(both, P(), P(), both, both, both, both, P(("prompt", "resp")), both),
        out_specs=(both, both, both, both),
        check_vma=False,
    )
```

```python
import functools
import math

import jax
import jax.numpy as jnp
from jax import lax
from jax.experimental import pallas as pl
from jax.experimental.pallas import tpu as pltpu
from jax.sharding import PartitionSpec as P

E = 128
PLEN = 512
SCALE = E ** (-0.5)
EXP2_SCALE = SCALE * math.log2(math.e)
HIDDEN = -1e30
BF16 = jnp.bfloat16
F32 = jnp.float32
NOTE_ROWS = 16
HEAD_BITS = (3, 4)
GATHER_BITS = (2, 1, 0)

ANY = pl.BlockSpec(memory_space=pl.ANY)
VMEM = pl.BlockSpec(memory_space=pltpu.VMEM)


def params(mebibytes=40):
    return pltpu.CompilerParams(vmem_limit_bytes=mebibytes * 1024 * 1024)


def cost(flops, bytes_accessed, transcendentals=0):
    return pl.CostEstimate(
        flops=int(flops), bytes_accessed=int(bytes_accessed), transcendentals=int(transcendentals)
    )


def lanes(index, width):
    return pl.ds(pl.multiple_of(index * width, 128), width)


def dot(a, b, a_dim, b_dim):
    return lax.dot_general(a, b, (((a_dim,), (b_dim,)), ((), ())), preferred_element_type=F32)


def place():
    prompt = lax.axis_index("prompt")
    device = prompt * lax.axis_size("resp") + lax.axis_index("resp")
    return sum(((device >> bit) & 1) << i for i, bit in enumerate(HEAD_BITS)), prompt


def project_kernel(n, steps, length_ref, prompts_ref, x_ref, kw_ref, vw_ref, *rest):
    outs, (kw, vw, key_sum, value_sum, length, prompts, sems, note_sems) = rest[:n], rest[n:]
    chunk = kw.shape[0] // steps
    copies = []
    for step in range(steps):
        span = slice(step * chunk, (step + 1) * chunk)
        for source, target in ((kw_ref, kw), (vw_ref, vw)):
            copies.append(
                pltpu.make_async_copy(
                    source.at[span, :], target.at[span, :], sems.at[len(copies)]
                )
            )
    note_copies = [
        pltpu.make_async_copy(length_ref, length, note_sems.at[0]),
        pltpu.make_async_copy(prompts_ref, prompts, note_sems.at[1]),
    ]
    for copy in copies + note_copies:
        copy.start()
    keys = values = None
    for step in range(steps):
        span = slice(step * chunk, (step + 1) * chunk)
        copies[2 * step].wait()
        part = dot(x_ref[:, span], kw[span, :], 1, 0)
        keys = part if step == 0 else keys + part
        copies[2 * step + 1].wait()
        part = dot(x_ref[:, span], vw[span, :], 1, 0)
        values = part if step == 0 else values + part
    key_sum[...] = keys.astype(BF16)
    value_sum[...] = values.astype(BF16)
    for copy in note_copies:
        copy.wait()
    lane = lax.broadcasted_iota(jnp.int32, (NOTE_ROWS, 2 * E), 1)
    row = lax.broadcasted_iota(jnp.int32, (NOTE_ROWS, 2 * E), 0)
    note = jnp.where(
        lane < E, length[0, 0], jnp.where(row < NOTE_ROWS // 2, prompts[0, 0], prompts[0, 1])
    )
    note = note.astype(F32).astype(BF16)
    head, _ = place()
    rows = x_ref.shape[0]
    for j in range(n):
        outs[j][:rows, :E] = key_sum[:, lanes(head ^ j, E)]
        outs[j][:rows, E:] = value_sum[:, lanes(head ^ j, E)]
        outs[j][rows:, :] = note


def project(first_length, resp_prompt, prompt_rows, key_weight, value_weight, n, steps=10):
    rows = prompt_rows.shape[0]
    depth, width = key_weight.shape
    return pl.pallas_call(
        functools.partial(project_kernel, n, steps),
        out_shape=[jax.ShapeDtypeStruct((rows + NOTE_ROWS, 2 * E), BF16)] * n,
        in_specs=[ANY, ANY, VMEM, ANY, ANY],
        out_specs=[VMEM] * n,
        scratch_shapes=[pltpu.VMEM(key_weight.shape, BF16)] * 2
        + [pltpu.VMEM((rows, width), BF16)] * 2
        + [pltpu.SMEM(first_length.shape, jnp.int32), pltpu.SMEM(resp_prompt.shape, jnp.int32)]
        + [pltpu.SemaphoreType.DMA((2 * steps,)), pltpu.SemaphoreType.DMA((2,))],
        compiler_params=params(60),
        cost_estimate=cost(4 * rows * depth * width, 4 * depth * width + 2 * rows * depth),
        name="project_prefix",
    )(first_length, resp_prompt, prompt_rows, key_weight, value_weight)


def pack_kernel(n, q_ref, g_ref, k_ref, v_ref, *outs):
    head, _ = place()
    for j in range(n):
        start = 0
        for source in (q_ref, g_ref, k_ref, v_ref):
            width = source.shape[1] // n
            outs[j][:, start : start + width] = source[:, lanes(head ^ j, width)]
            start += width


def pack(queries, out_grad, own_keys, own_values, n):
    rows = queries.shape[0]
    width = (2 * queries.shape[1] + 2 * own_keys.shape[1]) // n
    return pl.pallas_call(
        functools.partial(pack_kernel, n),
        out_shape=[jax.ShapeDtypeStruct((rows, width), BF16)] * n,
        in_specs=[VMEM] * 4,
        out_specs=[VMEM] * n,
        compiler_params=params(16),
        cost_estimate=cost(0, 4 * n * rows * width),
        name="pack_rows",
    )(queries, out_grad, own_keys, own_values)


def unpack_kernel(n, *rest):
    packets, targets = rest[:n], rest[n:]
    head, _ = place()
    for j in range(n):
        start = 0
        for target in targets:
            width = target.shape[1] // n
            target[:, lanes(head ^ j, width)] = packets[j][:, start : start + width]
            start += width


def unpack(packets, q_width, kv_width):
    n = len(packets)
    rows = packets[0].shape[0]
    return pl.pallas_call(
        functools.partial(unpack_kernel, n),
        out_shape=[
            jax.ShapeDtypeStruct((rows, width), BF16) for width in (q_width, kv_width, kv_width)
        ],
        in_specs=[VMEM] * n,
        out_specs=[VMEM] * 3,
        compiler_params=params(16),
        cost_estimate=cost(0, 4 * rows * (q_width + 2 * kv_width)),
        name="unpack_rows",
    )(*packets)


def attend_kernel(slots, n, group, rows, first, last, *rest):
    rest = list(rest)

    def take(count):
        taken = rest[:count]
        del rest[:count]
        return taken

    pieces = len(slots)
    packets = take(n)
    notes = take(n)
    kv_in = take(pieces)
    sums_in = take(0 if first else 2)
    grads_out = take(n)
    prefix_out = take(pieces if last else 0)
    if not last:
        key_acc, value_acc = take(2)
    keys, values = take(2)
    if last:
        key_acc, value_acc = take(2)
    part = kv_in[0].shape[1]
    blocks = kv_in[0].shape[0]
    _, prompt_place = place()

    for index in range(pieces):
        for j in range(blocks):
            prompt, slot = slots[index][j]
            span = slice(slot * part, (slot + 1) * part)
            keys[prompt, span, :] = kv_in[index][j, :, :E]
            values[prompt, span, :] = kv_in[index][j, :, E:]
    key_acc[...] = jnp.zeros_like(key_acc) if first else sums_in[0][...]
    value_acc[...] = jnp.zeros_like(value_acc) if first else sums_in[1][...]

    total_rows = group * rows
    row_in_column = lax.broadcasted_iota(jnp.int32, (total_rows, E), 0) & (rows - 1)
    row_in_lane = lax.broadcasted_iota(jnp.int32, (rows, total_rows), 1) & (rows - 1)
    own_key = lax.broadcasted_iota(jnp.int32, (rows, total_rows), 0)
    lane_row = lax.broadcasted_iota(jnp.int32, (E, total_rows), 1) & (rows - 1)

    def products(packet, note):
        note = note[part:, :].astype(F32)
        half = NOTE_ROWS // 2
        boundary, first_at, second_at = (
            jnp.max(block).astype(jnp.int32)
            for block in (note[:half, :E], note[:half, E:], note[half:, E:])
        )
        first_at, second_at = first_at ^ prompt_place, second_at ^ prompt_place
        heads = [packet[:, h * E : (h + 1) * E] for h in range(2 * group + 2)]
        query = jnp.concatenate(heads[:group], axis=0)
        grad = jnp.concatenate(heads[group : 2 * group], axis=0)
        own_k, own_v = heads[2 * group], heads[2 * group + 1]
        in_first = row_in_column < boundary

        def split(x):
            x = x.astype(F32)
            return jnp.concatenate(
                [jnp.where(in_first, x, 0.0), jnp.where(in_first, 0.0, x)], axis=1
            ).astype(BF16)

        query_pair = split(query)
        grad_pair = split(grad)
        key_pair = jnp.concatenate([keys[first_at], keys[second_at]], axis=1)
        value_pair = jnp.concatenate([values[first_at], values[second_at]], axis=1)

        visible = (own_key <= row_in_lane) & ((own_key >= boundary) == (row_in_lane >= boundary))
        return dict(
            boundary=boundary,
            first_at=first_at,
            second_at=second_at,
            query=query,
            grad=grad,
            own_k=own_k,
            query_pair=query_pair,
            grad_pair=grad_pair,
            key_pair=key_pair,
            scores=dot(key_pair, query_pair, 1, 1),
            own_scores=jnp.where(visible, dot(own_k, query, 1, 1), HIDDEN),
            dprobs=dot(value_pair, grad_pair, 1, 1),
            own_dprobs=dot(own_v, grad, 1, 1),
        )

    def soften(scores, own_scores, dprobs, own_dprobs, **_):
        top = jnp.maximum(
            jnp.max(scores, axis=0, keepdims=True), jnp.max(own_scores, axis=0, keepdims=True)
        )
        weight = jnp.exp2((scores - top) * EXP2_SCALE)
        own_weight = jnp.exp2((own_scores - top) * EXP2_SCALE)
        inverse = 1.0 / (
            jnp.sum(weight, axis=0, keepdims=True) + jnp.sum(own_weight, axis=0, keepdims=True)
        )
        probs = weight * inverse
        own_probs = own_weight * inverse
        probs_low = probs.astype(BF16)
        own_probs_low = own_probs.astype(BF16)
        delta = jnp.sum(probs_low.astype(F32) * dprobs, axis=0, keepdims=True) + jnp.sum(
            own_probs_low.astype(F32) * own_dprobs, axis=0, keepdims=True
        )
        return dict(
            probs_low=probs_low,
            own_probs_low=own_probs_low,
            dscores=(probs * (dprobs - delta)).astype(BF16),
            own_dscores=(own_probs * (own_dprobs - delta)).astype(BF16),
        )

    def gradients(
        grads, boundary, first_at, second_at, query, grad, own_k, query_pair, grad_pair, key_pair,
        probs_low, own_probs_low, dscores, own_dscores, **_
    ):
        key_part = dot(dscores, query_pair, 1, 0)
        value_part = dot(probs_low, grad_pair, 1, 0)
        key_acc[first_at] += key_part[:, :E]
        key_acc[second_at] += key_part[:, E:]
        value_acc[first_at] += value_part[:, :E]
        value_acc[second_at] += value_part[:, E:]

        query_both = dot(key_pair, dscores, 0, 0)
        query_part = jnp.where(lane_row < boundary, query_both[:E], query_both[E:])
        query_part = (query_part + dot(own_k, own_dscores, 0, 0)) * SCALE
        for h in range(group):
            grads[:, h * E : (h + 1) * E] = query_part[:, h * rows : (h + 1) * rows].T.astype(BF16)
        grads[:, group * E : (group + 1) * E] = (dot(own_dscores, query, 1, 0) * SCALE).astype(BF16)
        grads[:, (group + 1) * E :] = dot(own_probs_low, grad, 1, 0).astype(BF16)

    ahead = products(packets[0], notes[0])
    for j in range(n):
        now = ahead
        if j + 1 < n:
            ahead = products(packets[j + 1], notes[j + 1])
        gradients(grads_out[j], **now, **soften(**now))

    for index in range(pieces if last else 0):
        for j in range(blocks):
            prompt, slot = slots[index][j]
            span = slice(slot * part, (slot + 1) * part)
            target = prefix_out[index]
            target[j, :, :E] = (key_acc[prompt, span, :] * SCALE).astype(target.dtype)
            target[j, :, E:] = value_acc[prompt, span, :].astype(target.dtype)


def attend(packets, notes, kv_in, sums, slots, out_types, prompts):
    n = len(packets)
    rows, packet_width = packets[0].shape
    group = (packet_width // E - 2) // 2
    first, last = not sums, bool(out_types)
    sums_shape = (prompts, PLEN, E)
    out_shape = [jax.ShapeDtypeStruct((rows, (group + 2) * E), BF16)] * n
    scratch_shapes = [pltpu.VMEM(sums_shape, BF16)] * 2
    if last:
        out_shape += [jax.ShapeDtypeStruct(kv_in[0].shape, kind) for kind in out_types]
        scratch_shapes += [pltpu.VMEM(sums_shape, F32)] * 2
    else:
        out_shape += [jax.ShapeDtypeStruct(sums_shape, F32)] * 2
    operands = [*packets, *notes, *kv_in, *sums]
    outs = pl.pallas_call(
        functools.partial(attend_kernel, slots, n, group, rows, first, last),
        out_shape=out_shape,
        in_specs=[VMEM] * len(operands),
        out_specs=[VMEM] * len(out_shape),
        scratch_shapes=scratch_shapes,
        compiler_params=params(32),
        cost_estimate=cost(20 * n * group * rows * (PLEN + rows) * E, 1024),
        name="attend_head",
    )(*operands)
    return outs[:n], outs[n:]


def total_kernel(n, keep_ref, *rest):
    parts, outs = rest[:-n], rest[-n:]
    for j in range(n):
        result = keep_ref[j]
        for part in parts:
            result = result + part[j].astype(F32)
        outs[j][...] = result.astype(BF16)


def total(keep, parts):
    n = keep.shape[0]
    return pl.pallas_call(
        functools.partial(total_kernel, n),
        out_shape=[jax.ShapeDtypeStruct(keep.shape[1:], BF16)] * n,
        in_specs=[VMEM] * (1 + len(parts)),
        out_specs=[VMEM] * n,
        compiler_params=params(),
        cost_estimate=cost(len(parts) * keep.size, (6 + 2 * len(parts)) * keep.size),
        name="total_prefix_grads",
    )(keep, *parts)


def prompt_kernel(n, *rest):
    shares, (kw_ref, vw_ref, out_ref, key_grad, value_grad) = rest[:n], rest[n:]

    @pl.when(pl.program_id(0) == 0)
    def _():
        head, _ = place()
        for j in range(n):
            key_grad[:, lanes(head ^ j, E)] = shares[j][:, :E]
            value_grad[:, lanes(head ^ j, E)] = shares[j][:, E:]

    out_ref[...] = (
        dot(key_grad[...], kw_ref[...], 1, 1) + dot(value_grad[...], vw_ref[...], 1, 1)
    ).astype(BF16)


def prompt_gradient(shares, key_weight, value_weight, chunk=1024):
    n = len(shares)
    rows = shares[0].shape[0]
    depth, width = key_weight.shape
    weight_spec = pl.BlockSpec((chunk, width), lambda i: (i, 0))
    return pl.pallas_call(
        functools.partial(prompt_kernel, n),
        grid=(depth // chunk,),
        out_shape=jax.ShapeDtypeStruct((rows, depth), BF16),
        in_specs=[pl.BlockSpec(shares[0].shape, lambda i: (0, 0))] * n
        + [weight_spec, weight_spec],
        out_specs=pl.BlockSpec((rows, chunk), lambda i: (0, i)),
        scratch_shapes=[pltpu.VMEM((rows, width), BF16)] * 2,
        compiler_params=params(),
        cost_estimate=cost(4 * rows * depth * width, 4 * depth * width + 2 * rows * depth),
        name="prompt_gradient",
    )(*shares, key_weight, value_weight)


def spread(number, bits):
    return sum(((number >> i) & 1) << bit for i, bit in enumerate(bits))


def per_device(
    n_prompt,
    n_resp,
    prompt_rows,
    key_weight,
    value_weight,
    queries,
    own_keys,
    own_values,
    out_grad,
    first_length,
    resp_prompt,
):
    devices = n_prompt * n_resp
    heads = own_keys.shape[1] // E
    every_bit = range(devices.bit_length() - 1)
    rest_bits = [bit for bit in GATHER_BITS if bit in every_bit]
    rest_bits += [bit for bit in every_bit if bit not in rest_bits and bit not in HEAD_BITS]
    member = [spread(j, HEAD_BITS) for j in range(heads)]

    def swap(x, offset):
        return lax.ppermute(x, ("prompt", "resp"), [(i, i ^ offset) for i in range(devices)])

    def swap_group(items):
        return [items[0]] + [swap(items[j], member[j]) for j in range(1, heads)]

    part = prompt_rows.shape[0]
    projected = project(
        first_length.reshape(1, 1), resp_prompt, prompt_rows, key_weight, value_weight, heads
    )
    projected, queries = lax.optimization_barrier((projected, queries))
    packed = pack(queries, out_grad, own_keys, own_values, heads)
    notes = swap_group(projected)
    notes, packed = lax.optimization_barrier((notes, packed))
    pieces = {0: jnp.stack([x[:part] for x in notes])}
    packets = swap_group(packed)
    for bit in rest_bits:
        for offset in list(pieces):
            pieces[offset | 1 << bit] = swap(pieces[offset], 1 << bit)
    offsets = list(pieces)

    filled = [0] * n_prompt
    slots = []
    for offset in offsets:
        places = []
        for j in range(heads):
            at = (offset ^ member[j]) // n_resp
            places.append((at, filled[at]))
            filled[at] += 1
        slots.append(tuple(places))

    first_out = 1 << rest_bits[-1]
    out_types = [BF16 if offset & first_out else F32 for offset in offsets]
    kv_in = [pieces[offset] for offset in offsets]
    slots = tuple(slots)
    early = heads - 1
    grads, sums = attend(packets[:early], notes[:early], kv_in, [], slots, [], n_prompt)
    last_grads, outs = attend(
        packets[early:], notes[early:], kv_in, sums, slots, out_types, n_prompt
    )
    sums = dict(zip(offsets, outs))
    arrived = {offset: [] for offset in offsets}
    for bit in reversed(rest_bits):
        sent = None
        for offset in reversed(offsets):
            if offset & 1 << bit:
                piece = sums.pop(offset)
                for part in arrived.pop(offset):
                    piece = piece + part.astype(F32)
                if bit == rest_bits[0]:
                    arrived[0][-1], last_grads = lax.optimization_barrier(
                        (arrived[0][-1], last_grads)
                    )
                if bit != rest_bits[-1] and offset == 1 << bit and sent is not None:
                    piece, ahead = lax.optimization_barrier((piece, arrived[sent][-1]))
                    arrived[sent][-1] = ahead
                arrived[offset ^ 1 << bit].append(swap(piece.astype(BF16), 1 << bit))
                sent = offset ^ 1 << bit
        offsets = list(sums)
    back = [swap(grads[j], member[j]) for j in range(1, early)]
    shares, back = lax.optimization_barrier((total(sums[0], arrived[0]), back))
    shares = swap_group(shares)
    back = [grads[0], *back, swap(last_grads[0], member[early])]
    query_grad, key_grad, value_grad = unpack(back, queries.shape[1], own_keys.shape[1])
    prompt_grad = prompt_gradient(shares, key_weight, value_weight)
    return (query_grad, key_grad, value_grad, prompt_grad)


def solution(mesh):
    both = P(("prompt", "resp"), None)
    return jax.shard_map(
        functools.partial(per_device, mesh.shape["prompt"], mesh.shape["resp"]),
        mesh=mesh,
        in_specs=(both, P(), P(), both, both, both, both, P(("prompt", "resp")), both),
        out_specs=(both, both, both, both),
        check_vma=False,
    )
```

```python
import functools
import math

import jax
import jax.numpy as jnp
from jax import lax
from jax.experimental import pallas as pl
from jax.experimental.pallas import tpu as pltpu
from jax.sharding import PartitionSpec as P

E = 128
PLEN = 512
SCALE = E ** (-0.5)
EXP2_SCALE = SCALE * math.log2(math.e)
HIDDEN = -1e30
BF16 = jnp.bfloat16
F32 = jnp.float32
NOTE_ROWS = 16
HEAD_BITS = (3, 4)
GATHER_BITS = (2, 1, 0)

ANY = pl.BlockSpec(memory_space=pl.ANY)
VMEM = pl.BlockSpec(memory_space=pltpu.VMEM)


def params(mebibytes=40):
    return pltpu.CompilerParams(vmem_limit_bytes=mebibytes * 1024 * 1024)


def cost(flops, bytes_accessed, transcendentals=0):
    return pl.CostEstimate(
        flops=int(flops), bytes_accessed=int(bytes_accessed), transcendentals=int(transcendentals)
    )


def lanes(index, width):
    return pl.ds(pl.multiple_of(index * width, 128), width)


def dot(a, b, a_dim, b_dim):
    return lax.dot_general(a, b, (((a_dim,), (b_dim,)), ((), ())), preferred_element_type=F32)


def place():
    prompt = lax.axis_index("prompt")
    device = prompt * lax.axis_size("resp") + lax.axis_index("resp")
    return sum(((device >> bit) & 1) << i for i, bit in enumerate(HEAD_BITS)), prompt


def project_kernel(n, steps, length_ref, prompts_ref, x_ref, kw_ref, vw_ref, *rest):
    outs, (x, kw, vw, key_sum, value_sum, length, prompts, sems, note_sems) = rest[:n], rest[n:]
    chunk = kw.shape[0] // steps
    copies = []
    for step in range(steps):
        span = slice(step * chunk, (step + 1) * chunk)
        for source, target in ((kw_ref, kw), (vw_ref, vw)):
            copies.append(
                pltpu.make_async_copy(
                    source.at[span, :], target.at[span, :], sems.at[len(copies)]
                )
            )
    note_copies = [
        pltpu.make_async_copy(length_ref, length, note_sems.at[0]),
        pltpu.make_async_copy(prompts_ref, prompts, note_sems.at[1]),
    ]
    x_copy = pltpu.make_async_copy(x_ref, x, note_sems.at[2])
    for copy in [copies[0], x_copy, *copies[1:], *note_copies]:
        copy.start()
    x_copy.wait()
    keys = values = None
    for step in range(steps):
        span = slice(step * chunk, (step + 1) * chunk)
        copies[2 * step].wait()
        part = dot(x[:, span], kw[span, :], 1, 0)
        keys = part if step == 0 else keys + part
        copies[2 * step + 1].wait()
        part = dot(x[:, span], vw[span, :], 1, 0)
        values = part if step == 0 else values + part
    key_sum[...] = keys.astype(BF16)
    value_sum[...] = values.astype(BF16)
    for copy in note_copies:
        copy.wait()
    lane = lax.broadcasted_iota(jnp.int32, (NOTE_ROWS, 2 * E), 1)
    row = lax.broadcasted_iota(jnp.int32, (NOTE_ROWS, 2 * E), 0)
    note = jnp.where(
        lane < E, length[0, 0], jnp.where(row < NOTE_ROWS // 2, prompts[0, 0], prompts[0, 1])
    )
    note = note.astype(F32).astype(BF16)
    head, _ = place()
    rows = x_ref.shape[0]
    for j in range(n):
        outs[j][:rows, :E] = key_sum[:, lanes(head ^ j, E)]
        outs[j][:rows, E:] = value_sum[:, lanes(head ^ j, E)]
        outs[j][rows:, :] = note


def project(first_length, resp_prompt, prompt_rows, key_weight, value_weight, n, steps=10):
    rows = prompt_rows.shape[0]
    depth, width = key_weight.shape
    return pl.pallas_call(
        functools.partial(project_kernel, n, steps),
        out_shape=[jax.ShapeDtypeStruct((rows + NOTE_ROWS, 2 * E), BF16)] * n,
        in_specs=[ANY] * 5,
        out_specs=[VMEM] * n,
        scratch_shapes=[pltpu.VMEM(prompt_rows.shape, BF16)]
        + [pltpu.VMEM(key_weight.shape, BF16)] * 2
        + [pltpu.VMEM((rows, width), BF16)] * 2
        + [pltpu.SMEM(first_length.shape, jnp.int32), pltpu.SMEM(resp_prompt.shape, jnp.int32)]
        + [pltpu.SemaphoreType.DMA((2 * steps,)), pltpu.SemaphoreType.DMA((3,))],
        compiler_params=params(60),
        cost_estimate=cost(4 * rows * depth * width, 4 * depth * width + 2 * rows * depth),
        name="project_prefix",
    )(first_length, resp_prompt, prompt_rows, key_weight, value_weight)


def pack_kernel(n, q_ref, g_ref, k_ref, v_ref, *outs):
    head, _ = place()
    for j in range(n):
        start = 0
        for source in (q_ref, g_ref, k_ref, v_ref):
            width = source.shape[1] // n
            outs[j][:, start : start + width] = source[:, lanes(head ^ j, width)]
            start += width


def pack(queries, out_grad, own_keys, own_values, n):
    rows = queries.shape[0]
    width = (2 * queries.shape[1] + 2 * own_keys.shape[1]) // n
    return pl.pallas_call(
        functools.partial(pack_kernel, n),
        out_shape=[jax.ShapeDtypeStruct((rows, width), BF16)] * n,
        in_specs=[VMEM] * 4,
        out_specs=[VMEM] * n,
        compiler_params=params(16),
        cost_estimate=cost(0, 4 * n * rows * width),
        name="pack_rows",
    )(queries, out_grad, own_keys, own_values)


def unpack_kernel(n, *rest):
    packets, targets = rest[:n], rest[n:]
    head, _ = place()
    for j in range(n):
        start = 0
        for target in targets:
            width = target.shape[1] // n
            target[:, lanes(head ^ j, width)] = packets[j][:, start : start + width]
            start += width


def unpack(packets, q_width, kv_width):
    n = len(packets)
    rows = packets[0].shape[0]
    return pl.pallas_call(
        functools.partial(unpack_kernel, n),
        out_shape=[
            jax.ShapeDtypeStruct((rows, width), BF16) for width in (q_width, kv_width, kv_width)
        ],
        in_specs=[VMEM] * n,
        out_specs=[VMEM] * 3,
        compiler_params=params(16),
        cost_estimate=cost(0, 4 * rows * (q_width + 2 * kv_width)),
        name="unpack_rows",
    )(*packets)


def attend_kernel(slots, n, group, rows, first, last, *rest):
    rest = list(rest)

    def take(count):
        taken = rest[:count]
        del rest[:count]
        return taken

    pieces = len(slots)
    packets = take(n)
    notes = take(n)
    kv_in = take(pieces)
    sums_in = take(0 if first else 2)
    grads_out = take(n)
    prefix_out = take(pieces if last else 0)
    if not last:
        key_acc, value_acc = take(2)
    keys, values = take(2)
    if last:
        key_acc, value_acc = take(2)
    part = kv_in[0].shape[1]
    blocks = kv_in[0].shape[0]
    _, prompt_place = place()

    for index in range(pieces):
        for j in range(blocks):
            prompt, slot = slots[index][j]
            span = slice(slot * part, (slot + 1) * part)
            keys[prompt, span, :] = kv_in[index][j, :, :E]
            values[prompt, span, :] = kv_in[index][j, :, E:]
    key_acc[...] = jnp.zeros_like(key_acc) if first else sums_in[0][...]
    value_acc[...] = jnp.zeros_like(value_acc) if first else sums_in[1][...]

    total_rows = group * rows
    row_in_column = lax.broadcasted_iota(jnp.int32, (total_rows, E), 0) & (rows - 1)
    row_in_lane = lax.broadcasted_iota(jnp.int32, (rows, total_rows), 1) & (rows - 1)
    own_key = lax.broadcasted_iota(jnp.int32, (rows, total_rows), 0)
    lane_row = lax.broadcasted_iota(jnp.int32, (E, total_rows), 1) & (rows - 1)

    def products(packet, note):
        note = note[part:, :].astype(F32)
        half = NOTE_ROWS // 2
        boundary, first_at, second_at = (
            jnp.max(block).astype(jnp.int32)
            for block in (note[:half, :E], note[:half, E:], note[half:, E:])
        )
        first_at, second_at = first_at ^ prompt_place, second_at ^ prompt_place
        heads = [packet[:, h * E : (h + 1) * E] for h in range(2 * group + 2)]
        query = jnp.concatenate(heads[:group], axis=0)
        grad = jnp.concatenate(heads[group : 2 * group], axis=0)
        own_k, own_v = heads[2 * group], heads[2 * group + 1]
        in_first = row_in_column < boundary

        def split(x):
            x = x.astype(F32)
            return jnp.concatenate(
                [jnp.where(in_first, x, 0.0), jnp.where(in_first, 0.0, x)], axis=1
            ).astype(BF16)

        query_pair = split(query)
        grad_pair = split(grad)
        key_pair = jnp.concatenate([keys[first_at], keys[second_at]], axis=1)
        value_pair = jnp.concatenate([values[first_at], values[second_at]], axis=1)

        visible = (own_key <= row_in_lane) & ((own_key >= boundary) == (row_in_lane >= boundary))
        return dict(
            boundary=boundary,
            first_at=first_at,
            second_at=second_at,
            query=query,
            grad=grad,
            own_k=own_k,
            query_pair=query_pair,
            grad_pair=grad_pair,
            key_pair=key_pair,
            scores=dot(key_pair, query_pair, 1, 1),
            own_scores=jnp.where(visible, dot(own_k, query, 1, 1), HIDDEN),
            dprobs=dot(value_pair, grad_pair, 1, 1),
            own_dprobs=dot(own_v, grad, 1, 1),
        )

    def soften(scores, own_scores, dprobs, own_dprobs, **_):
        top = jnp.maximum(
            jnp.max(scores, axis=0, keepdims=True), jnp.max(own_scores, axis=0, keepdims=True)
        )
        weight = jnp.exp2((scores - top) * EXP2_SCALE)
        own_weight = jnp.exp2((own_scores - top) * EXP2_SCALE)
        inverse = 1.0 / (
            jnp.sum(weight, axis=0, keepdims=True) + jnp.sum(own_weight, axis=0, keepdims=True)
        )
        probs = weight * inverse
        own_probs = own_weight * inverse
        probs_low = probs.astype(BF16)
        own_probs_low = own_probs.astype(BF16)
        delta = jnp.sum(probs_low.astype(F32) * dprobs, axis=0, keepdims=True) + jnp.sum(
            own_probs_low.astype(F32) * own_dprobs, axis=0, keepdims=True
        )
        return dict(
            probs_low=probs_low,
            own_probs_low=own_probs_low,
            dscores=(probs * (dprobs - delta)).astype(BF16),
            own_dscores=(own_probs * (own_dprobs - delta)).astype(BF16),
        )

    def gradients(
        grads, boundary, first_at, second_at, query, grad, own_k, query_pair, grad_pair, key_pair,
        probs_low, own_probs_low, dscores, own_dscores, **_
    ):
        key_part = dot(dscores, query_pair, 1, 0)
        value_part = dot(probs_low, grad_pair, 1, 0)
        key_acc[first_at] += key_part[:, :E]
        key_acc[second_at] += key_part[:, E:]
        value_acc[first_at] += value_part[:, :E]
        value_acc[second_at] += value_part[:, E:]

        query_both = dot(key_pair, dscores, 0, 0)
        query_part = jnp.where(lane_row < boundary, query_both[:E], query_both[E:])
        query_part = (query_part + dot(own_k, own_dscores, 0, 0)) * SCALE
        for h in range(group):
            grads[:, h * E : (h + 1) * E] = query_part[:, h * rows : (h + 1) * rows].T.astype(BF16)
        grads[:, group * E : (group + 1) * E] = (dot(own_dscores, query, 1, 0) * SCALE).astype(BF16)
        grads[:, (group + 1) * E :] = dot(own_probs_low, grad, 1, 0).astype(BF16)

    ahead = products(packets[0], notes[0])
    for j in range(n):
        now = ahead
        if j + 1 < n:
            ahead = products(packets[j + 1], notes[j + 1])
        gradients(grads_out[j], **now, **soften(**now))

    for index in range(pieces if last else 0):
        for j in range(blocks):
            prompt, slot = slots[index][j]
            span = slice(slot * part, (slot + 1) * part)
            target = prefix_out[index]
            target[j, :, :E] = (key_acc[prompt, span, :] * SCALE).astype(target.dtype)
            target[j, :, E:] = value_acc[prompt, span, :].astype(target.dtype)


def attend(packets, notes, kv_in, sums, slots, last, prompts):
    n = len(packets)
    rows, packet_width = packets[0].shape
    group = (packet_width // E - 2) // 2
    first = not sums
    sums_shape = (prompts, PLEN, E)
    out_shape = [jax.ShapeDtypeStruct((rows, (group + 2) * E), BF16)] * n
    scratch_shapes = [pltpu.VMEM(sums_shape, BF16)] * 2
    if last:
        out_shape += [
            jax.ShapeDtypeStruct(x.shape, BF16 if index % 2 else F32)
            for index, x in enumerate(kv_in)
        ]
        scratch_shapes += [pltpu.VMEM(sums_shape, F32)] * 2
    else:
        out_shape += [jax.ShapeDtypeStruct(sums_shape, F32)] * 2
    operands = [*packets, *notes, *kv_in, *sums]
    outs = pl.pallas_call(
        functools.partial(attend_kernel, slots, n, group, rows, first, last),
        out_shape=out_shape,
        in_specs=[VMEM] * len(operands),
        out_specs=[VMEM] * len(out_shape),
        scratch_shapes=scratch_shapes,
        compiler_params=params(32),
        cost_estimate=cost(0, 1024),
        name="attend_head",
    )(*operands)
    return outs[:n], outs[n:]


def total_kernel(n, keep_ref, *rest):
    parts, outs = rest[:-n], rest[-n:]
    for j in range(n):
        result = keep_ref[j]
        for part in parts:
            result = result + part[j].astype(F32)
        outs[j][...] = result.astype(BF16)


def total(keep, parts):
    n = keep.shape[0]
    return pl.pallas_call(
        functools.partial(total_kernel, n),
        out_shape=[jax.ShapeDtypeStruct(keep.shape[1:], BF16)] * n,
        in_specs=[VMEM] * (1 + len(parts)),
        out_specs=[VMEM] * n,
        compiler_params=params(16),
        cost_estimate=cost(0, 1 << 25),
        name="total_prefix_grads",
    )(keep, *parts)


def prompt_kernel(n, chunk, *rest):
    shares, (kw_ref, vw_ref, out_ref, key_grad, value_grad, out, sems) = rest[:n], rest[n:]
    head, _ = place()
    for j in range(n):
        key_grad[:, lanes(head ^ j, E)] = shares[j][:, :E]
        value_grad[:, lanes(head ^ j, E)] = shares[j][:, E:]
    copies = []
    for index in range(kw_ref.shape[0] // chunk):
        span = slice(index * chunk, (index + 1) * chunk)
        turned = dot(kw_ref[span, :], key_grad[...], 1, 1)
        turned = turned + dot(vw_ref[span, :], value_grad[...], 1, 1)
        out[:, span] = turned.T.astype(BF16)
        copies.append(pltpu.make_async_copy(out.at[:, span], out_ref.at[:, span], sems.at[index]))
        copies[-1].start()
    for copy in copies:
        copy.wait()


def prompt_gradient(shares, key_weight, value_weight, chunk=1024):
    n = len(shares)
    rows = shares[0].shape[0]
    depth, width = key_weight.shape
    return pl.pallas_call(
        functools.partial(prompt_kernel, n, chunk),
        out_shape=jax.ShapeDtypeStruct((rows, depth), BF16),
        in_specs=[VMEM] * (n + 2),
        out_specs=ANY,
        scratch_shapes=[pltpu.VMEM((rows, width), BF16)] * 2
        + [pltpu.VMEM((rows, depth), BF16), pltpu.SemaphoreType.DMA((depth // chunk,))],
        compiler_params=params(32),
        cost_estimate=cost(4 * rows * depth * width, 4 * depth * width + 2 * rows * depth),
        name="prompt_gradient",
    )(*shares, key_weight, value_weight)


def spread(number, bits):
    return sum(((number >> i) & 1) << bit for i, bit in enumerate(bits))


def per_device(
    n_prompt,
    n_resp,
    prompt_rows,
    key_weight,
    value_weight,
    queries,
    own_keys,
    own_values,
    out_grad,
    first_length,
    resp_prompt,
):
    devices = n_prompt * n_resp
    heads = own_keys.shape[1] // E
    every_bit = range(devices.bit_length() - 1)
    rest_bits = [bit for bit in GATHER_BITS if bit in every_bit]
    rest_bits += [bit for bit in every_bit if bit not in rest_bits and bit not in HEAD_BITS]
    member = [spread(j, HEAD_BITS) for j in range(heads)]

    def swap(x, offset):
        return lax.ppermute(x, ("prompt", "resp"), [(i, i ^ offset) for i in range(devices)])

    def swap_group(items):
        return [items[0]] + [swap(items[j], member[j]) for j in range(1, heads)]

    part = prompt_rows.shape[0]
    projected = project(
        first_length.reshape(1, 1), resp_prompt, prompt_rows, key_weight, value_weight, heads
    )
    projected, queries = lax.optimization_barrier((projected, queries))
    packed = pack(queries, out_grad, own_keys, own_values, heads)
    notes = swap_group(projected)
    notes, packed = lax.optimization_barrier((notes, packed))
    pieces = {0: jnp.stack([x[:part] for x in notes])}
    packets = swap_group(packed)
    for bit in rest_bits:
        for offset in list(pieces):
            pieces[offset | 1 << bit] = swap(pieces[offset], 1 << bit)
    core = 1 << rest_bits[-1]
    offsets = [o ^ c for o in pieces if not o & core for c in (0, core)]

    filled = [0] * n_prompt
    slots = []
    for offset in offsets:
        places = []
        for j in range(heads):
            at = (offset ^ member[j]) // n_resp
            places.append((at, filled[at]))
            filled[at] += 1
        slots.append(tuple(places))

    kv_in = [pieces[offset] for offset in offsets]
    slots = tuple(slots)
    early = heads - 1
    grads, sums = attend(packets[:early], notes[:early], kv_in, [], slots, False, n_prompt)
    back = [grads[0]] + [swap(grads[j], member[j]) for j in range(1, early)]
    last_grads, outs = attend(packets[early:], notes[early:], kv_in, sums, slots, True, n_prompt)

    keep = outs[0::2]
    sent = [swap(piece, core) for piece in outs[1::2]]
    sent, last_grads = lax.optimization_barrier((sent, last_grads))
    arrived = []
    for index in range(1, len(keep)):
        piece = (keep[index] + sent[index].astype(F32)).astype(BF16)
        arrived.append(swap(piece, offsets[2 * index]))
    back.append(swap(last_grads[0], member[early]))
    shares = swap_group(total(keep[0], [sent[0], *arrived]))
    unpacked = unpack(back, queries.shape[1], own_keys.shape[1])
    shares, unpacked = lax.optimization_barrier((shares, unpacked))
    query_grad, key_grad, value_grad = unpacked
    prompt_grad = prompt_gradient(shares, key_weight, value_weight)
    return (query_grad, key_grad, value_grad, prompt_grad)


def solution(mesh):
    both = P(("prompt", "resp"), None)
    return jax.shard_map(
        functools.partial(per_device, mesh.shape["prompt"], mesh.shape["resp"]),
        mesh=mesh,
        in_specs=(both, P(), P(), both, both, both, both, P(("prompt", "resp")), both),
        out_specs=(both, both, both, both),
        check_vma=False,
    )
```

```python
import functools
import math

import jax
import jax.numpy as jnp
from jax import lax
from jax.experimental import pallas as pl
from jax.experimental.pallas import tpu as pltpu
from jax.sharding import PartitionSpec as P

E = 128
PLEN = 512
SCALE = E ** (-0.5)
EXP2_SCALE = SCALE * math.log2(math.e)
HIDDEN = -1e30
BF16 = jnp.bfloat16
F32 = jnp.float32
NOTE_ROWS = 16
HEAD_BITS = (3, 4)
GATHER_BITS = (2, 1, 0)

ANY = pl.BlockSpec(memory_space=pl.ANY)
VMEM = pl.BlockSpec(memory_space=pltpu.VMEM)


def params(mebibytes=40):
    return pltpu.CompilerParams(vmem_limit_bytes=mebibytes * 1024 * 1024)


def cost(flops, bytes_accessed, transcendentals=0):
    return pl.CostEstimate(
        flops=int(flops), bytes_accessed=int(bytes_accessed), transcendentals=int(transcendentals)
    )


def lanes(index, width):
    return pl.ds(pl.multiple_of(index * width, 128), width)


def dot(a, b, a_dim, b_dim):
    return lax.dot_general(a, b, (((a_dim,), (b_dim,)), ((), ())), preferred_element_type=F32)


def place():
    prompt = lax.axis_index("prompt")
    device = prompt * lax.axis_size("resp") + lax.axis_index("resp")
    return sum(((device >> bit) & 1) << i for i, bit in enumerate(HEAD_BITS)), prompt


def project_kernel(n, steps, length_ref, prompts_ref, x_ref, kw_ref, vw_ref, *rest):
    outs, (kw, vw, key_sum, value_sum, length, prompts, sems, note_sems) = rest[:n], rest[n:]
    chunk = kw.shape[0] // steps
    copies = []
    for step in range(steps):
        span = slice(step * chunk, (step + 1) * chunk)
        for source, target in ((kw_ref, kw), (vw_ref, vw)):
            copies.append(
                pltpu.make_async_copy(
                    source.at[span, :], target.at[span, :], sems.at[len(copies)]
                )
            )
    note_copies = [
        pltpu.make_async_copy(length_ref, length, note_sems.at[0]),
        pltpu.make_async_copy(prompts_ref, prompts, note_sems.at[1]),
    ]
    for copy in copies + note_copies:
        copy.start()
    keys = values = None
    for step in range(steps):
        span = slice(step * chunk, (step + 1) * chunk)
        copies[2 * step].wait()
        part = dot(x_ref[:, span], kw[span, :], 1, 0)
        keys = part if step == 0 else keys + part
        copies[2 * step + 1].wait()
        part = dot(x_ref[:, span], vw[span, :], 1, 0)
        values = part if step == 0 else values + part
    key_sum[...] = keys.astype(BF16)
    value_sum[...] = values.astype(BF16)
    for copy in note_copies:
        copy.wait()
    lane = lax.broadcasted_iota(jnp.int32, (NOTE_ROWS, 2 * E), 1)
    row = lax.broadcasted_iota(jnp.int32, (NOTE_ROWS, 2 * E), 0)
    note = jnp.where(
        lane < E, length[0, 0], jnp.where(row < NOTE_ROWS // 2, prompts[0, 0], prompts[0, 1])
    )
    note = note.astype(F32).astype(BF16)
    head, _ = place()
    rows = x_ref.shape[0]
    for j in range(n):
        outs[j][:rows, :E] = key_sum[:, lanes(head ^ j, E)]
        outs[j][:rows, E:] = value_sum[:, lanes(head ^ j, E)]
        outs[j][rows:, :] = note


def project(first_length, resp_prompt, prompt_rows, key_weight, value_weight, n, steps=10):
    rows = prompt_rows.shape[0]
    depth, width = key_weight.shape
    return pl.pallas_call(
        functools.partial(project_kernel, n, steps),
        out_shape=[jax.ShapeDtypeStruct((rows + NOTE_ROWS, 2 * E), BF16)] * n,
        in_specs=[ANY, ANY, VMEM, ANY, ANY],
        out_specs=[VMEM] * n,
        scratch_shapes=[pltpu.VMEM(key_weight.shape, BF16)] * 2
        + [pltpu.VMEM((rows, width), BF16)] * 2
        + [pltpu.SMEM(first_length.shape, jnp.int32), pltpu.SMEM(resp_prompt.shape, jnp.int32)]
        + [pltpu.SemaphoreType.DMA((2 * steps,)), pltpu.SemaphoreType.DMA((2,))],
        compiler_params=params(60),
        cost_estimate=cost(4 * rows * depth * width, 4 * depth * width + 2 * rows * depth),
        name="project_prefix",
    )(first_length, resp_prompt, prompt_rows, key_weight, value_weight)


def pack_kernel(n, q_ref, g_ref, k_ref, v_ref, *outs):
    head, _ = place()
    for j in range(n):
        start = 0
        for source in (q_ref, g_ref, k_ref, v_ref):
            width = source.shape[1] // n
            outs[j][:, start : start + width] = source[:, lanes(head ^ j, width)]
            start += width


def pack(queries, out_grad, own_keys, own_values, n):
    rows = queries.shape[0]
    width = (2 * queries.shape[1] + 2 * own_keys.shape[1]) // n
    return pl.pallas_call(
        functools.partial(pack_kernel, n),
        out_shape=[jax.ShapeDtypeStruct((rows, width), BF16)] * n,
        in_specs=[VMEM] * 4,
        out_specs=[VMEM] * n,
        compiler_params=params(16),
        cost_estimate=cost(0, 4 * n * rows * width),
        name="pack_rows",
    )(queries, out_grad, own_keys, own_values)


def unpack_kernel(n, *rest):
    packets, targets = rest[:n], rest[n:]
    head, _ = place()
    for j in range(n):
        start = 0
        for target in targets:
            width = target.shape[1] // n
            target[:, lanes(head ^ j, width)] = packets[j][:, start : start + width]
            start += width


def unpack(packets, q_width, kv_width):
    n = len(packets)
    rows = packets[0].shape[0]
    return pl.pallas_call(
        functools.partial(unpack_kernel, n),
        out_shape=[
            jax.ShapeDtypeStruct((rows, width), BF16) for width in (q_width, kv_width, kv_width)
        ],
        in_specs=[VMEM] * n,
        out_specs=[VMEM] * 3,
        compiler_params=params(16),
        cost_estimate=cost(0, 4 * rows * (q_width + 2 * kv_width)),
        name="unpack_rows",
    )(*packets)


def attend_kernel(slots, n, group, rows, first, last, *rest):
    rest = list(rest)

    def take(count):
        taken = rest[:count]
        del rest[:count]
        return taken

    pieces = len(slots)
    packets = take(n)
    notes = take(n)
    kv_in = take(pieces)
    sums_in = take(0 if first else 2)
    grads_out = take(n)
    prefix_out = take(pieces if last else 0)
    if not last:
        key_acc, value_acc = take(2)
    keys, values = take(2)
    if last:
        key_acc, value_acc = take(2)
    part = kv_in[0].shape[1]
    blocks = kv_in[0].shape[0]
    _, prompt_place = place()

    for index in range(pieces):
        for j in range(blocks):
            prompt, slot = slots[index][j]
            span = slice(slot * part, (slot + 1) * part)
            keys[prompt, span, :] = kv_in[index][j, :, :E]
            values[prompt, span, :] = kv_in[index][j, :, E:]
    key_acc[...] = jnp.zeros_like(key_acc) if first else sums_in[0][...]
    value_acc[...] = jnp.zeros_like(value_acc) if first else sums_in[1][...]

    total_rows = group * rows
    row_in_column = lax.broadcasted_iota(jnp.int32, (total_rows, E), 0) & (rows - 1)
    row_in_lane = lax.broadcasted_iota(jnp.int32, (rows, total_rows), 1) & (rows - 1)
    own_key = lax.broadcasted_iota(jnp.int32, (rows, total_rows), 0)
    lane_row = lax.broadcasted_iota(jnp.int32, (E, total_rows), 1) & (rows - 1)

    def products(packet, note):
        note = note[part:, :].astype(F32)
        half = NOTE_ROWS // 2
        boundary, first_at, second_at = (
            jnp.max(block).astype(jnp.int32)
            for block in (note[:half, :E], note[:half, E:], note[half:, E:])
        )
        first_at, second_at = first_at ^ prompt_place, second_at ^ prompt_place
        heads = [packet[:, h * E : (h + 1) * E] for h in range(2 * group + 2)]
        query = jnp.concatenate(heads[:group], axis=0)
        grad = jnp.concatenate(heads[group : 2 * group], axis=0)
        own_k, own_v = heads[2 * group], heads[2 * group + 1]
        in_first = row_in_column < boundary

        def split(x):
            x = x.astype(F32)
            return jnp.concatenate(
                [jnp.where(in_first, x, 0.0), jnp.where(in_first, 0.0, x)], axis=1
            ).astype(BF16)

        query_pair = split(query)
        grad_pair = split(grad)
        key_pair = jnp.concatenate([keys[first_at], keys[second_at]], axis=1)
        value_pair = jnp.concatenate([values[first_at], values[second_at]], axis=1)

        visible = (own_key <= row_in_lane) & ((own_key >= boundary) == (row_in_lane >= boundary))
        return dict(
            boundary=boundary,
            first_at=first_at,
            second_at=second_at,
            query=query,
            grad=grad,
            own_k=own_k,
            query_pair=query_pair,
            grad_pair=grad_pair,
            key_pair=key_pair,
            scores=dot(key_pair, query_pair, 1, 1),
            own_scores=jnp.where(visible, dot(own_k, query, 1, 1), HIDDEN),
            dprobs=dot(value_pair, grad_pair, 1, 1),
            own_dprobs=dot(own_v, grad, 1, 1),
        )

    def soften(scores, own_scores, dprobs, own_dprobs, **_):
        top = jnp.maximum(
            jnp.max(scores, axis=0, keepdims=True), jnp.max(own_scores, axis=0, keepdims=True)
        )
        weight = jnp.exp2((scores - top) * EXP2_SCALE)
        own_weight = jnp.exp2((own_scores - top) * EXP2_SCALE)
        inverse = 1.0 / (
            jnp.sum(weight, axis=0, keepdims=True) + jnp.sum(own_weight, axis=0, keepdims=True)
        )
        probs = weight * inverse
        own_probs = own_weight * inverse
        probs_low = probs.astype(BF16)
        own_probs_low = own_probs.astype(BF16)
        delta = jnp.sum(probs_low.astype(F32) * dprobs, axis=0, keepdims=True) + jnp.sum(
            own_probs_low.astype(F32) * own_dprobs, axis=0, keepdims=True
        )
        return dict(
            probs_low=probs_low,
            own_probs_low=own_probs_low,
            dscores=(probs * (dprobs - delta)).astype(BF16),
            own_dscores=(own_probs * (own_dprobs - delta)).astype(BF16),
        )

    def gradients(
        grads, boundary, first_at, second_at, query, grad, own_k, query_pair, grad_pair, key_pair,
        probs_low, own_probs_low, dscores, own_dscores, **_
    ):
        key_part = dot(dscores, query_pair, 1, 0)
        value_part = dot(probs_low, grad_pair, 1, 0)
        key_acc[first_at] += key_part[:, :E]
        key_acc[second_at] += key_part[:, E:]
        value_acc[first_at] += value_part[:, :E]
        value_acc[second_at] += value_part[:, E:]

        query_both = dot(key_pair, dscores, 0, 0)
        query_part = jnp.where(lane_row < boundary, query_both[:E], query_both[E:])
        query_part = (query_part + dot(own_k, own_dscores, 0, 0)) * SCALE
        for h in range(group):
            grads[:, h * E : (h + 1) * E] = query_part[:, h * rows : (h + 1) * rows].T.astype(BF16)
        grads[:, group * E : (group + 1) * E] = (dot(own_dscores, query, 1, 0) * SCALE).astype(BF16)
        grads[:, (group + 1) * E :] = dot(own_probs_low, grad, 1, 0).astype(BF16)

    ahead = products(packets[0], notes[0])
    for j in range(n):
        now = ahead
        if j + 1 < n:
            ahead = products(packets[j + 1], notes[j + 1])
        gradients(grads_out[j], **now, **soften(**now))

    for index in range(pieces if last else 0):
        for j in range(blocks):
            prompt, slot = slots[index][j]
            span = slice(slot * part, (slot + 1) * part)
            target = prefix_out[index]
            target[j, :, :E] = (key_acc[prompt, span, :] * SCALE).astype(target.dtype)
            target[j, :, E:] = value_acc[prompt, span, :].astype(target.dtype)


def attend(packets, notes, kv_in, sums, slots, last, prompts):
    n = len(packets)
    rows, packet_width = packets[0].shape
    group = (packet_width // E - 2) // 2
    first = not sums
    sums_shape = (prompts, PLEN, E)
    out_shape = [jax.ShapeDtypeStruct((rows, (group + 2) * E), BF16)] * n
    scratch_shapes = [pltpu.VMEM(sums_shape, BF16)] * 2
    if last:
        out_shape += [
            jax.ShapeDtypeStruct(x.shape, BF16 if index % 2 else F32)
            for index, x in enumerate(kv_in)
        ]
        scratch_shapes += [pltpu.VMEM(sums_shape, F32)] * 2
    else:
        out_shape += [jax.ShapeDtypeStruct(sums_shape, F32)] * 2
    operands = [*packets, *notes, *kv_in, *sums]
    outs = pl.pallas_call(
        functools.partial(attend_kernel, slots, n, group, rows, first, last),
        out_shape=out_shape,
        in_specs=[VMEM] * len(operands),
        out_specs=[VMEM] * len(out_shape),
        scratch_shapes=scratch_shapes,
        compiler_params=params(32),
        cost_estimate=cost(0, 1024),
        name="attend_head",
    )(*operands)
    return outs[:n], outs[n:]


def total_kernel(n, keep_ref, *rest):
    parts, outs = rest[:-n], rest[-n:]
    for j in range(n):
        result = keep_ref[j]
        for part in parts:
            result = result + part[j].astype(F32)
        outs[j][...] = result.astype(BF16)


def total(keep, parts):
    n = keep.shape[0]
    return pl.pallas_call(
        functools.partial(total_kernel, n),
        out_shape=[jax.ShapeDtypeStruct(keep.shape[1:], BF16)] * n,
        in_specs=[VMEM] * (1 + len(parts)),
        out_specs=[VMEM] * n,
        compiler_params=params(16),
        cost_estimate=cost(0, 1 << 25),
        name="total_prefix_grads",
    )(keep, *parts)


def prompt_kernel(n, chunk, *rest):
    shares, (kw_ref, vw_ref, out_ref, key_grad, value_grad, out, sems) = rest[:n], rest[n:]
    head, _ = place()
    for j in range(n):
        key_grad[:, lanes(head ^ j, E)] = shares[j][:, :E]
        value_grad[:, lanes(head ^ j, E)] = shares[j][:, E:]
    copies = []
    for index in range(kw_ref.shape[0] // chunk):
        span = slice(index * chunk, (index + 1) * chunk)
        turned = dot(kw_ref[span, :], key_grad[...], 1, 1)
        turned = turned + dot(vw_ref[span, :], value_grad[...], 1, 1)
        out[:, span] = turned.T.astype(BF16)
        copies.append(pltpu.make_async_copy(out.at[:, span], out_ref.at[:, span], sems.at[index]))
        copies[-1].start()
    for copy in copies:
        copy.wait()


def prompt_gradient(shares, key_weight, value_weight, chunk=1024):
    n = len(shares)
    rows = shares[0].shape[0]
    depth, width = key_weight.shape
    return pl.pallas_call(
        functools.partial(prompt_kernel, n, chunk),
        out_shape=jax.ShapeDtypeStruct((rows, depth), BF16),
        in_specs=[VMEM] * (n + 2),
        out_specs=ANY,
        scratch_shapes=[pltpu.VMEM((rows, width), BF16)] * 2
        + [pltpu.VMEM((rows, depth), BF16), pltpu.SemaphoreType.DMA((depth // chunk,))],
        compiler_params=params(32),
        cost_estimate=cost(4 * rows * depth * width, 4 * depth * width + 2 * rows * depth),
        name="prompt_gradient",
    )(*shares, key_weight, value_weight)


def spread(number, bits):
    return sum(((number >> i) & 1) << bit for i, bit in enumerate(bits))


def per_device(
    n_prompt,
    n_resp,
    prompt_rows,
    key_weight,
    value_weight,
    queries,
    own_keys,
    own_values,
    out_grad,
    first_length,
    resp_prompt,
):
    devices = n_prompt * n_resp
    heads = own_keys.shape[1] // E
    every_bit = range(devices.bit_length() - 1)
    rest_bits = [bit for bit in GATHER_BITS if bit in every_bit]
    rest_bits += [bit for bit in every_bit if bit not in rest_bits and bit not in HEAD_BITS]
    member = [spread(j, HEAD_BITS) for j in range(heads)]

    def swap(x, offset):
        return lax.ppermute(x, ("prompt", "resp"), [(i, i ^ offset) for i in range(devices)])

    def swap_group(items):
        return [items[0]] + [swap(items[j], member[j]) for j in range(1, len(items))]

    part = prompt_rows.shape[0]
    projected = project(
        first_length.reshape(1, 1), resp_prompt, prompt_rows, key_weight, value_weight, heads
    )
    projected, queries = lax.optimization_barrier((projected, queries))
    packed = pack(queries, out_grad, own_keys, own_values, heads)
    notes = swap_group(projected)
    notes, packed = lax.optimization_barrier((notes, packed))
    pieces = {0: jnp.stack([x[:part] for x in notes])}
    packets = swap_group(packed[:-1])
    for bit in rest_bits:
        for offset in list(pieces):
            pieces[offset | 1 << bit] = swap(pieces[offset], 1 << bit)
        if len(pieces) == 2:
            pieces[1 << bit], late = lax.optimization_barrier((pieces[1 << bit], packed[-1]))
            packets.append(swap(late, member[-1]))
    core = 1 << rest_bits[-1]
    offsets = [o ^ c for o in pieces if not o & core for c in (0, core)]

    filled = [0] * n_prompt
    slots = []
    for offset in offsets:
        places = []
        for j in range(heads):
            at = (offset ^ member[j]) // n_resp
            places.append((at, filled[at]))
            filled[at] += 1
        slots.append(tuple(places))

    kv_in = [pieces[offset] for offset in offsets]
    slots = tuple(slots)
    early = heads - 1
    grads, sums = attend(packets[:early], notes[:early], kv_in, [], slots, False, n_prompt)
    back = [grads[0]] + [swap(grads[j], member[j]) for j in range(1, early)]
    last_grads, outs = attend(packets[early:], notes[early:], kv_in, sums, slots, True, n_prompt)

    sent = [swap(piece, core) for piece in outs[1::2]]
    sent, last_grads = lax.optimization_barrier((sent, last_grads))
    sums = dict(zip(offsets[0::2], outs[0::2]))
    arrived = {offset: [part] for offset, part in zip(sums, sent)}
    for bit in reversed(rest_bits[:-1]):
        first = None
        for offset in sorted(sums, reverse=True):
            if offset & 1 << bit:
                piece = sums.pop(offset)
                for part in arrived.pop(offset):
                    piece = piece + part.astype(F32)
                if offset == 1 << bit and first is not None:
                    piece, arrived[first][-1] = lax.optimization_barrier(
                        (piece, arrived[first][-1])
                    )
                arrived[offset ^ 1 << bit].append(swap(piece.astype(BF16), 1 << bit))
                first = offset ^ 1 << bit if first is None else first
    back.append(swap(last_grads[0], member[early]))
    shares = swap_group(total(sums[0], arrived[0]))
    unpacked = unpack(back, queries.shape[1], own_keys.shape[1])
    shares, unpacked = lax.optimization_barrier((shares, unpacked))
    query_grad, key_grad, value_grad = unpacked
    prompt_grad = prompt_gradient(shares, key_weight, value_weight)
    return (query_grad, key_grad, value_grad, prompt_grad)


def solution(mesh):
    both = P(("prompt", "resp"), None)
    return jax.shard_map(
        functools.partial(per_device, mesh.shape["prompt"], mesh.shape["resp"]),
        mesh=mesh,
        in_specs=(both, P(), P(), both, both, both, both, P(("prompt", "resp")), both),
        out_specs=(both, both, both, both),
        check_vma=False,
    )
```

```python
import functools
import math

import jax
import jax.numpy as jnp
from jax import lax
from jax.experimental import pallas as pl
from jax.experimental.pallas import tpu as pltpu
from jax.sharding import PartitionSpec as P

E = 128
PLEN = 512
SCALE = E ** (-0.5)
EXP2_SCALE = SCALE * math.log2(math.e)
HIDDEN = -1e30
BF16 = jnp.bfloat16
F32 = jnp.float32
NOTE_ROWS = 32
CORE, X, Y = 0, 3, 4
GATHER_BITS = (2, 1)
MEMBERS = (0, 1 << CORE, 1 << X, 1 << X | 1 << CORE)

SMEM = pl.BlockSpec(memory_space=pltpu.SMEM)
ANY = pl.BlockSpec(memory_space=pl.ANY)
VMEM = pl.BlockSpec(memory_space=pltpu.VMEM)


def params(mebibytes=40):
    return pltpu.CompilerParams(vmem_limit_bytes=mebibytes * 1024 * 1024)


def cost(flops, bytes_accessed, transcendentals=0):
    return pl.CostEstimate(
        flops=int(flops), bytes_accessed=int(bytes_accessed), transcendentals=int(transcendentals)
    )


def lanes(index, width):
    return pl.ds(pl.multiple_of(index * width, 128), width)


def dot(a, b, a_dim, b_dim):
    return lax.dot_general(a, b, (((a_dim,), (b_dim,)), ((), ())), preferred_element_type=F32)


def crossed(offset, core):
    change = ((offset >> X) ^ (offset >> Y)) & core
    return offset ^ (change << X | change << Y)


def place():
    prompt = lax.axis_index("prompt")
    device = prompt * lax.axis_size("resp") + lax.axis_index("resp")
    core, x, y = ((device >> bit) & 1 for bit in (CORE, X, Y))
    own, other = jnp.where(core == 0, x, 2 + y), jnp.where(core == 0, 2 + y, x)
    return (own, other, own ^ 1, other ^ 1), core, prompt


def project_kernel(steps, note_ref, other_note_ref, x_ref, other_ref, kw_ref, vw_ref, *rest):
    keep_ref, send_ref, rows_in, weights, sums, sems, row_sems = rest
    heads, core, _ = place()
    width = weights.shape[1] // 2
    chunk = weights.shape[0] // steps
    copies = []
    for step in range(steps):
        span = slice(step * chunk, (step + 1) * chunk)
        for index, source in enumerate((kw_ref, vw_ref)):
            copies.append(
                pltpu.make_async_copy(
                    source.at[span, lanes(core, width)],
                    weights.at[span, index * width : (index + 1) * width],
                    sems.at[len(copies)],
                )
            )
    part = x_ref.shape[0]
    row_copies = [
        pltpu.make_async_copy(source, rows_in.at[at : at + part, :], row_sems.at[index])
        for index, (source, at) in enumerate(((x_ref, 0), (other_ref, part)))
    ]
    for copy in row_copies + copies[:4]:
        copy.start()
    for copy in row_copies:
        copy.wait()
    total = None
    for step in range(steps):
        span = slice(step * chunk, (step + 1) * chunk)
        copies[2 * step].wait()
        copies[2 * step + 1].wait()
        for copy in copies[2 * step + 4 : 2 * step + 6]:
            copy.start()
        product = dot(rows_in[:, span], weights[span, :], 1, 0)
        total = product if step == 0 else total + product
    sums[...] = total.astype(BF16)
    lane = lax.broadcasted_iota(jnp.int32, (NOTE_ROWS, 2 * E), 1)
    row = lax.broadcasted_iota(jnp.int32, (NOTE_ROWS, 2 * E), 0)
    note = jnp.where(
        row < NOTE_ROWS // 4,
        jnp.where(lane < E, note_ref[0], note_ref[1]),
        jnp.where(
            row < NOTE_ROWS // 2,
            note_ref[2],
            jnp.where(
                row < 3 * (NOTE_ROWS // 4),
                jnp.where(lane < E, other_note_ref[0], other_note_ref[1]),
                other_note_ref[2],
            ),
        ),
    )
    note = note.astype(F32).astype(BF16)
    rows = sums.shape[0]
    for out, head in ((keep_ref, heads[0] & 1), (send_ref, heads[2] & 1)):
        out[:rows, :E] = sums[:, lanes(head, E)]
        out[:rows, E:] = sums[:, lanes(head + 2, E)]
        out[rows:, :] = note


def project(note, other_note, prompt_rows, other_rows, key_weight, value_weight, steps=5):
    rows = 2 * prompt_rows.shape[0]
    depth, width = key_weight.shape
    return pl.pallas_call(
        functools.partial(project_kernel, steps),
        out_shape=[jax.ShapeDtypeStruct((rows + NOTE_ROWS, 2 * E), BF16)] * 2,
        in_specs=[SMEM, SMEM] + [ANY] * 4,
        out_specs=[VMEM] * 2,
        scratch_shapes=[
            pltpu.VMEM((rows, depth), BF16),
            pltpu.VMEM((depth, width), BF16),
            pltpu.VMEM((rows, width), BF16),
            pltpu.SemaphoreType.DMA((2 * steps,)),
            pltpu.SemaphoreType.DMA((2,)),
        ],
        compiler_params=params(50),
        cost_estimate=cost(2 * rows * depth * width, 2 * depth * width + 2 * rows * depth),
        name="project_prefix",
    )(note, other_note, prompt_rows, other_rows, key_weight, value_weight)


def pack_kernel(q_ref, g_ref, k_ref, v_ref, *outs):
    heads, _, _ = place()
    for head, out in zip(heads, outs):
        start = 0
        for source in (q_ref, g_ref, k_ref, v_ref):
            width = source.shape[1] // len(outs)
            out[:, start : start + width] = source[:, lanes(head, width)]
            start += width


def pack(queries, out_grad, own_keys, own_values):
    rows = queries.shape[0]
    n = len(MEMBERS)
    width = (2 * queries.shape[1] + 2 * own_keys.shape[1]) // n
    return pl.pallas_call(
        pack_kernel,
        out_shape=[jax.ShapeDtypeStruct((rows, width), BF16)] * n,
        in_specs=[VMEM] * 4,
        out_specs=[VMEM] * n,
        compiler_params=params(62),
        cost_estimate=cost(0, 4 * n * rows * width),
        name="pack_rows",
    )(queries, out_grad, own_keys, own_values)


def unpack_kernel(n, *rest):
    packets, targets = rest[:n], rest[n:]
    heads, _, _ = place()
    for head, packet in zip(heads, packets):
        start = 0
        for target in targets:
            width = target.shape[1] // n
            target[:, lanes(head, width)] = packet[:, start : start + width]
            start += width


def unpack(packets, q_width, kv_width):
    n = len(packets)
    rows = packets[0].shape[0]
    return pl.pallas_call(
        functools.partial(unpack_kernel, n),
        out_shape=[
            jax.ShapeDtypeStruct((rows, width), BF16) for width in (q_width, kv_width, kv_width)
        ],
        in_specs=[VMEM] * n,
        out_specs=[VMEM] * 3,
        compiler_params=params(16),
        cost_estimate=cost(0, 4 * rows * (q_width + 2 * kv_width)),
        name="unpack_rows",
    )(*packets)


def attend_kernel(slots, group, rows, resp_bits, *rest):
    rest = list(rest)

    def take(count):
        taken = rest[:count]
        del rest[:count]
        return taken

    pieces = len(slots)
    n = len(MEMBERS)
    packets = take(n)
    notes = take(2)
    kv_in = take(pieces)
    grads_out = take(n)
    prefix_out = take(pieces)
    keys, values, key_acc, value_acc = rest
    blocks, part, _ = kv_in[0].shape
    _, core, prompt_place = place()

    for index in range(pieces):
        for j in range(blocks):
            prompt, slot = slots[index][j]
            span = slice(slot * part, (slot + 1) * part)
            keys[prompt, span, :] = kv_in[index][j, :, :E]
            values[prompt, span, :] = kv_in[index][j, :, E:]
    key_acc[...] = jnp.zeros_like(key_acc)
    value_acc[...] = jnp.zeros_like(value_acc)

    total_rows = group * rows
    row_in_column = lax.broadcasted_iota(jnp.int32, (total_rows, E), 0) & (rows - 1)
    row_in_lane = lax.broadcasted_iota(jnp.int32, (rows, total_rows), 1) & (rows - 1)
    own_key = lax.broadcasted_iota(jnp.int32, (rows, total_rows), 0)
    lane_row = lax.broadcasted_iota(jnp.int32, (E, total_rows), 1) & (rows - 1)

    def products(j):
        packet = packets[j]
        note = notes[j // 2][2 * part :, :].astype(F32)
        step = NOTE_ROWS // 4
        at = 2 * step * (j % 2)
        boundary, first_at, second_at = (
            jnp.max(block).astype(jnp.int32)
            for block in (
                note[at : at + step, :E],
                note[at : at + step, E:],
                note[at + step : at + 2 * step, E:],
            )
        )
        first_at, second_at = (
            crossed((prompt ^ prompt_place) << resp_bits, core) >> resp_bits
            for prompt in (first_at, second_at)
        )
        heads = [packet[:, h * E : (h + 1) * E] for h in range(2 * group + 2)]
        query = jnp.concatenate(heads[:group], axis=0)
        grad = jnp.concatenate(heads[group : 2 * group], axis=0)
        own_k, own_v = heads[2 * group], heads[2 * group + 1]
        in_first = row_in_column < boundary

        def split(x):
            x = x.astype(F32)
            return jnp.concatenate(
                [jnp.where(in_first, x, 0.0), jnp.where(in_first, 0.0, x)], axis=1
            ).astype(BF16)

        query_pair = split(query)
        grad_pair = split(grad)
        key_pair = jnp.concatenate([keys[first_at], keys[second_at]], axis=1)
        value_pair = jnp.concatenate([values[first_at], values[second_at]], axis=1)

        visible = (own_key <= row_in_lane) & ((own_key >= boundary) == (row_in_lane >= boundary))
        return dict(
            boundary=boundary,
            first_at=first_at,
            second_at=second_at,
            query=query,
            grad=grad,
            own_k=own_k,
            query_pair=query_pair,
            grad_pair=grad_pair,
            key_pair=key_pair,
            scores=dot(key_pair, query_pair, 1, 1),
            own_scores=jnp.where(visible, dot(own_k, query, 1, 1), HIDDEN),
            dprobs=dot(value_pair, grad_pair, 1, 1),
            own_dprobs=dot(own_v, grad, 1, 1),
        )

    def soften(scores, own_scores, dprobs, own_dprobs, **_):
        top = jnp.maximum(
            jnp.max(scores, axis=0, keepdims=True), jnp.max(own_scores, axis=0, keepdims=True)
        )
        weight = jnp.exp2((scores - top) * EXP2_SCALE)
        own_weight = jnp.exp2((own_scores - top) * EXP2_SCALE)
        inverse = 1.0 / (
            jnp.sum(weight, axis=0, keepdims=True) + jnp.sum(own_weight, axis=0, keepdims=True)
        )
        probs = weight * inverse
        own_probs = own_weight * inverse
        probs_low = probs.astype(BF16)
        own_probs_low = own_probs.astype(BF16)
        delta = jnp.sum(probs_low.astype(F32) * dprobs, axis=0, keepdims=True) + jnp.sum(
            own_probs_low.astype(F32) * own_dprobs, axis=0, keepdims=True
        )
        return dict(
            probs_low=probs_low,
            own_probs_low=own_probs_low,
            dscores=(probs * (dprobs - delta)).astype(BF16),
            own_dscores=(own_probs * (own_dprobs - delta)).astype(BF16),
        )

    def gradients(
        grads, boundary, first_at, second_at, query, grad, own_k, query_pair, grad_pair, key_pair,
        probs_low, own_probs_low, dscores, own_dscores, **_
    ):
        key_part = dot(dscores, query_pair, 1, 0)
        value_part = dot(probs_low, grad_pair, 1, 0)
        key_acc[first_at] += key_part[:, :E]
        key_acc[second_at] += key_part[:, E:]
        value_acc[first_at] += value_part[:, :E]
        value_acc[second_at] += value_part[:, E:]

        query_both = dot(key_pair, dscores, 0, 0)
        query_part = jnp.where(lane_row < boundary, query_both[:E], query_both[E:])
        query_part = (query_part + dot(own_k, own_dscores, 0, 0)) * SCALE
        for h in range(group):
            grads[:, h * E : (h + 1) * E] = query_part[:, h * rows : (h + 1) * rows].T.astype(BF16)
        grads[:, group * E : (group + 1) * E] = (dot(own_dscores, query, 1, 0) * SCALE).astype(BF16)
        grads[:, (group + 1) * E :] = dot(own_probs_low, grad, 1, 0).astype(BF16)

    ahead = products(0)
    for j in range(n):
        now = ahead
        if j + 1 < n:
            ahead = products(j + 1)
        gradients(grads_out[j], **now, **soften(**now))

    for index in range(pieces):
        for j in range(blocks):
            prompt, slot = slots[index][j]
            span = slice(slot * part, (slot + 1) * part)
            target = prefix_out[index]
            target[j, :, :E] = (key_acc[prompt, span, :] * SCALE).astype(target.dtype)
            target[j, :, E:] = value_acc[prompt, span, :].astype(target.dtype)


def attend(packets, notes, kv_in, slots, prompts, resp_bits):
    rows, packet_width = packets[0].shape
    group = (packet_width // E - 2) // 2
    sums_shape = (prompts, PLEN, E)
    out_shape = [jax.ShapeDtypeStruct((rows, (group + 2) * E), BF16)] * len(packets)
    out_shape += [
        jax.ShapeDtypeStruct(x.shape, BF16 if 2 * index >= len(kv_in) else F32)
        for index, x in enumerate(kv_in)
    ]
    operands = [*packets, *notes, *kv_in]
    outs = pl.pallas_call(
        functools.partial(attend_kernel, slots, group, rows, resp_bits),
        out_shape=out_shape,
        in_specs=[VMEM] * len(operands),
        out_specs=[VMEM] * len(out_shape),
        scratch_shapes=[pltpu.VMEM(sums_shape, BF16)] * 2 + [pltpu.VMEM(sums_shape, F32)] * 2,
        compiler_params=params(32),
        cost_estimate=cost(
            20 * len(packets) * group * rows * (PLEN + rows) * E, 1 << 24
        ),
        name="attend_head",
    )(*operands)
    return outs[: len(packets)], outs[len(packets) :]


def total_kernel(keep_ref, *rest):
    parts, (own_ref, other_ref, away_ref) = rest[:-3], rest[-3:]
    for j, out in enumerate((own_ref, other_ref, away_ref.at[0], away_ref.at[1])):
        result = keep_ref[j]
        for part in parts:
            result = result + part[j].astype(F32)
        out[...] = result.astype(BF16)


def total(keep, parts):
    _, rows, width = keep.shape
    return pl.pallas_call(
        total_kernel,
        out_shape=[
            jax.ShapeDtypeStruct(shape, BF16)
            for shape in ((rows, width), (rows, width), (2, rows, width))
        ],
        in_specs=[VMEM] * (1 + len(parts)),
        out_specs=[VMEM] * 3,
        compiler_params=params(16),
        cost_estimate=cost(0, 1 << 25),
        name="total_prefix_grads",
    )(keep, *parts)


def prompt_kernel(n, chunk, *rest):
    shares, (kw_ref, vw_ref, out_ref, key_grad, value_grad, out, sems) = rest[:n], rest[n:]
    heads, _, _ = place()
    for head, share in zip(heads, shares):
        key_grad[:, lanes(head, E)] = share[:, :E]
        value_grad[:, lanes(head, E)] = share[:, E:]
    copies = []
    for index in range(kw_ref.shape[0] // chunk):
        span = slice(index * chunk, (index + 1) * chunk)
        turned = dot(kw_ref[span, :], key_grad[...], 1, 1)
        turned = turned + dot(vw_ref[span, :], value_grad[...], 1, 1)
        out[:, span] = turned.T.astype(BF16)
        copies.append(pltpu.make_async_copy(out.at[:, span], out_ref.at[:, span], sems.at[index]))
        copies[-1].start()
    for copy in copies:
        copy.wait()


def prompt_gradient(shares, key_weight, value_weight, chunk=1024):
    n = len(shares)
    rows = shares[0].shape[0]
    depth, width = key_weight.shape
    return pl.pallas_call(
        functools.partial(prompt_kernel, n, chunk),
        out_shape=jax.ShapeDtypeStruct((rows, depth), BF16),
        in_specs=[VMEM] * (n + 2),
        out_specs=ANY,
        scratch_shapes=[pltpu.VMEM((rows, width), BF16)] * 2
        + [pltpu.VMEM((rows, depth), BF16), pltpu.SemaphoreType.DMA((depth // chunk,))],
        compiler_params=params(32),
        cost_estimate=cost(4 * rows * depth * width, 4 * depth * width + 2 * rows * depth),
        name="prompt_gradient",
    )(*shares, key_weight, value_weight)


def per_device(
    n_prompt,
    n_resp,
    prompt_rows,
    key_weight,
    value_weight,
    queries,
    own_keys,
    own_values,
    out_grad,
    first_length,
    resp_prompt,
):
    devices = n_prompt * n_resp
    every_bit = range(devices.bit_length() - 1)
    line_bits = [bit for bit in GATHER_BITS if bit in every_bit]
    line_bits += [bit for bit in every_bit if bit not in (CORE, X, Y, *line_bits)]
    part = prompt_rows.shape[0]

    def fetch(x, offset):
        pairs = [(i ^ crossed(offset, i >> CORE & 1), i) for i in range(devices)]
        return lax.ppermute(x, ("prompt", "resp"), pairs)

    def give(x, offset):
        pairs = [(i, i ^ crossed(offset, i >> CORE & 1)) for i in range(devices)]
        return lax.ppermute(x, ("prompt", "resp"), pairs)

    other_rows = fetch(prompt_rows, MEMBERS[1])
    note = jnp.concatenate([first_length, resp_prompt.reshape(-1)])
    other_note = fetch(note, MEMBERS[1])
    packed = pack(queries, out_grad, own_keys, own_values)
    packed, other_rows = lax.optimization_barrier((packed, other_rows))
    packets = [packed[0], fetch(packed[1], MEMBERS[1]), fetch(packed[2], MEMBERS[2])]
    keep, send = project(note, other_note, prompt_rows, other_rows, key_weight, value_weight)
    send, packets[2] = lax.optimization_barrier((send, packets[2]))
    notes = [keep, fetch(send, MEMBERS[2])]
    notes[1], late = lax.optimization_barrier((notes[1], packed[3]))
    packets.append(fetch(late, MEMBERS[3]))

    pieces = {0: jnp.concatenate([x[: 2 * part] for x in notes]).reshape(len(MEMBERS), part, -1)}
    for bit in line_bits:
        for offset in list(pieces):
            pieces[offset | 1 << bit] = fetch(pieces[offset], 1 << bit)
    line = list(pieces)
    for offset in line:
        piece = pieces[offset]
        if offset == 0:
            piece, packets[3] = lax.optimization_barrier((piece, packets[3]))
        pieces[offset | 1 << Y] = fetch(piece, 1 << Y)

    filled = [0] * n_prompt
    slots = []
    for offset in pieces:
        places = []
        for member in MEMBERS:
            at = (offset ^ member) // n_resp
            places.append((at, filled[at]))
            filled[at] += 1
        slots.append(tuple(places))
    kv_in = list(pieces.values())
    resp_bits = n_resp.bit_length() - 1
    grads, outs = attend(packets, notes, kv_in, tuple(slots), n_prompt, resp_bits)

    sums = dict(zip(line, outs))
    arrived = {o: [give(x, 1 << Y)] for o, x in zip(line, outs[len(line) :])}
    far = sorted(line, reverse=True)[: len(line) // 2]
    ready, grads = lax.optimization_barrier(([arrived[o][0] for o in far], grads))
    for offset, x in zip(far, ready):
        arrived[offset] = [x]
    for bit in reversed(line_bits):
        first = None
        for offset in sorted(sums, reverse=True):
            if offset & 1 << bit:
                piece = sums.pop(offset)
                for x in arrived.pop(offset):
                    piece = piece + x.astype(F32)
                if offset == 1 << bit and first is not None:
                    piece, arrived[first][-1] = lax.optimization_barrier(
                        (piece, arrived[first][-1])
                    )
                arrived[offset ^ 1 << bit].append(give(piece.astype(BF16), 1 << bit))
                first = offset ^ 1 << bit if first is None else first
    back = [grads[0]] + [give(grads[j], MEMBERS[j]) for j in range(1, len(MEMBERS))]
    (own, other, away), back = lax.optimization_barrier((total(sums[0], arrived[0]), back))
    near = give(away, MEMBERS[2])
    shares = [own, give(other, MEMBERS[1]), near[0], give(near[1], MEMBERS[1])]
    unpacked = unpack(back, queries.shape[1], own_keys.shape[1])
    shares, unpacked = lax.optimization_barrier((shares, unpacked))
    query_grad, key_grad, value_grad = unpacked
    prompt_grad = prompt_gradient(shares, key_weight, value_weight)
    return (query_grad, key_grad, value_grad, prompt_grad)


def solution(mesh):
    both = P(("prompt", "resp"), None)
    return jax.shard_map(
        functools.partial(per_device, mesh.shape["prompt"], mesh.shape["resp"]),
        mesh=mesh,
        in_specs=(both, P(), P(), both, both, both, both, P(("prompt", "resp")), both),
        out_specs=(both, both, both, both),
        check_vma=False,
    )
```

```python
import functools
import math

import jax
import jax.numpy as jnp
from jax import lax
from jax.experimental import pallas as pl
from jax.experimental.pallas import tpu as pltpu
from jax.sharding import PartitionSpec as P

E = 128
PLEN = 512
SCALE = E ** (-0.5)
EXP2_SCALE = SCALE * math.log2(math.e)
HIDDEN = -1e30
BF16 = jnp.bfloat16
F32 = jnp.float32
NOTE_ROWS = 16
CORE, X, Y = 0, 3, 4
GATHER_BITS = (2, 1)
MEMBERS = (0, 1 << CORE, 1 << X, 1 << X | 1 << CORE)

SMEM = pl.BlockSpec(memory_space=pltpu.SMEM)
ANY = pl.BlockSpec(memory_space=pl.ANY)
VMEM = pl.BlockSpec(memory_space=pltpu.VMEM)


def params(mebibytes=40):
    return pltpu.CompilerParams(vmem_limit_bytes=mebibytes * 1024 * 1024)


def cost(flops, bytes_accessed, transcendentals=0):
    return pl.CostEstimate(
        flops=int(flops), bytes_accessed=int(bytes_accessed), transcendentals=int(transcendentals)
    )


def lanes(index, width):
    return pl.ds(pl.multiple_of(index * width, 128), width)


def dot(a, b, a_dim, b_dim):
    return lax.dot_general(a, b, (((a_dim,), (b_dim,)), ((), ())), preferred_element_type=F32)


def crossed(offset, core):
    change = ((offset >> X) ^ (offset >> Y)) & core
    return offset ^ (change << X | change << Y)


def place():
    prompt = lax.axis_index("prompt")
    device = prompt * lax.axis_size("resp") + lax.axis_index("resp")
    core, x, y = ((device >> bit) & 1 for bit in (CORE, X, Y))
    own, other = jnp.where(core == 0, x, 2 + y), jnp.where(core == 0, 2 + y, x)
    return (own, other, own ^ 1, other ^ 1), core, prompt


def project_kernel(steps, x_ref, other_ref, kw_ref, vw_ref, *rest):
    keep_ref, send_ref, rows_in, weights, sums, sems, row_sems = rest
    heads, core, _ = place()
    width = weights.shape[1] // 2
    chunk = weights.shape[0] // steps
    copies = []
    for step in range(steps):
        span = slice(step * chunk, (step + 1) * chunk)
        for index, source in enumerate((kw_ref, vw_ref)):
            copies.append(
                pltpu.make_async_copy(
                    source.at[span, lanes(core, width)],
                    weights.at[span, index * width : (index + 1) * width],
                    sems.at[len(copies)],
                )
            )
    part = x_ref.shape[0]
    row_copies = [
        pltpu.make_async_copy(source, rows_in.at[at : at + part, :], row_sems.at[index])
        for index, (source, at) in enumerate(((x_ref, 0), (other_ref, part)))
    ]
    for copy in row_copies + copies[:8]:
        copy.start()
    for copy in row_copies:
        copy.wait()
    total = None
    for step in range(steps):
        span = slice(step * chunk, (step + 1) * chunk)
        copies[2 * step].wait()
        copies[2 * step + 1].wait()
        for copy in copies[2 * step + 8 : 2 * step + 10]:
            copy.start()
        product = dot(rows_in[:, span], weights[span, :], 1, 0)
        total = product if step == 0 else total + product
    sums[...] = total.astype(BF16)
    for out, head in ((keep_ref, heads[0] & 1), (send_ref, heads[2] & 1)):
        out[:, :E] = sums[:, lanes(head, E)]
        out[:, E:] = sums[:, lanes(head + 2, E)]


def project(prompt_rows, other_rows, key_weight, value_weight, steps=10):
    rows = 2 * prompt_rows.shape[0]
    depth, width = key_weight.shape
    return pl.pallas_call(
        functools.partial(project_kernel, steps),
        out_shape=[jax.ShapeDtypeStruct((rows, 2 * E), BF16)] * 2,
        in_specs=[ANY] * 4,
        out_specs=[VMEM] * 2,
        scratch_shapes=[
            pltpu.VMEM((rows, depth), BF16),
            pltpu.VMEM((depth, width), BF16),
            pltpu.VMEM((rows, width), BF16),
            pltpu.SemaphoreType.DMA((2 * steps,)),
            pltpu.SemaphoreType.DMA((2,)),
        ],
        compiler_params=params(50),
        cost_estimate=cost(2 * rows * depth * width, 2 * depth * width + 2 * rows * depth),
        name="project_prefix",
    )(prompt_rows, other_rows, key_weight, value_weight)


def pack_kernel(length_ref, prompts_ref, q_ref, g_ref, k_ref, v_ref, *outs):
    heads, _, _ = place()
    row = lax.broadcasted_iota(jnp.int32, (q_ref.shape[0], E), 0)
    note = jnp.where(
        row < NOTE_ROWS,
        length_ref[0],
        jnp.where(row < 2 * NOTE_ROWS, prompts_ref[0, 0], prompts_ref[0, 1]),
    )
    note = note.astype(F32).astype(BF16)
    for head, out in zip(heads, outs):
        start = 0
        for source in (q_ref, g_ref, k_ref, v_ref):
            width = source.shape[1] // len(outs)
            out[:, start : start + width] = source[:, lanes(head, width)]
            start += width
        out[:, start:] = note


def pack(first_length, resp_prompt, queries, out_grad, own_keys, own_values):
    rows = queries.shape[0]
    n = len(MEMBERS)
    width = (2 * queries.shape[1] + 2 * own_keys.shape[1]) // n + E
    return pl.pallas_call(
        pack_kernel,
        out_shape=[jax.ShapeDtypeStruct((rows, width), BF16)] * n,
        in_specs=[SMEM] * 2 + [VMEM] * 4,
        out_specs=[VMEM] * n,
        compiler_params=params(16),
        cost_estimate=cost(0, 4 * n * rows * width),
        name="pack_rows",
    )(first_length, resp_prompt, queries, out_grad, own_keys, own_values)


def unpack_kernel(n, *rest):
    packets, targets = rest[:n], rest[n:]
    heads, _, _ = place()
    for head, packet in zip(heads, packets):
        start = 0
        for target in targets:
            width = target.shape[1] // n
            target[:, lanes(head, width)] = packet[:, start : start + width]
            start += width


def unpack(packets, q_width, kv_width):
    n = len(packets)
    rows = packets[0].shape[0]
    return pl.pallas_call(
        functools.partial(unpack_kernel, n),
        out_shape=[
            jax.ShapeDtypeStruct((rows, width), BF16) for width in (q_width, kv_width, kv_width)
        ],
        in_specs=[VMEM] * n,
        out_specs=[VMEM] * 3,
        compiler_params=params(16),
        cost_estimate=cost(0, 4 * rows * (q_width + 2 * kv_width)),
        name="unpack_rows",
    )(*packets)


def attend_kernel(slots, group, rows, resp_bits, *rest):
    rest = list(rest)

    def take(count):
        taken = rest[:count]
        del rest[:count]
        return taken

    def unstack(near, stacks):
        return near + [stack.at[index] for stack in stacks for index in range(stack.shape[0])]

    pieces = len(slots)
    n = len(MEMBERS)
    packets = take(n)
    kv_in = unstack(take(pieces // 2), take(2))
    grads_out = take(n)
    prefix_out = unstack(take(pieces // 2), take(2))
    keys, values, key_acc, value_acc = rest
    blocks, part, _ = kv_in[0].shape
    _, core, prompt_place = place()

    for index in range(pieces):
        for j in range(blocks):
            prompt, slot = slots[index][j]
            span = slice(slot * part, (slot + 1) * part)
            keys[prompt, span, :] = kv_in[index][j, :, :E]
            values[prompt, span, :] = kv_in[index][j, :, E:]
    key_acc[...] = jnp.zeros_like(key_acc)
    value_acc[...] = jnp.zeros_like(value_acc)

    total_rows = group * rows
    row_in_column = lax.broadcasted_iota(jnp.int32, (total_rows, E), 0) & (rows - 1)
    row_in_lane = lax.broadcasted_iota(jnp.int32, (rows, total_rows), 1) & (rows - 1)
    own_key = lax.broadcasted_iota(jnp.int32, (rows, total_rows), 0)
    lane_row = lax.broadcasted_iota(jnp.int32, (E, total_rows), 1) & (rows - 1)

    def products(j):
        packet = packets[j]
        boundary, first_at, second_at = (
            jnp.max(packet[at : at + NOTE_ROWS, -E:].astype(F32)).astype(jnp.int32)
            for at in (0, NOTE_ROWS, 2 * NOTE_ROWS)
        )
        first_at, second_at = (
            crossed((prompt ^ prompt_place) << resp_bits, core) >> resp_bits
            for prompt in (first_at, second_at)
        )
        heads = [packet[:, h * E : (h + 1) * E] for h in range(2 * group + 2)]
        query = jnp.concatenate(heads[:group], axis=0)
        grad = jnp.concatenate(heads[group : 2 * group], axis=0)
        own_k, own_v = heads[2 * group], heads[2 * group + 1]
        in_first = row_in_column < boundary

        def split(x):
            x = x.astype(F32)
            return jnp.concatenate(
                [jnp.where(in_first, x, 0.0), jnp.where(in_first, 0.0, x)], axis=1
            ).astype(BF16)

        query_pair = split(query)
        grad_pair = split(grad)
        key_pair = jnp.concatenate([keys[first_at], keys[second_at]], axis=1)
        value_pair = jnp.concatenate([values[first_at], values[second_at]], axis=1)

        visible = (own_key <= row_in_lane) & ((own_key >= boundary) == (row_in_lane >= boundary))
        return dict(
            boundary=boundary,
            first_at=first_at,
            second_at=second_at,
            query=query,
            grad=grad,
            own_k=own_k,
            query_pair=query_pair,
            grad_pair=grad_pair,
            key_pair=key_pair,
            scores=dot(key_pair, query_pair, 1, 1),
            own_scores=jnp.where(visible, dot(own_k, query, 1, 1), HIDDEN),
            dprobs=dot(value_pair, grad_pair, 1, 1),
            own_dprobs=dot(own_v, grad, 1, 1),
        )

    def soften(scores, own_scores, dprobs, own_dprobs, **_):
        top = jnp.maximum(
            jnp.max(scores, axis=0, keepdims=True), jnp.max(own_scores, axis=0, keepdims=True)
        )
        weight = jnp.exp2((scores - top) * EXP2_SCALE)
        own_weight = jnp.exp2((own_scores - top) * EXP2_SCALE)
        inverse = 1.0 / (
            jnp.sum(weight, axis=0, keepdims=True) + jnp.sum(own_weight, axis=0, keepdims=True)
        )
        probs = weight * inverse
        own_probs = own_weight * inverse
        probs_low = probs.astype(BF16)
        own_probs_low = own_probs.astype(BF16)
        delta = jnp.sum(probs_low.astype(F32) * dprobs, axis=0, keepdims=True) + jnp.sum(
            own_probs_low.astype(F32) * own_dprobs, axis=0, keepdims=True
        )
        return dict(
            probs_low=probs_low,
            own_probs_low=own_probs_low,
            dscores=(probs * (dprobs - delta)).astype(BF16),
            own_dscores=(own_probs * (own_dprobs - delta)).astype(BF16),
        )

    def gradients(
        grads, boundary, first_at, second_at, query, grad, own_k, query_pair, grad_pair, key_pair,
        probs_low, own_probs_low, dscores, own_dscores, **_
    ):
        key_part = dot(dscores, query_pair, 1, 0)
        value_part = dot(probs_low, grad_pair, 1, 0)
        key_acc[first_at] += key_part[:, :E]
        key_acc[second_at] += key_part[:, E:]
        value_acc[first_at] += value_part[:, :E]
        value_acc[second_at] += value_part[:, E:]

        query_both = dot(key_pair, dscores, 0, 0)
        query_part = jnp.where(lane_row < boundary, query_both[:E], query_both[E:])
        query_part = (query_part + dot(own_k, own_dscores, 0, 0)) * SCALE
        for h in range(group):
            grads[:, h * E : (h + 1) * E] = query_part[:, h * rows : (h + 1) * rows].T.astype(BF16)
        grads[:, group * E : (group + 1) * E] = (dot(own_dscores, query, 1, 0) * SCALE).astype(BF16)
        grads[:, (group + 1) * E :] = dot(own_probs_low, grad, 1, 0).astype(BF16)

    ahead = products(0)
    for j in range(n):
        now = ahead
        if j + 1 < n:
            ahead = products(j + 1)
        gradients(grads_out[j], **now, **soften(**now))

    for index in range(pieces):
        for j in range(blocks):
            prompt, slot = slots[index][j]
            span = slice(slot * part, (slot + 1) * part)
            target = prefix_out[index]
            target[j, :, :E] = (key_acc[prompt, span, :] * SCALE).astype(target.dtype)
            target[j, :, E:] = value_acc[prompt, span, :].astype(target.dtype)


def attend(packets, line, stacks, slots, prompts, resp_bits):
    rows, packet_width = packets[0].shape
    group = (packet_width // E - 3) // 2
    sums_shape = (prompts, PLEN, E)
    out_shape = [jax.ShapeDtypeStruct((rows, (group + 2) * E), BF16)] * len(packets)
    out_shape += [jax.ShapeDtypeStruct(x.shape, F32) for x in line]
    out_shape += [jax.ShapeDtypeStruct(x.shape, BF16) for x in stacks]
    operands = [*packets, *line, *stacks]
    outs = pl.pallas_call(
        functools.partial(attend_kernel, slots, group, rows, resp_bits),
        out_shape=out_shape,
        in_specs=[VMEM] * len(operands),
        out_specs=[VMEM] * len(out_shape),
        scratch_shapes=[pltpu.VMEM(sums_shape, BF16)] * 2 + [pltpu.VMEM(sums_shape, F32)] * 2,
        compiler_params=params(32),
        cost_estimate=cost(
            20 * len(packets) * group * rows * (PLEN + rows) * E, 1 << 24
        ),
        name="attend_head",
    )(*operands)
    return outs[: len(packets)], outs[len(packets) : -2], outs[-2:]


def total_kernel(keep_ref, *rest):
    parts, (own_ref, other_ref, away_ref) = rest[:-3], rest[-3:]
    for j, out in enumerate((own_ref, other_ref, away_ref.at[0], away_ref.at[1])):
        result = keep_ref[j]
        for part in parts:
            result = result + part[j].astype(F32)
        out[...] = result.astype(BF16)


def total(keep, parts):
    _, rows, width = keep.shape
    return pl.pallas_call(
        total_kernel,
        out_shape=[
            jax.ShapeDtypeStruct(shape, BF16)
            for shape in ((rows, width), (rows, width), (2, rows, width))
        ],
        in_specs=[VMEM] * (1 + len(parts)),
        out_specs=[VMEM] * 3,
        compiler_params=params(16),
        cost_estimate=cost(0, 1 << 25),
        name="total_prefix_grads",
    )(keep, *parts)


def prompt_kernel(n, chunk, *rest):
    shares, (kw_ref, vw_ref, out_ref, key_grad, value_grad, out, sems) = rest[:n], rest[n:]
    heads, _, _ = place()
    for head, share in zip(heads, shares):
        key_grad[:, lanes(head, E)] = share[:, :E]
        value_grad[:, lanes(head, E)] = share[:, E:]
    copies = []
    for index in range(kw_ref.shape[0] // chunk):
        span = slice(index * chunk, (index + 1) * chunk)
        turned = dot(kw_ref[span, :], key_grad[...], 1, 1)
        turned = turned + dot(vw_ref[span, :], value_grad[...], 1, 1)
        out[:, span] = turned.T.astype(BF16)
        copies.append(pltpu.make_async_copy(out.at[:, span], out_ref.at[:, span], sems.at[index]))
        copies[-1].start()
    for copy in copies:
        copy.wait()


def prompt_gradient(shares, key_weight, value_weight, chunk=1024):
    n = len(shares)
    rows = shares[0].shape[0]
    depth, width = key_weight.shape
    return pl.pallas_call(
        functools.partial(prompt_kernel, n, chunk),
        out_shape=jax.ShapeDtypeStruct((rows, depth), BF16),
        in_specs=[VMEM] * (n + 2),
        out_specs=ANY,
        scratch_shapes=[pltpu.VMEM((rows, width), BF16)] * 2
        + [pltpu.VMEM((rows, depth), BF16), pltpu.SemaphoreType.DMA((depth // chunk,))],
        compiler_params=params(32),
        cost_estimate=cost(4 * rows * depth * width, 4 * depth * width + 2 * rows * depth),
        name="prompt_gradient",
    )(*shares, key_weight, value_weight)


def per_device(
    n_prompt,
    n_resp,
    prompt_rows,
    key_weight,
    value_weight,
    queries,
    own_keys,
    own_values,
    out_grad,
    first_length,
    resp_prompt,
):
    devices = n_prompt * n_resp
    every_bit = range(devices.bit_length() - 1)
    line_bits = [bit for bit in GATHER_BITS if bit in every_bit]
    line_bits += [bit for bit in every_bit if bit not in (CORE, X, Y, *line_bits)]
    part = prompt_rows.shape[0]

    def fetch(x, offset):
        pairs = [(i ^ crossed(offset, i >> CORE & 1), i) for i in range(devices)]
        return lax.ppermute(x, ("prompt", "resp"), pairs)

    def give(x, offset):
        pairs = [(i, i ^ crossed(offset, i >> CORE & 1)) for i in range(devices)]
        return lax.ppermute(x, ("prompt", "resp"), pairs)

    other_rows = fetch(prompt_rows, MEMBERS[1])
    keep, send = project(prompt_rows, other_rows, key_weight, value_weight)
    send, queries = lax.optimization_barrier((send, queries))
    packed = pack(first_length, resp_prompt, queries, out_grad, own_keys, own_values)
    arriving = fetch(send, MEMBERS[2])
    joined = jnp.concatenate([keep, arriving]).reshape(len(MEMBERS), part, -1)
    joined, packed = lax.optimization_barrier((joined, packed))
    packets = [packed[0]] + [fetch(packed[j], MEMBERS[j]) for j in range(1, len(MEMBERS))]

    pieces = {0: joined}
    for bit in line_bits:
        for offset in list(pieces):
            pieces[offset | 1 << bit] = fetch(pieces[offset], 1 << bit)
    offsets = list(pieces)
    half = len(offsets) // 2
    stacks = [
        jnp.stack([pieces[offset] for offset in some])
        for some in (offsets[:half], offsets[half:])
    ]
    stacks[1], packets = lax.optimization_barrier((stacks[1], packets))
    stacks = [fetch(x, 1 << Y) for x in stacks]

    filled = [0] * n_prompt
    slots = []
    for offset in offsets + [offset | 1 << Y for offset in offsets]:
        places = []
        for member in MEMBERS:
            at = (offset ^ member) // n_resp
            places.append((at, filled[at]))
            filled[at] += 1
        slots.append(tuple(places))
    resp_bits = n_resp.bit_length() - 1
    grads, sums, back_stacks = attend(
        packets, list(pieces.values()), stacks, tuple(slots), n_prompt, resp_bits
    )

    sums = dict(zip(offsets, sums))
    far = give(back_stacks[1], 1 << Y)
    near = give(back_stacks[0], 1 << Y)
    far, grads = lax.optimization_barrier((far, grads))
    arrived = {offset: [near[index]] for index, offset in enumerate(offsets[:half])}
    arrived.update({offset: [far[index]] for index, offset in enumerate(offsets[half:])})
    for bit in reversed(line_bits):
        first = None
        for offset in sorted(sums, reverse=True):
            if offset & 1 << bit:
                piece = sums.pop(offset)
                for x in arrived.pop(offset):
                    piece = piece + x.astype(F32)
                if offset == 1 << bit and first is not None:
                    piece, arrived[first][-1] = lax.optimization_barrier(
                        (piece, arrived[first][-1])
                    )
                arrived[offset ^ 1 << bit].append(give(piece.astype(BF16), 1 << bit))
                first = offset ^ 1 << bit if first is None else first
    back = [grads[0]] + [give(grads[j], MEMBERS[j]) for j in range(1, len(MEMBERS))]
    (own, other, away), back = lax.optimization_barrier((total(sums[0], arrived[0]), back))
    near = give(away, MEMBERS[2])
    shares = [own, give(other, MEMBERS[1]), near[0], give(near[1], MEMBERS[1])]
    unpacked = unpack(back, queries.shape[1], own_keys.shape[1])
    shares, unpacked = lax.optimization_barrier((shares, unpacked))
    query_grad, key_grad, value_grad = unpacked
    prompt_grad = prompt_gradient(shares, key_weight, value_weight)
    return (query_grad, key_grad, value_grad, prompt_grad)


def solution(mesh):
    both = P(("prompt", "resp"), None)
    return jax.shard_map(
        functools.partial(per_device, mesh.shape["prompt"], mesh.shape["resp"]),
        mesh=mesh,
        in_specs=(both, P(), P(), both, both, both, both, P(("prompt", "resp")), both),
        out_specs=(both, both, both, both),
        check_vma=False,
    )
```

```python
import functools
import math

import jax
import jax.numpy as jnp
from jax import lax
from jax.experimental import pallas as pl
from jax.experimental.pallas import tpu as pltpu
from jax.sharding import PartitionSpec as P

E = 128
PLEN = 512
SCALE = E ** (-0.5)
EXP2_SCALE = SCALE * math.log2(math.e)
HIDDEN = -1e30
BF16 = jnp.bfloat16
F32 = jnp.float32
NOTE_ROWS = 16
CORE, X, Y = 0, 3, 4
GATHER_BITS = (2, 1)
MEMBERS = (0, 1 << CORE, 1 << X, 1 << X | 1 << CORE)

SMEM = pl.BlockSpec(memory_space=pltpu.SMEM)
ANY = pl.BlockSpec(memory_space=pl.ANY)
VMEM = pl.BlockSpec(memory_space=pltpu.VMEM)


def params(mebibytes=40):
    return pltpu.CompilerParams(vmem_limit_bytes=mebibytes * 1024 * 1024)


def cost(flops, bytes_accessed, transcendentals=0):
    return pl.CostEstimate(
        flops=int(flops), bytes_accessed=int(bytes_accessed), transcendentals=int(transcendentals)
    )


def lanes(index, width):
    return pl.ds(pl.multiple_of(index * width, 128), width)


def dot(a, b, a_dim, b_dim):
    return lax.dot_general(a, b, (((a_dim,), (b_dim,)), ((), ())), preferred_element_type=F32)


def crossed(offset, core):
    change = ((offset >> X) ^ (offset >> Y)) & core
    return offset ^ (change << X | change << Y)


def place():
    prompt = lax.axis_index("prompt")
    device = prompt * lax.axis_size("resp") + lax.axis_index("resp")
    core, x, y = ((device >> bit) & 1 for bit in (CORE, X, Y))
    own, other = jnp.where(core == 0, x, 2 + y), jnp.where(core == 0, 2 + y, x)
    return (own, other, own ^ 1, other ^ 1), core, prompt


def project_kernel(steps, x_ref, other_ref, kw_ref, vw_ref, *rest):
    keep_ref, send_ref, rows_in, weights, sums, sems, row_sems = rest
    heads, core, _ = place()
    width = weights.shape[1] // 2
    chunk = weights.shape[0] // steps
    copies = []
    for step in range(steps):
        span = slice(step * chunk, (step + 1) * chunk)
        for index, source in enumerate((kw_ref, vw_ref)):
            copies.append(
                pltpu.make_async_copy(
                    source.at[span, lanes(core, width)],
                    weights.at[span, index * width : (index + 1) * width],
                    sems.at[len(copies)],
                )
            )
    part = x_ref.shape[0]
    row_copies = [
        pltpu.make_async_copy(source, rows_in.at[at : at + part, :], row_sems.at[index])
        for index, (source, at) in enumerate(((x_ref, 0), (other_ref, part)))
    ]
    for copy in row_copies + copies[:8]:
        copy.start()
    for copy in row_copies:
        copy.wait()
    total = None
    for step in range(steps):
        span = slice(step * chunk, (step + 1) * chunk)
        copies[2 * step].wait()
        copies[2 * step + 1].wait()
        for copy in copies[2 * step + 8 : 2 * step + 10]:
            copy.start()
        product = dot(rows_in[:, span], weights[span, :], 1, 0)
        total = product if step == 0 else total + product
    sums[...] = total.astype(BF16)
    for out, head in ((keep_ref, heads[0] & 1), (send_ref, heads[2] & 1)):
        out[:, :E] = sums[:, lanes(head, E)]
        out[:, E:] = sums[:, lanes(head + 2, E)]


def project(prompt_rows, other_rows, key_weight, value_weight, steps=10):
    rows = 2 * prompt_rows.shape[0]
    depth, width = key_weight.shape
    return pl.pallas_call(
        functools.partial(project_kernel, steps),
        out_shape=[jax.ShapeDtypeStruct((rows, 2 * E), BF16)] * 2,
        in_specs=[ANY] * 4,
        out_specs=[VMEM] * 2,
        scratch_shapes=[
            pltpu.VMEM((rows, depth), BF16),
            pltpu.VMEM((depth, width), BF16),
            pltpu.VMEM((rows, width), BF16),
            pltpu.SemaphoreType.DMA((2 * steps,)),
            pltpu.SemaphoreType.DMA((2,)),
        ],
        compiler_params=params(50),
        cost_estimate=cost(2 * rows * depth * width, 2 * depth * width + 2 * rows * depth),
        name="project_prefix",
    )(prompt_rows, other_rows, key_weight, value_weight)


def pack_kernel(length_ref, prompts_ref, q_ref, g_ref, k_ref, v_ref, *outs):
    heads, _, _ = place()
    row = lax.broadcasted_iota(jnp.int32, (q_ref.shape[0], E), 0)
    note = jnp.where(
        row < NOTE_ROWS,
        length_ref[0],
        jnp.where(row < 2 * NOTE_ROWS, prompts_ref[0, 0], prompts_ref[0, 1]),
    )
    note = note.astype(F32).astype(BF16)
    for head, out in zip(heads, outs):
        start = 0
        for source in (q_ref, g_ref, k_ref, v_ref):
            width = source.shape[1] // len(outs)
            out[:, start : start + width] = source[:, lanes(head, width)]
            start += width
        out[:, start:] = note


def pack(first_length, resp_prompt, queries, out_grad, own_keys, own_values):
    rows = queries.shape[0]
    n = len(MEMBERS)
    width = (2 * queries.shape[1] + 2 * own_keys.shape[1]) // n + E
    return pl.pallas_call(
        pack_kernel,
        out_shape=[jax.ShapeDtypeStruct((rows, width), BF16)] * n,
        in_specs=[SMEM] * 2 + [VMEM] * 4,
        out_specs=[VMEM] * n,
        compiler_params=params(16),
        cost_estimate=cost(0, 4 * n * rows * width),
        name="pack_rows",
    )(first_length, resp_prompt, queries, out_grad, own_keys, own_values)


def unpack_kernel(n, *rest):
    packets, targets = rest[:n], rest[n:]
    heads, _, _ = place()
    for head, packet in zip(heads, packets):
        start = 0
        for target in targets:
            width = target.shape[1] // n
            target[:, lanes(head, width)] = packet[:, start : start + width]
            start += width


def unpack(packets, q_width, kv_width):
    n = len(packets)
    rows = packets[0].shape[0]
    return pl.pallas_call(
        functools.partial(unpack_kernel, n),
        out_shape=[
            jax.ShapeDtypeStruct((rows, width), BF16) for width in (q_width, kv_width, kv_width)
        ],
        in_specs=[VMEM] * n,
        out_specs=[VMEM] * 3,
        compiler_params=params(16),
        cost_estimate=cost(0, 4 * rows * (q_width + 2 * kv_width)),
        name="unpack_rows",
    )(*packets)


def attend_kernel(slots, group, rows, resp_bits, *rest):
    rest = list(rest)

    def take(count):
        taken = rest[:count]
        del rest[:count]
        return taken

    def unstack(near, stacks):
        return near + [stack.at[index] for stack in stacks for index in range(stack.shape[0])]

    pieces = len(slots)
    n = len(MEMBERS)
    packets = take(n)
    kv_in = unstack(take(pieces // 2), take(3))
    grads_out = take(n)
    prefix_out = unstack(take(pieces // 2), take(2))
    keys, values, key_acc, value_acc = rest
    blocks, part, _ = kv_in[0].shape
    _, core, prompt_place = place()

    for index in range(pieces):
        for j in range(blocks):
            prompt, slot = slots[index][j]
            span = slice(slot * part, (slot + 1) * part)
            keys[prompt, span, :] = kv_in[index][j, :, :E]
            values[prompt, span, :] = kv_in[index][j, :, E:]
    key_acc[...] = jnp.zeros_like(key_acc)
    value_acc[...] = jnp.zeros_like(value_acc)

    total_rows = group * rows
    row_in_column = lax.broadcasted_iota(jnp.int32, (total_rows, E), 0) & (rows - 1)
    row_in_lane = lax.broadcasted_iota(jnp.int32, (rows, total_rows), 1) & (rows - 1)
    own_key = lax.broadcasted_iota(jnp.int32, (rows, total_rows), 0)
    lane_row = lax.broadcasted_iota(jnp.int32, (E, total_rows), 1) & (rows - 1)

    def products(j):
        packet = packets[j]
        boundary, first_at, second_at = (
            jnp.max(packet[at : at + NOTE_ROWS, -E:].astype(F32)).astype(jnp.int32)
            for at in (0, NOTE_ROWS, 2 * NOTE_ROWS)
        )
        first_at, second_at = (
            crossed((prompt ^ prompt_place) << resp_bits, core) >> resp_bits
            for prompt in (first_at, second_at)
        )
        heads = [packet[:, h * E : (h + 1) * E] for h in range(2 * group + 2)]
        query = jnp.concatenate(heads[:group], axis=0)
        grad = jnp.concatenate(heads[group : 2 * group], axis=0)
        own_k, own_v = heads[2 * group], heads[2 * group + 1]
        in_first = row_in_column < boundary

        def split(x):
            x = x.astype(F32)
            return jnp.concatenate(
                [jnp.where(in_first, x, 0.0), jnp.where(in_first, 0.0, x)], axis=1
            ).astype(BF16)

        query_pair = split(query)
        grad_pair = split(grad)
        spans = [slice(at, at + E) for at in range(0, PLEN, E)]
        key_pairs, value_pairs = (
            [jnp.concatenate([x[first_at, span], x[second_at, span]], axis=1) for span in spans]
            for x in (keys, values)
        )
        visible = (own_key <= row_in_lane) & ((own_key >= boundary) == (row_in_lane >= boundary))
        scores = [dot(key_pair, query_pair, 1, 1) for key_pair in key_pairs]
        scores.append(jnp.where(visible, dot(own_k, query, 1, 1), HIDDEN))
        return dict(
            boundary=boundary,
            places=[(first_at, second_at, span) for span in spans],
            keys=key_pairs + [own_k],
            values=value_pairs + [own_v],
            queries=[query_pair] * len(spans) + [query],
            grads=[grad_pair] * len(spans) + [grad],
            scores=scores,
        )

    def gradients(out, boundary, places, keys, values, queries, grads, scores):
        top = functools.reduce(jnp.maximum, [jnp.max(x, axis=0, keepdims=True) for x in scores])
        weights, dprobs = [], []
        for x, value, grad in zip(scores, values, grads):
            dprobs.append(dot(value, grad, 1, 1))
            weights.append(jnp.exp2((x - top) * EXP2_SCALE))
        inverse = 1.0 / sum(jnp.sum(x, axis=0, keepdims=True) for x in weights)
        probs = []
        delta = 0.0
        for index, (weight, dprob, grad) in enumerate(zip(weights, dprobs, grads)):
            probs.append(weight * inverse)
            low = probs[-1].astype(BF16)
            delta = delta + jnp.sum(low.astype(F32) * dprob, axis=0, keepdims=True)
            part = dot(low, grad, 1, 0)
            if index < len(places):
                first_at, second_at, span = places[index]
                value_acc[first_at, span] += part[:, :E]
                value_acc[second_at, span] += part[:, E:]
            else:
                out[:, (group + 1) * E :] = part.astype(BF16)
        both = own = None
        for index, (prob, dprob, key, query) in enumerate(zip(probs, dprobs, keys, queries)):
            dscore = (prob * (dprob - delta)).astype(BF16)
            part = dot(dscore, query, 1, 0)
            turned = dot(key, dscore, 0, 0)
            if index < len(places):
                first_at, second_at, span = places[index]
                key_acc[first_at, span] += part[:, :E]
                key_acc[second_at, span] += part[:, E:]
                both = turned if both is None else both + turned
            else:
                out[:, group * E : (group + 1) * E] = (part * SCALE).astype(BF16)
                own = turned
        whole = (jnp.where(lane_row < boundary, both[:E], both[E:]) + own) * SCALE
        for h in range(group):
            out[:, h * E : (h + 1) * E] = whole[:, h * rows : (h + 1) * rows].T.astype(BF16)

    ahead = products(0)
    for j in range(n):
        now = ahead
        if j + 1 < n:
            ahead = products(j + 1)
        gradients(grads_out[j], **now)

    for index in range(pieces):
        for j in range(blocks):
            prompt, slot = slots[index][j]
            span = slice(slot * part, (slot + 1) * part)
            target = prefix_out[index]
            target[j, :, :E] = (key_acc[prompt, span, :] * SCALE).astype(target.dtype)
            target[j, :, E:] = value_acc[prompt, span, :].astype(target.dtype)


def attend(packets, line, stacks, slots, prompts, resp_bits):
    rows, packet_width = packets[0].shape
    group = (packet_width // E - 3) // 2
    sums_shape = (prompts, PLEN, E)
    out_shape = [jax.ShapeDtypeStruct((rows, (group + 2) * E), BF16)] * len(packets)
    out_shape += [jax.ShapeDtypeStruct(x.shape, F32) for x in line]
    half = len(line) // 2
    out_shape += [jax.ShapeDtypeStruct((half, *line[0].shape), BF16)] * 2
    operands = [*packets, *line, *stacks]
    outs = pl.pallas_call(
        functools.partial(attend_kernel, slots, group, rows, resp_bits),
        out_shape=out_shape,
        in_specs=[VMEM] * len(operands),
        out_specs=[VMEM] * len(out_shape),
        scratch_shapes=[pltpu.VMEM(sums_shape, BF16)] * 2 + [pltpu.VMEM(sums_shape, F32)] * 2,
        compiler_params=params(32),
        cost_estimate=cost(
            20 * len(packets) * group * rows * (PLEN + rows) * E, 1 << 24
        ),
        name="attend_head",
    )(*operands)
    return outs[: len(packets)], outs[len(packets) : -2], outs[-2:]


def total_kernel(keep_ref, *rest):
    parts, outs = rest[: -len(MEMBERS)], rest[-len(MEMBERS) :]
    for j, out in enumerate(outs):
        result = keep_ref[j]
        for part in parts:
            result = result + part[j].astype(F32)
        out[...] = result.astype(BF16)


def total(keep, parts):
    return pl.pallas_call(
        total_kernel,
        out_shape=[jax.ShapeDtypeStruct(keep.shape[1:], BF16)] * len(MEMBERS),
        in_specs=[VMEM] * (1 + len(parts)),
        out_specs=[VMEM] * len(MEMBERS),
        compiler_params=params(16),
        cost_estimate=cost(0, 1 << 25),
        name="total_prefix_grads",
    )(keep, *parts)


def prompt_kernel(chunk, members, first, *rest):
    rest = list(rest)
    shares = [rest.pop(0) for _ in members]
    kw_ref, vw_ref = rest.pop(0), rest.pop(0)
    start_ref = None if first else rest.pop(0)
    out_ref, *scratch = rest
    heads, _, _ = place()
    key_grad, value_grad = (
        jnp.concatenate([share[:, at : at + E] for share in shares], axis=1) for at in (0, E)
    )
    copies = []
    for index in range(kw_ref.shape[0] // chunk):
        span = slice(index * chunk, (index + 1) * chunk)
        key_part, value_part = (
            jnp.concatenate([weight[span, lanes(heads[j], E)] for j in members], axis=1)
            for weight in (kw_ref, vw_ref)
        )
        turned = dot(key_part, key_grad, 1, 1) + dot(value_part, value_grad, 1, 1)
        if first:
            out_ref[span, :] = turned
            continue
        out, sems = scratch
        out[:, span] = (turned + start_ref[span, :]).T.astype(BF16)
        copies.append(pltpu.make_async_copy(out.at[:, span], out_ref.at[:, span], sems.at[index]))
        copies[-1].start()
    for copy in copies:
        copy.wait()


def prompt_gradient(members, shares, key_weight, value_weight, start=None, chunk=1024):
    first = start is None
    rows = shares[0].shape[0]
    depth, width = key_weight.shape
    operands = [*shares, key_weight, value_weight] + ([] if first else [start])
    out = jax.ShapeDtypeStruct((depth, rows), F32)
    if not first:
        out = jax.ShapeDtypeStruct((rows, depth), BF16)
    return pl.pallas_call(
        functools.partial(prompt_kernel, chunk, members, first),
        out_shape=out,
        in_specs=[VMEM] * len(operands),
        out_specs=VMEM if first else ANY,
        scratch_shapes=[]
        if first
        else [pltpu.VMEM((rows, depth), BF16), pltpu.SemaphoreType.DMA((depth // chunk,))],
        compiler_params=params(24),
        cost_estimate=cost(2 * rows * depth * width, 2 * depth * width + 2 * rows * depth),
        name="prompt_gradient",
    )(*operands)


def per_device(
    n_prompt,
    n_resp,
    prompt_rows,
    key_weight,
    value_weight,
    queries,
    own_keys,
    own_values,
    out_grad,
    first_length,
    resp_prompt,
):
    devices = n_prompt * n_resp
    every_bit = range(devices.bit_length() - 1)
    line_bits = [bit for bit in GATHER_BITS if bit in every_bit]
    line_bits += [bit for bit in every_bit if bit not in (CORE, X, Y, *line_bits)]
    part = prompt_rows.shape[0]

    def fetch(x, offset):
        pairs = [(i ^ crossed(offset, i >> CORE & 1), i) for i in range(devices)]
        return lax.ppermute(x, ("prompt", "resp"), pairs)

    def give(x, offset):
        pairs = [(i, i ^ crossed(offset, i >> CORE & 1)) for i in range(devices)]
        return lax.ppermute(x, ("prompt", "resp"), pairs)

    other_rows = fetch(prompt_rows, MEMBERS[1])
    keep, send = project(prompt_rows, other_rows, key_weight, value_weight)
    send, queries = lax.optimization_barrier((send, queries))
    packed = pack(first_length, resp_prompt, queries, out_grad, own_keys, own_values)
    arriving = fetch(send, MEMBERS[2])
    joined = jnp.concatenate([keep, arriving]).reshape(len(MEMBERS), part, -1)
    joined, packed = lax.optimization_barrier((joined, packed))
    packets = [packed[0]] + [fetch(packed[j], MEMBERS[j]) for j in range(1, len(MEMBERS))]

    pieces = {0: joined}
    for bit in line_bits:
        for offset in list(pieces):
            pieces[offset | 1 << bit] = fetch(pieces[offset], 1 << bit)
    offsets = list(pieces)
    long = 1 << line_bits[0]
    some = [offset for offset in offsets if not offset & long]
    many = [offset for offset in offsets if offset & long]
    groups = [some, many[:-1], many[-1:]]
    stacks = [jnp.stack([pieces[offset] for offset in group]) for group in groups]
    stacks[2], packets = lax.optimization_barrier((stacks[2], packets))
    stacks = [fetch(x, 1 << Y) for x in stacks]

    filled = [0] * n_prompt
    slots = []
    for offset in offsets + [offset | 1 << Y for group in groups for offset in group]:
        places = []
        for member in MEMBERS:
            at = (offset ^ member) // n_resp
            places.append((at, filled[at]))
            filled[at] += 1
        slots.append(tuple(places))
    resp_bits = n_resp.bit_length() - 1
    grads, sums, back_stacks = attend(
        packets, list(pieces.values()), stacks, tuple(slots), n_prompt, resp_bits
    )

    sums = dict(zip(offsets, sums))
    far = give(back_stacks[1], 1 << Y)
    near = give(back_stacks[0], 1 << Y)
    far, grads = lax.optimization_barrier((far, grads))
    arrived = {
        offset: [stack[index]]
        for group, stack in ((some, near), (many, far))
        for index, offset in enumerate(group)
    }
    for bit in reversed(line_bits):
        first = None
        for offset in sorted(sums, reverse=True):
            if offset & 1 << bit:
                piece = sums.pop(offset)
                for x in arrived.pop(offset):
                    piece = piece + x.astype(F32)
                if offset == 1 << bit and first is not None:
                    piece, arrived[first][-1] = lax.optimization_barrier(
                        (piece, arrived[first][-1])
                    )
                arrived[offset ^ 1 << bit].append(give(piece.astype(BF16), 1 << bit))
                first = offset ^ 1 << bit if first is None else first
    back = [grads[0]] + [give(grads[j], MEMBERS[j]) for j in range(1, len(MEMBERS))]
    blocks, back = lax.optimization_barrier((total(sums[0], arrived[0]), back))
    shares = [blocks[0]] + [give(blocks[j], MEMBERS[j]) for j in range(1, len(MEMBERS))]
    start = prompt_gradient((0, 1), shares[:2], key_weight, value_weight)
    unpacked = unpack(back, queries.shape[1], own_keys.shape[1])
    start, unpacked = lax.optimization_barrier((start, unpacked))
    query_grad, key_grad, value_grad = unpacked
    prompt_grad = prompt_gradient((2, 3), shares[2:], key_weight, value_weight, start)
    return (query_grad, key_grad, value_grad, prompt_grad)


def solution(mesh):
    both = P(("prompt", "resp"), None)
    return jax.shard_map(
        functools.partial(per_device, mesh.shape["prompt"], mesh.shape["resp"]),
        mesh=mesh,
        in_specs=(both, P(), P(), both, both, both, both, P(("prompt", "resp")), both),
        out_specs=(both, both, both, both),
        check_vma=False,
    )
```

```python
import functools
import math

import jax
import jax.numpy as jnp
from jax import lax
from jax.experimental import pallas as pl
from jax.experimental.pallas import tpu as pltpu
from jax.sharding import PartitionSpec as P

E = 128
PLEN = 512
SCALE = E ** (-0.5)
EXP2_SCALE = SCALE * math.log2(math.e)
HIDDEN = -1e30
BF16 = jnp.bfloat16
F32 = jnp.float32
NOTE_ROWS = 16
CORE, X, Y = 0, 3, 4
GATHER_BITS = (2, 1)
MEMBERS = (0, 1 << CORE, 1 << X, 1 << X | 1 << CORE)

SMEM = pl.BlockSpec(memory_space=pltpu.SMEM)
ANY = pl.BlockSpec(memory_space=pl.ANY)
VMEM = pl.BlockSpec(memory_space=pltpu.VMEM)


def params(mebibytes=40):
    return pltpu.CompilerParams(vmem_limit_bytes=mebibytes * 1024 * 1024)


def cost(flops, bytes_accessed, transcendentals=0):
    return pl.CostEstimate(
        flops=int(flops), bytes_accessed=int(bytes_accessed), transcendentals=int(transcendentals)
    )


def lanes(index, width):
    return pl.ds(pl.multiple_of(index * width, 128), width)


def dot(a, b, a_dim, b_dim):
    return lax.dot_general(a, b, (((a_dim,), (b_dim,)), ((), ())), preferred_element_type=F32)


def crossed(offset, core):
    change = ((offset >> X) ^ (offset >> Y)) & core
    return offset ^ (change << X | change << Y)


def place():
    prompt = lax.axis_index("prompt")
    device = prompt * lax.axis_size("resp") + lax.axis_index("resp")
    core, x, y = ((device >> bit) & 1 for bit in (CORE, X, Y))
    own, other = jnp.where(core == 0, x, 2 + y), jnp.where(core == 0, 2 + y, x)
    return (own, other, own ^ 1, other ^ 1), core, prompt


def project_kernel(steps, x_ref, other_ref, kw_ref, vw_ref, *rest):
    keep_ref, send_ref, rows_in, weights, sums, sems, row_sems = rest
    heads, core, _ = place()
    width = weights.shape[1] // 2
    chunk = weights.shape[0] // steps
    copies = []
    for step in range(steps):
        span = slice(step * chunk, (step + 1) * chunk)
        for index, source in enumerate((kw_ref, vw_ref)):
            copies.append(
                pltpu.make_async_copy(
                    source.at[span, lanes(core, width)],
                    weights.at[span, index * width : (index + 1) * width],
                    sems.at[len(copies)],
                )
            )
    part = x_ref.shape[0]
    row_copies = [
        pltpu.make_async_copy(source, rows_in.at[at : at + part, :], row_sems.at[index])
        for index, (source, at) in enumerate(((x_ref, 0), (other_ref, part)))
    ]
    for copy in row_copies + copies[:8]:
        copy.start()
    for copy in row_copies:
        copy.wait()
    total = None
    for step in range(steps):
        span = slice(step * chunk, (step + 1) * chunk)
        copies[2 * step].wait()
        copies[2 * step + 1].wait()
        for copy in copies[2 * step + 8 : 2 * step + 10]:
            copy.start()
        product = dot(rows_in[:, span], weights[span, :], 1, 0)
        total = product if step == 0 else total + product
    sums[...] = total.astype(BF16)
    for out, head in ((keep_ref, heads[0] & 1), (send_ref, heads[2] & 1)):
        out[:, :E] = sums[:, lanes(head, E)]
        out[:, E:] = sums[:, lanes(head + 2, E)]


def project(prompt_rows, other_rows, key_weight, value_weight, steps=10):
    rows = 2 * prompt_rows.shape[0]
    depth, width = key_weight.shape
    return pl.pallas_call(
        functools.partial(project_kernel, steps),
        out_shape=[jax.ShapeDtypeStruct((rows, 2 * E), BF16)] * 2,
        in_specs=[ANY] * 4,
        out_specs=[VMEM] * 2,
        scratch_shapes=[
            pltpu.VMEM((rows, depth), BF16),
            pltpu.VMEM((depth, width), BF16),
            pltpu.VMEM((rows, width), BF16),
            pltpu.SemaphoreType.DMA((2 * steps,)),
            pltpu.SemaphoreType.DMA((2,)),
        ],
        compiler_params=params(50),
        cost_estimate=cost(2 * rows * depth * width, 2 * depth * width + 2 * rows * depth),
        name="project_prefix",
    )(prompt_rows, other_rows, key_weight, value_weight)


def pack_kernel(length_ref, prompts_ref, q_ref, g_ref, k_ref, v_ref, *outs):
    heads, _, _ = place()
    row = lax.broadcasted_iota(jnp.int32, (q_ref.shape[0], E), 0)
    note = jnp.where(
        row < NOTE_ROWS,
        length_ref[0],
        jnp.where(row < 2 * NOTE_ROWS, prompts_ref[0, 0], prompts_ref[0, 1]),
    )
    note = note.astype(F32).astype(BF16)
    for head, out in zip(heads, outs):
        start = 0
        for source in (q_ref, g_ref, k_ref, v_ref):
            width = source.shape[1] // len(outs)
            out[:, start : start + width] = source[:, lanes(head, width)]
            start += width
        out[:, start:] = note


def pack(first_length, resp_prompt, queries, out_grad, own_keys, own_values):
    rows = queries.shape[0]
    n = len(MEMBERS)
    width = (2 * queries.shape[1] + 2 * own_keys.shape[1]) // n + E
    return pl.pallas_call(
        pack_kernel,
        out_shape=[jax.ShapeDtypeStruct((rows, width), BF16)] * n,
        in_specs=[SMEM] * 2 + [VMEM] * 4,
        out_specs=[VMEM] * n,
        compiler_params=params(16),
        cost_estimate=cost(0, 4 * n * rows * width),
        name="pack_rows",
    )(first_length, resp_prompt, queries, out_grad, own_keys, own_values)


def unpack_kernel(n, *rest):
    packets, targets = rest[:n], rest[n:]
    heads, _, _ = place()
    for head, packet in zip(heads, packets):
        start = 0
        for target in targets:
            width = target.shape[1] // n
            target[:, lanes(head, width)] = packet[:, start : start + width]
            start += width


def unpack(packets, q_width, kv_width):
    n = len(packets)
    rows = packets[0].shape[0]
    return pl.pallas_call(
        functools.partial(unpack_kernel, n),
        out_shape=[
            jax.ShapeDtypeStruct((rows, width), BF16) for width in (q_width, kv_width, kv_width)
        ],
        in_specs=[VMEM] * n,
        out_specs=[VMEM] * 3,
        compiler_params=params(16),
        cost_estimate=cost(0, 4 * rows * (q_width + 2 * kv_width)),
        name="unpack_rows",
    )(*packets)


def attend_kernel(slots, group, rows, resp_bits, *rest):
    rest = list(rest)

    def take(count):
        taken = rest[:count]
        del rest[:count]
        return taken

    def unstack(near, stacks):
        return near + [stack.at[index] for stack in stacks for index in range(stack.shape[0])]

    pieces = len(slots)
    n = len(MEMBERS)
    packets = take(n)
    kv_in = unstack(take(pieces // 2), take(2))
    grads_out = take(n)
    prefix_out = unstack(take(pieces // 2), take(3))
    keys, values, key_acc, value_acc = rest
    blocks, part, _ = kv_in[0].shape
    _, core, prompt_place = place()

    for index in range(pieces):
        for j in range(blocks):
            prompt, slot = slots[index][j]
            span = slice(slot * part, (slot + 1) * part)
            keys[prompt, span, :] = kv_in[index][j, :, :E]
            values[prompt, span, :] = kv_in[index][j, :, E:]
    key_acc[...] = jnp.zeros_like(key_acc)
    value_acc[...] = jnp.zeros_like(value_acc)

    total_rows = group * rows
    row_in_column = lax.broadcasted_iota(jnp.int32, (total_rows, E), 0) & (rows - 1)
    row_in_lane = lax.broadcasted_iota(jnp.int32, (rows, total_rows), 1) & (rows - 1)
    own_key = lax.broadcasted_iota(jnp.int32, (rows, total_rows), 0)
    lane_row = lax.broadcasted_iota(jnp.int32, (E, total_rows), 1) & (rows - 1)

    def products(j):
        packet = packets[j]
        boundary, first_at, second_at = (
            jnp.max(packet[at : at + NOTE_ROWS, -E:].astype(F32)).astype(jnp.int32)
            for at in (0, NOTE_ROWS, 2 * NOTE_ROWS)
        )
        first_at, second_at = (
            crossed((prompt ^ prompt_place) << resp_bits, core) >> resp_bits
            for prompt in (first_at, second_at)
        )
        heads = [packet[:, h * E : (h + 1) * E] for h in range(2 * group + 2)]
        query = jnp.concatenate(heads[:group], axis=0)
        grad = jnp.concatenate(heads[group : 2 * group], axis=0)
        own_k, own_v = heads[2 * group], heads[2 * group + 1]
        in_first = row_in_column < boundary

        def split(x):
            x = x.astype(F32)
            return jnp.concatenate(
                [jnp.where(in_first, x, 0.0), jnp.where(in_first, 0.0, x)], axis=1
            ).astype(BF16)

        query_pair = split(query)
        grad_pair = split(grad)
        key_pair = jnp.concatenate([keys[first_at], keys[second_at]], axis=1)
        value_pair = jnp.concatenate([values[first_at], values[second_at]], axis=1)

        visible = (own_key <= row_in_lane) & ((own_key >= boundary) == (row_in_lane >= boundary))
        return dict(
            boundary=boundary,
            first_at=first_at,
            second_at=second_at,
            query=query,
            grad=grad,
            own_k=own_k,
            query_pair=query_pair,
            grad_pair=grad_pair,
            key_pair=key_pair,
            scores=dot(key_pair, query_pair, 1, 1),
            own_scores=jnp.where(visible, dot(own_k, query, 1, 1), HIDDEN),
            dprobs=dot(value_pair, grad_pair, 1, 1),
            own_dprobs=dot(own_v, grad, 1, 1),
        )

    def soften(scores, own_scores, dprobs, own_dprobs, **_):
        top = jnp.maximum(
            jnp.max(scores, axis=0, keepdims=True), jnp.max(own_scores, axis=0, keepdims=True)
        )
        weight = jnp.exp2((scores - top) * EXP2_SCALE)
        own_weight = jnp.exp2((own_scores - top) * EXP2_SCALE)
        inverse = 1.0 / (
            jnp.sum(weight, axis=0, keepdims=True) + jnp.sum(own_weight, axis=0, keepdims=True)
        )
        probs = weight * inverse
        own_probs = own_weight * inverse
        probs_low = probs.astype(BF16)
        own_probs_low = own_probs.astype(BF16)
        delta = jnp.sum(probs_low.astype(F32) * dprobs, axis=0, keepdims=True) + jnp.sum(
            own_probs_low.astype(F32) * own_dprobs, axis=0, keepdims=True
        )
        return dict(
            probs_low=probs_low,
            own_probs_low=own_probs_low,
            dscores=(probs * (dprobs - delta)).astype(BF16),
            own_dscores=(own_probs * (own_dprobs - delta)).astype(BF16),
        )

    def gradients(
        grads, boundary, first_at, second_at, query, grad, own_k, query_pair, grad_pair, key_pair,
        probs_low, own_probs_low, dscores, own_dscores, **_
    ):
        key_part = dot(dscores, query_pair, 1, 0)
        value_part = dot(probs_low, grad_pair, 1, 0)
        key_acc[first_at] += key_part[:, :E]
        key_acc[second_at] += key_part[:, E:]
        value_acc[first_at] += value_part[:, :E]
        value_acc[second_at] += value_part[:, E:]

        query_both = dot(key_pair, dscores, 0, 0)
        query_part = jnp.where(lane_row < boundary, query_both[:E], query_both[E:])
        query_part = (query_part + dot(own_k, own_dscores, 0, 0)) * SCALE
        for h in range(group):
            grads[:, h * E : (h + 1) * E] = query_part[:, h * rows : (h + 1) * rows].T.astype(BF16)
        grads[:, group * E : (group + 1) * E] = (dot(own_dscores, query, 1, 0) * SCALE).astype(BF16)
        grads[:, (group + 1) * E :] = dot(own_probs_low, grad, 1, 0).astype(BF16)

    ahead = products(0)
    for j in range(n):
        now = ahead
        if j + 1 < n:
            ahead = products(j + 1)
        gradients(grads_out[j], **now, **soften(**now))

    for index in range(pieces):
        for j in range(blocks):
            prompt, slot = slots[index][j]
            span = slice(slot * part, (slot + 1) * part)
            target = prefix_out[index]
            target[j, :, :E] = (key_acc[prompt, span, :] * SCALE).astype(target.dtype)
            target[j, :, E:] = value_acc[prompt, span, :].astype(target.dtype)


def attend(packets, line, stacks, slots, prompts, resp_bits):
    rows, packet_width = packets[0].shape
    group = (packet_width // E - 3) // 2
    sums_shape = (prompts, PLEN, E)
    out_shape = [jax.ShapeDtypeStruct((rows, (group + 2) * E), BF16)] * len(packets)
    out_shape += [jax.ShapeDtypeStruct(x.shape, F32) for x in line]
    out_shape += [
        jax.ShapeDtypeStruct((count, *line[0].shape), BF16) for count in (1, len(line) - 2, 1)
    ]
    operands = [*packets, *line, *stacks]
    outs = pl.pallas_call(
        functools.partial(attend_kernel, slots, group, rows, resp_bits),
        out_shape=out_shape,
        in_specs=[VMEM] * len(operands),
        out_specs=[VMEM] * len(out_shape),
        scratch_shapes=[pltpu.VMEM(sums_shape, BF16)] * 2 + [pltpu.VMEM(sums_shape, F32)] * 2,
        compiler_params=params(32),
        cost_estimate=cost(
            20 * len(packets) * group * rows * (PLEN + rows) * E, 1 << 24
        ),
        name="attend_head",
    )(*operands)
    return outs[: len(packets)], outs[len(packets) : -3], outs[-3:]


def total_kernel(keep_ref, *rest):
    parts, outs = rest[: -len(MEMBERS)], rest[-len(MEMBERS) :]
    for j, out in enumerate(outs):
        result = keep_ref[j]
        for part in parts:
            result = result + part[j].astype(F32)
        out[...] = result.astype(BF16)


def total(keep, parts):
    return pl.pallas_call(
        total_kernel,
        out_shape=[jax.ShapeDtypeStruct(keep.shape[1:], BF16)] * len(MEMBERS),
        in_specs=[VMEM] * (1 + len(parts)),
        out_specs=[VMEM] * len(MEMBERS),
        compiler_params=params(16),
        cost_estimate=cost(0, 1 << 25),
        name="total_prefix_grads",
    )(keep, *parts)


def prompt_kernel(chunk, members, first, *rest):
    rest = list(rest)
    shares = [rest.pop(0) for _ in members]
    kw_ref, vw_ref = rest.pop(0), rest.pop(0)
    start_ref = None if first else rest.pop(0)
    out_ref, *scratch = rest
    heads, _, _ = place()
    key_grad, value_grad = (
        jnp.concatenate([share[:, at : at + E] for share in shares], axis=1) for at in (0, E)
    )
    copies = []
    for index in range(kw_ref.shape[0] // chunk):
        span = slice(index * chunk, (index + 1) * chunk)
        key_part, value_part = (
            jnp.concatenate([weight[span, lanes(heads[j], E)] for j in members], axis=1)
            for weight in (kw_ref, vw_ref)
        )
        turned = dot(key_part, key_grad, 1, 1) + dot(value_part, value_grad, 1, 1)
        if first:
            out_ref[span, :] = turned
            continue
        out, sems = scratch
        out[:, span] = (turned + start_ref[span, :]).T.astype(BF16)
        copies.append(pltpu.make_async_copy(out.at[:, span], out_ref.at[:, span], sems.at[index]))
        copies[-1].start()
    for copy in copies:
        copy.wait()


def prompt_gradient(members, shares, key_weight, value_weight, start=None, chunk=1024):
    first = start is None
    rows = shares[0].shape[0]
    depth, width = key_weight.shape
    operands = [*shares, key_weight, value_weight] + ([] if first else [start])
    out = jax.ShapeDtypeStruct((depth, rows), F32)
    if not first:
        out = jax.ShapeDtypeStruct((rows, depth), BF16)
    return pl.pallas_call(
        functools.partial(prompt_kernel, chunk, members, first),
        out_shape=out,
        in_specs=[VMEM] * len(operands),
        out_specs=VMEM if first else ANY,
        scratch_shapes=[]
        if first
        else [pltpu.VMEM((rows, depth), BF16), pltpu.SemaphoreType.DMA((depth // chunk,))],
        compiler_params=params(24),
        cost_estimate=cost(2 * rows * depth * width, 2 * depth * width + 2 * rows * depth),
        name="prompt_gradient",
    )(*operands)


def per_device(
    n_prompt,
    n_resp,
    prompt_rows,
    key_weight,
    value_weight,
    queries,
    own_keys,
    own_values,
    out_grad,
    first_length,
    resp_prompt,
):
    devices = n_prompt * n_resp
    every_bit = range(devices.bit_length() - 1)
    line_bits = [bit for bit in GATHER_BITS if bit in every_bit]
    line_bits += [bit for bit in every_bit if bit not in (CORE, X, Y, *line_bits)]
    part = prompt_rows.shape[0]

    def fetch(x, offset):
        pairs = [(i ^ crossed(offset, i >> CORE & 1), i) for i in range(devices)]
        return lax.ppermute(x, ("prompt", "resp"), pairs)

    def give(x, offset):
        pairs = [(i, i ^ crossed(offset, i >> CORE & 1)) for i in range(devices)]
        return lax.ppermute(x, ("prompt", "resp"), pairs)

    other_rows = fetch(prompt_rows, MEMBERS[1])
    keep, send = project(prompt_rows, other_rows, key_weight, value_weight)
    send, queries = lax.optimization_barrier((send, queries))
    packed = pack(first_length, resp_prompt, queries, out_grad, own_keys, own_values)
    arriving = fetch(send, MEMBERS[2])
    joined = jnp.concatenate([keep, arriving]).reshape(len(MEMBERS), part, -1)
    joined, packed = lax.optimization_barrier((joined, packed))
    packets = [packed[0]] + [fetch(packed[j], MEMBERS[j]) for j in range(1, len(MEMBERS))]

    pieces = {0: joined}
    for bit in line_bits:
        for offset in list(pieces):
            pieces[offset | 1 << bit] = fetch(pieces[offset], 1 << bit)
    offsets = list(pieces)
    stacks = [
        jnp.stack([pieces[offset] for offset in some]) for some in (offsets[:-1], offsets[-1:])
    ]
    stacks[1], packets = lax.optimization_barrier((stacks[1], packets))
    stacks = [fetch(x, 1 << Y) for x in stacks]

    filled = [0] * n_prompt
    slots = []
    for offset in offsets + [offset | 1 << Y for offset in offsets]:
        places = []
        for member in MEMBERS:
            at = (offset ^ member) // n_resp
            places.append((at, filled[at]))
            filled[at] += 1
        slots.append(tuple(places))
    resp_bits = n_resp.bit_length() - 1
    grads, sums, back_stacks = attend(
        packets, list(pieces.values()), stacks, tuple(slots), n_prompt, resp_bits
    )

    sums = dict(zip(offsets, sums))
    far = give(back_stacks[2], 1 << Y)
    middle = give(back_stacks[1], 1 << Y)
    near = give(back_stacks[0], 1 << Y)
    far, grads = lax.optimization_barrier((far, grads))
    back = [grads[0]] + [give(grads[j], MEMBERS[j]) for j in range(1, len(MEMBERS))]
    arrived = {offset: [middle[index]] for index, offset in enumerate(offsets[1:-1])}
    arrived.update({offsets[0]: [near[0]], offsets[-1]: [far[0]]})
    for bit in reversed(line_bits):
        for offset in sorted(sums, reverse=True):
            if offset & 1 << bit:
                piece = sums.pop(offset)
                for x in arrived.pop(offset):
                    piece = piece + x.astype(F32)
                if offset == 1 << bit and bit != line_bits[0]:
                    piece, back[2] = lax.optimization_barrier((piece, back[2]))
                arrived[offset ^ 1 << bit].append(give(piece.astype(BF16), 1 << bit))
    unpacked = unpack(back, queries.shape[1], own_keys.shape[1])
    arrived[0], unpacked = lax.optimization_barrier((arrived[0], unpacked))
    query_grad, key_grad, value_grad = unpacked
    blocks = total(sums[0], arrived[0])
    shares = [blocks[0]] + [give(blocks[j], MEMBERS[j]) for j in range(1, len(MEMBERS))]
    start = prompt_gradient((0, 1), shares[:2], key_weight, value_weight)
    prompt_grad = prompt_gradient((2, 3), shares[2:], key_weight, value_weight, start)
    return (query_grad, key_grad, value_grad, prompt_grad)


def solution(mesh):
    both = P(("prompt", "resp"), None)
    return jax.shard_map(
        functools.partial(per_device, mesh.shape["prompt"], mesh.shape["resp"]),
        mesh=mesh,
        in_specs=(both, P(), P(), both, both, both, both, P(("prompt", "resp")), both),
        out_specs=(both, both, both, both),
        check_vma=False,
    )
```

```python
import functools
import math

import jax
import jax.numpy as jnp
from jax import lax
from jax.experimental import pallas as pl
from jax.experimental.pallas import tpu as pltpu
from jax.sharding import PartitionSpec as P

E = 128
PLEN = 512
SCALE = E ** (-0.5)
EXP2_SCALE = SCALE * math.log2(math.e)
HIDDEN = -1e30
BF16 = jnp.bfloat16
F32 = jnp.float32
NOTE_ROWS = 16
CORE, X, Y = 0, 3, 4
GATHER_BITS = (2, 1)
MEMBERS = (0, 1 << CORE, 1 << X, 1 << X | 1 << CORE)

SMEM = pl.BlockSpec(memory_space=pltpu.SMEM)
ANY = pl.BlockSpec(memory_space=pl.ANY)
VMEM = pl.BlockSpec(memory_space=pltpu.VMEM)


def params(mebibytes=40):
    return pltpu.CompilerParams(vmem_limit_bytes=mebibytes * 1024 * 1024)


def cost(flops, bytes_accessed, transcendentals=0):
    return pl.CostEstimate(
        flops=int(flops), bytes_accessed=int(bytes_accessed), transcendentals=int(transcendentals)
    )


def lanes(index, width):
    return pl.ds(pl.multiple_of(index * width, 128), width)


def dot(a, b, a_dim, b_dim):
    return lax.dot_general(a, b, (((a_dim,), (b_dim,)), ((), ())), preferred_element_type=F32)


def crossed(offset, core):
    change = ((offset >> X) ^ (offset >> Y)) & core
    return offset ^ (change << X | change << Y)


def place():
    prompt = lax.axis_index("prompt")
    device = prompt * lax.axis_size("resp") + lax.axis_index("resp")
    core, x, y = ((device >> bit) & 1 for bit in (CORE, X, Y))
    own, other = jnp.where(core == 0, x, 2 + y), jnp.where(core == 0, 2 + y, x)
    return (own, other, own ^ 1, other ^ 1), core, prompt


def project_kernel(steps, x_ref, kw_ref, vw_ref, out_ref, weights, sems):
    _, core, _ = place()
    width = weights.shape[1] // 2
    chunk = weights.shape[0] // steps
    copies = []
    for step in range(steps):
        span = slice(step * chunk, (step + 1) * chunk)
        for index, source in enumerate((kw_ref, vw_ref)):
            copies.append(
                pltpu.make_async_copy(
                    source.at[span, lanes(core, width)],
                    weights.at[span, index * width : (index + 1) * width],
                    sems.at[len(copies)],
                )
            )
    for copy in copies[:8]:
        copy.start()
    total = None
    for step in range(steps):
        span = slice(step * chunk, (step + 1) * chunk)
        copies[2 * step].wait()
        copies[2 * step + 1].wait()
        for copy in copies[2 * step + 8 : 2 * step + 10]:
            copy.start()
        product = dot(x_ref[:, span], weights[span, :], 1, 0)
        total = product if step == 0 else total + product
    out_ref[...] = total.astype(BF16)


def project(prompt_rows, key_weight, value_weight, steps=10):
    rows = prompt_rows.shape[0]
    depth, width = key_weight.shape
    return pl.pallas_call(
        functools.partial(project_kernel, steps),
        out_shape=[
            jax.ShapeDtypeStruct((rows, width), BF16),
            jax.ShapeDtypeStruct((depth, width), BF16),
        ],
        in_specs=[VMEM, ANY, ANY],
        out_specs=[VMEM] * 2,
        scratch_shapes=[pltpu.SemaphoreType.DMA((2 * steps,))],
        compiler_params=params(44),
        cost_estimate=cost(2 * rows * depth * width, 2 * depth * width + 2 * rows * depth),
        name="project_own",
    )(prompt_rows, key_weight, value_weight)


def project_other_kernel(x_ref, weights, first_ref, keep_ref, send_ref, second_ref):
    heads, _, _ = place()
    second_ref[...] = dot(x_ref[...], weights[...], 1, 0).astype(BF16)
    part = x_ref.shape[0]
    for out, head in ((keep_ref, heads[0] & 1), (send_ref, heads[2] & 1)):
        for index, source in enumerate((first_ref, second_ref)):
            span = slice(index * part, (index + 1) * part)
            out[span, :E] = source[:, lanes(head, E)]
            out[span, E:] = source[:, lanes(head + 2, E)]


def project_other(other_rows, weights, first):
    rows, depth = other_rows.shape
    return pl.pallas_call(
        project_other_kernel,
        out_shape=[jax.ShapeDtypeStruct((2 * rows, 2 * E), BF16)] * 2,
        in_specs=[VMEM] * 3,
        out_specs=[VMEM] * 2,
        scratch_shapes=[pltpu.VMEM(first.shape, BF16)],
        compiler_params=params(16),
        cost_estimate=cost(2 * rows * depth * first.shape[1], 2 * weights.size),
        name="project_other",
    )(other_rows, weights, first)


def pack_kernel(length_ref, prompts_ref, q_ref, g_ref, k_ref, v_ref, *outs):
    heads, _, _ = place()
    row = lax.broadcasted_iota(jnp.int32, (q_ref.shape[0], E), 0)
    note = jnp.where(
        row < NOTE_ROWS,
        length_ref[0],
        jnp.where(row < 2 * NOTE_ROWS, prompts_ref[0, 0], prompts_ref[0, 1]),
    )
    note = note.astype(F32).astype(BF16)
    for head, out in zip(heads, outs):
        start = 0
        for source in (q_ref, g_ref, k_ref, v_ref):
            width = source.shape[1] // len(outs)
            out[:, start : start + width] = source[:, lanes(head, width)]
            start += width
        out[:, start:] = note


def pack(first_length, resp_prompt, queries, out_grad, own_keys, own_values):
    rows = queries.shape[0]
    n = len(MEMBERS)
    width = (2 * queries.shape[1] + 2 * own_keys.shape[1]) // n + E
    return pl.pallas_call(
        pack_kernel,
        out_shape=[jax.ShapeDtypeStruct((rows, width), BF16)] * n,
        in_specs=[SMEM] * 2 + [VMEM] * 4,
        out_specs=[VMEM] * n,
        compiler_params=params(16),
        cost_estimate=cost(0, 4 * n * rows * width),
        name="pack_rows",
    )(first_length, resp_prompt, queries, out_grad, own_keys, own_values)


def unpack_kernel(n, *rest):
    packets, targets = rest[:n], rest[n:]
    heads, _, _ = place()
    for head, packet in zip(heads, packets):
        start = 0
        for target in targets:
            width = target.shape[1] // n
            target[:, lanes(head, width)] = packet[:, start : start + width]
            start += width


def unpack(packets, q_width, kv_width):
    n = len(packets)
    rows = packets[0].shape[0]
    return pl.pallas_call(
        functools.partial(unpack_kernel, n),
        out_shape=[
            jax.ShapeDtypeStruct((rows, width), BF16) for width in (q_width, kv_width, kv_width)
        ],
        in_specs=[VMEM] * n,
        out_specs=[VMEM] * 3,
        compiler_params=params(16),
        cost_estimate=cost(0, 4 * rows * (q_width + 2 * kv_width)),
        name="unpack_rows",
    )(*packets)


def attend_kernel(slots, group, rows, resp_bits, *rest):
    rest = list(rest)

    def take(count):
        taken = rest[:count]
        del rest[:count]
        return taken

    def unstack(near, stacks):
        return near + [stack.at[index] for stack in stacks for index in range(stack.shape[0])]

    pieces = len(slots)
    n = len(MEMBERS)
    packets = take(n)
    kv_in = unstack(take(pieces // 2), take(2))
    grads_out = take(n)
    prefix_out = unstack(take(pieces // 2), take(3))
    keys, values, key_acc, value_acc = rest
    blocks, part, _ = kv_in[0].shape
    _, core, prompt_place = place()

    for index in range(pieces):
        for j in range(blocks):
            prompt, slot = slots[index][j]
            span = slice(slot * part, (slot + 1) * part)
            keys[prompt, span, :] = kv_in[index][j, :, :E]
            values[prompt, span, :] = kv_in[index][j, :, E:]
    key_acc[...] = jnp.zeros_like(key_acc)
    value_acc[...] = jnp.zeros_like(value_acc)

    total_rows = group * rows
    row_in_column = lax.broadcasted_iota(jnp.int32, (total_rows, E), 0) & (rows - 1)
    row_in_lane = lax.broadcasted_iota(jnp.int32, (rows, total_rows), 1) & (rows - 1)
    own_key = lax.broadcasted_iota(jnp.int32, (rows, total_rows), 0)
    lane_row = lax.broadcasted_iota(jnp.int32, (E, total_rows), 1) & (rows - 1)

    def products(j):
        packet = packets[j]
        boundary, first_at, second_at = (
            jnp.max(packet[at : at + NOTE_ROWS, -E:].astype(F32)).astype(jnp.int32)
            for at in (0, NOTE_ROWS, 2 * NOTE_ROWS)
        )
        first_at, second_at = (
            crossed((prompt ^ prompt_place) << resp_bits, core) >> resp_bits
            for prompt in (first_at, second_at)
        )
        heads = [packet[:, h * E : (h + 1) * E] for h in range(2 * group + 2)]
        query = jnp.concatenate(heads[:group], axis=0)
        grad = jnp.concatenate(heads[group : 2 * group], axis=0)
        own_k, own_v = heads[2 * group], heads[2 * group + 1]
        in_first = row_in_column < boundary

        def split(x):
            x = x.astype(F32)
            return jnp.concatenate(
                [jnp.where(in_first, x, 0.0), jnp.where(in_first, 0.0, x)], axis=1
            ).astype(BF16)

        query_pair = split(query)
        grad_pair = split(grad)
        key_pair = jnp.concatenate([keys[first_at], keys[second_at]], axis=1)
        value_pair = jnp.concatenate([values[first_at], values[second_at]], axis=1)

        visible = (own_key <= row_in_lane) & ((own_key >= boundary) == (row_in_lane >= boundary))
        return dict(
            boundary=boundary,
            first_at=first_at,
            second_at=second_at,
            query=query,
            grad=grad,
            own_k=own_k,
            query_pair=query_pair,
            grad_pair=grad_pair,
            key_pair=key_pair,
            scores=dot(key_pair, query_pair, 1, 1),
            own_scores=jnp.where(visible, dot(own_k, query, 1, 1), HIDDEN),
            dprobs=dot(value_pair, grad_pair, 1, 1),
            own_dprobs=dot(own_v, grad, 1, 1),
        )

    def soften(scores, own_scores, dprobs, own_dprobs, **_):
        top = jnp.maximum(
            jnp.max(scores, axis=0, keepdims=True), jnp.max(own_scores, axis=0, keepdims=True)
        )
        weight = jnp.exp2((scores - top) * EXP2_SCALE)
        own_weight = jnp.exp2((own_scores - top) * EXP2_SCALE)
        inverse = 1.0 / (
            jnp.sum(weight, axis=0, keepdims=True) + jnp.sum(own_weight, axis=0, keepdims=True)
        )
        probs = weight * inverse
        own_probs = own_weight * inverse
        probs_low = probs.astype(BF16)
        own_probs_low = own_probs.astype(BF16)
        delta = jnp.sum(probs_low.astype(F32) * dprobs, axis=0, keepdims=True) + jnp.sum(
            own_probs_low.astype(F32) * own_dprobs, axis=0, keepdims=True
        )
        return dict(
            probs_low=probs_low,
            own_probs_low=own_probs_low,
            dscores=(probs * (dprobs - delta)).astype(BF16),
            own_dscores=(own_probs * (own_dprobs - delta)).astype(BF16),
        )

    def gradients(
        grads, boundary, first_at, second_at, query, grad, own_k, query_pair, grad_pair, key_pair,
        probs_low, own_probs_low, dscores, own_dscores, **_
    ):
        key_part = dot(dscores, query_pair, 1, 0)
        value_part = dot(probs_low, grad_pair, 1, 0)
        key_acc[first_at] += key_part[:, :E]
        key_acc[second_at] += key_part[:, E:]
        value_acc[first_at] += value_part[:, :E]
        value_acc[second_at] += value_part[:, E:]

        query_both = dot(key_pair, dscores, 0, 0)
        query_part = jnp.where(lane_row < boundary, query_both[:E], query_both[E:])
        query_part = (query_part + dot(own_k, own_dscores, 0, 0)) * SCALE
        for h in range(group):
            grads[:, h * E : (h + 1) * E] = query_part[:, h * rows : (h + 1) * rows].T.astype(BF16)
        grads[:, group * E : (group + 1) * E] = (dot(own_dscores, query, 1, 0) * SCALE).astype(BF16)
        grads[:, (group + 1) * E :] = dot(own_probs_low, grad, 1, 0).astype(BF16)

    ahead = products(0)
    for j in range(n):
        now = ahead
        if j + 1 < n:
            ahead = products(j + 1)
        gradients(grads_out[j], **now, **soften(**now))

    for index in range(pieces):
        for j in range(blocks):
            prompt, slot = slots[index][j]
            span = slice(slot * part, (slot + 1) * part)
            target = prefix_out[index]
            target[j, :, :E] = (key_acc[prompt, span, :] * SCALE).astype(target.dtype)
            target[j, :, E:] = value_acc[prompt, span, :].astype(target.dtype)


def attend(packets, line, stacks, slots, prompts, resp_bits):
    rows, packet_width = packets[0].shape
    group = (packet_width // E - 3) // 2
    sums_shape = (prompts, PLEN, E)
    out_shape = [jax.ShapeDtypeStruct((rows, (group + 2) * E), BF16)] * len(packets)
    out_shape += [jax.ShapeDtypeStruct(x.shape, F32) for x in line]
    out_shape += [
        jax.ShapeDtypeStruct((count, *line[0].shape), BF16) for count in (1, len(line) - 2, 1)
    ]
    operands = [*packets, *line, *stacks]
    outs = pl.pallas_call(
        functools.partial(attend_kernel, slots, group, rows, resp_bits),
        out_shape=out_shape,
        in_specs=[VMEM] * len(operands),
        out_specs=[VMEM] * len(out_shape),
        scratch_shapes=[pltpu.VMEM(sums_shape, BF16)] * 2 + [pltpu.VMEM(sums_shape, F32)] * 2,
        compiler_params=params(32),
        cost_estimate=cost(
            20 * len(packets) * group * rows * (PLEN + rows) * E, 1 << 24
        ),
        name="attend_head",
    )(*operands)
    return outs[: len(packets)], outs[len(packets) : -3], outs[-3:]


def total_kernel(keep_ref, *rest):
    parts, outs = rest[: -len(MEMBERS)], rest[-len(MEMBERS) :]
    for j, out in enumerate(outs):
        result = keep_ref[j]
        for part in parts:
            result = result + part[j].astype(F32)
        out[...] = result.astype(BF16)


def total(keep, parts):
    return pl.pallas_call(
        total_kernel,
        out_shape=[jax.ShapeDtypeStruct(keep.shape[1:], BF16)] * len(MEMBERS),
        in_specs=[VMEM] * (1 + len(parts)),
        out_specs=[VMEM] * len(MEMBERS),
        compiler_params=params(16),
        cost_estimate=cost(0, 1 << 25),
        name="total_prefix_grads",
    )(keep, *parts)


def prompt_kernel(chunk, members, first, *rest):
    rest = list(rest)
    shares = [rest.pop(0) for _ in members]
    kw_ref, vw_ref = rest.pop(0), rest.pop(0)
    start_ref = None if first else rest.pop(0)
    out_ref, *scratch = rest
    heads, _, _ = place()
    key_grad, value_grad = (
        jnp.concatenate([share[:, at : at + E] for share in shares], axis=1) for at in (0, E)
    )
    copies = []
    for index in range(kw_ref.shape[0] // chunk):
        span = slice(index * chunk, (index + 1) * chunk)
        key_part, value_part = (
            jnp.concatenate([weight[span, lanes(heads[j], E)] for j in members], axis=1)
            for weight in (kw_ref, vw_ref)
        )
        turned = dot(key_part, key_grad, 1, 1) + dot(value_part, value_grad, 1, 1)
        if first:
            out_ref[span, :] = turned
            continue
        out, sems = scratch
        out[:, span] = (turned + start_ref[span, :]).T.astype(BF16)
        copies.append(pltpu.make_async_copy(out.at[:, span], out_ref.at[:, span], sems.at[index]))
        copies[-1].start()
    for copy in copies:
        copy.wait()


def prompt_gradient(members, shares, key_weight, value_weight, start=None, chunk=1024):
    first = start is None
    rows = shares[0].shape[0]
    depth, width = key_weight.shape
    operands = [*shares, key_weight, value_weight] + ([] if first else [start])
    out = jax.ShapeDtypeStruct((depth, rows), F32)
    if not first:
        out = jax.ShapeDtypeStruct((rows, depth), BF16)
    return pl.pallas_call(
        functools.partial(prompt_kernel, chunk, members, first),
        out_shape=out,
        in_specs=[VMEM] * len(operands),
        out_specs=VMEM if first else ANY,
        scratch_shapes=[]
        if first
        else [pltpu.VMEM((rows, depth), BF16), pltpu.SemaphoreType.DMA((depth // chunk,))],
        compiler_params=params(24),
        cost_estimate=cost(2 * rows * depth * width, 2 * depth * width + 2 * rows * depth),
        name="prompt_gradient",
    )(*operands)


def per_device(
    n_prompt,
    n_resp,
    prompt_rows,
    key_weight,
    value_weight,
    queries,
    own_keys,
    own_values,
    out_grad,
    first_length,
    resp_prompt,
):
    devices = n_prompt * n_resp
    every_bit = range(devices.bit_length() - 1)
    line_bits = [bit for bit in GATHER_BITS if bit in every_bit]
    line_bits += [bit for bit in every_bit if bit not in (CORE, X, Y, *line_bits)]
    part = prompt_rows.shape[0]

    def fetch(x, offset):
        pairs = [(i ^ crossed(offset, i >> CORE & 1), i) for i in range(devices)]
        return lax.ppermute(x, ("prompt", "resp"), pairs)

    def give(x, offset):
        pairs = [(i, i ^ crossed(offset, i >> CORE & 1)) for i in range(devices)]
        return lax.ppermute(x, ("prompt", "resp"), pairs)

    other_rows = fetch(prompt_rows, MEMBERS[1])
    first, weights = project(prompt_rows, key_weight, value_weight)
    keep, send = project_other(other_rows, weights, first)
    send, queries = lax.optimization_barrier((send, queries))
    packed = pack(first_length, resp_prompt, queries, out_grad, own_keys, own_values)
    arriving = fetch(send, MEMBERS[2])
    joined = jnp.concatenate([keep, arriving]).reshape(len(MEMBERS), part, -1)
    joined, packed = lax.optimization_barrier((joined, packed))
    packets = [packed[0]] + [fetch(packed[j], MEMBERS[j]) for j in range(1, len(MEMBERS))]

    pieces = {0: joined}
    for bit in line_bits:
        for offset in list(pieces):
            pieces[offset | 1 << bit] = fetch(pieces[offset], 1 << bit)
            if len(pieces) == 2:
                pieces[1 << bit], packets[2] = lax.optimization_barrier(
                    (pieces[1 << bit], packets[2])
                )
    offsets = list(pieces)
    stacks = [
        jnp.stack([pieces[offset] for offset in some]) for some in (offsets[:-1], offsets[-1:])
    ]
    stacks[1], packets = lax.optimization_barrier((stacks[1], packets))
    stacks = [fetch(x, 1 << Y) for x in stacks]

    filled = [0] * n_prompt
    slots = []
    for offset in offsets + [offset | 1 << Y for offset in offsets]:
        places = []
        for member in MEMBERS:
            at = (offset ^ member) // n_resp
            places.append((at, filled[at]))
            filled[at] += 1
        slots.append(tuple(places))
    resp_bits = n_resp.bit_length() - 1
    grads, sums, back_stacks = attend(
        packets, list(pieces.values()), stacks, tuple(slots), n_prompt, resp_bits
    )

    sums = dict(zip(offsets, sums))
    far = give(back_stacks[2], 1 << Y)
    middle = give(back_stacks[1], 1 << Y)
    near = give(back_stacks[0], 1 << Y)
    middle, grads = lax.optimization_barrier((middle, grads))
    back = [grads[0]] + [give(grads[j], MEMBERS[j]) for j in range(1, len(MEMBERS))]
    arrived = {offset: [middle[index]] for index, offset in enumerate(offsets[1:-1])}
    arrived.update({offsets[0]: [near[0]], offsets[-1]: [far[0]]})
    line_ahead = offsets[-1] ^ 1 << line_bits[-1]
    for bit in reversed(line_bits):
        for offset in sorted(sums, reverse=True):
            if offset & 1 << bit:
                piece = sums.pop(offset)
                for x in arrived.pop(offset):
                    piece = piece + x.astype(F32)
                if offset == 1 << bit and bit == line_bits[-1]:
                    ahead = arrived[line_ahead]
                    piece, ahead[-1] = lax.optimization_barrier((piece, ahead[-1]))
                arrived[offset ^ 1 << bit].append(give(piece.astype(BF16), 1 << bit))
    unpacked = unpack(back, queries.shape[1], own_keys.shape[1])
    arrived[0], unpacked = lax.optimization_barrier((arrived[0], unpacked))
    query_grad, key_grad, value_grad = unpacked
    blocks = total(sums[0], arrived[0])
    shares = [blocks[0]] + [give(blocks[j], MEMBERS[j]) for j in range(1, len(MEMBERS))]
    start = prompt_gradient((0, 1), shares[:2], key_weight, value_weight)
    prompt_grad = prompt_gradient((2, 3), shares[2:], key_weight, value_weight, start)
    return (query_grad, key_grad, value_grad, prompt_grad)


def solution(mesh):
    both = P(("prompt", "resp"), None)
    return jax.shard_map(
        functools.partial(per_device, mesh.shape["prompt"], mesh.shape["resp"]),
        mesh=mesh,
        in_specs=(both, P(), P(), both, both, both, both, P(("prompt", "resp")), both),
        out_specs=(both, both, both, both),
        check_vma=False,
    )
```

```python
import functools
import math

import jax
import jax.numpy as jnp
from jax import lax
from jax.experimental import pallas as pl
from jax.experimental.pallas import tpu as pltpu
from jax.sharding import PartitionSpec as P

E = 128
PLEN = 512
SCALE = E ** (-0.5)
EXP2_SCALE = SCALE * math.log2(math.e)
HIDDEN = -1e30
BF16 = jnp.bfloat16
F32 = jnp.float32
NOTE_ROWS = 16
CORE, X, Y = 0, 3, 4
GATHER_BITS = (2, 1)
MEMBERS = (0, 1 << CORE, 1 << X, 1 << X | 1 << CORE)

SMEM = pl.BlockSpec(memory_space=pltpu.SMEM)
ANY = pl.BlockSpec(memory_space=pl.ANY)
VMEM = pl.BlockSpec(memory_space=pltpu.VMEM)


def params(mebibytes=40):
    return pltpu.CompilerParams(vmem_limit_bytes=mebibytes * 1024 * 1024)


def cost(flops, bytes_accessed, transcendentals=0):
    return pl.CostEstimate(
        flops=int(flops), bytes_accessed=int(bytes_accessed), transcendentals=int(transcendentals)
    )


def lanes(index, width):
    return pl.ds(pl.multiple_of(index * width, 128), width)


def dot(a, b, a_dim, b_dim):
    return lax.dot_general(a, b, (((a_dim,), (b_dim,)), ((), ())), preferred_element_type=F32)


def crossed(offset, core):
    change = ((offset >> X) ^ (offset >> Y)) & core
    return offset ^ (change << X | change << Y)


def place():
    prompt = lax.axis_index("prompt")
    device = prompt * lax.axis_size("resp") + lax.axis_index("resp")
    core, x, y = ((device >> bit) & 1 for bit in (CORE, X, Y))
    own, other = jnp.where(core == 0, x, 2 + y), jnp.where(core == 0, 2 + y, x)
    return (own, other, own ^ 1, other ^ 1), core, prompt


def project_kernel(steps, x_ref, kw_ref, vw_ref, out_ref, weights, sems):
    _, core, _ = place()
    width = weights.shape[1] // 2
    chunk = weights.shape[0] // steps
    copies = []
    for step in range(steps):
        span = slice(step * chunk, (step + 1) * chunk)
        for index, source in enumerate((kw_ref, vw_ref)):
            copies.append(
                pltpu.make_async_copy(
                    source.at[span, lanes(core, width)],
                    weights.at[span, index * width : (index + 1) * width],
                    sems.at[len(copies)],
                )
            )
    for copy in copies[:8]:
        copy.start()
    total = None
    for step in range(steps):
        span = slice(step * chunk, (step + 1) * chunk)
        copies[2 * step].wait()
        copies[2 * step + 1].wait()
        for copy in copies[2 * step + 8 : 2 * step + 10]:
            copy.start()
        product = dot(x_ref[:, span], weights[span, :], 1, 0)
        total = product if step == 0 else total + product
    out_ref[...] = total.astype(BF16)


def project(prompt_rows, key_weight, value_weight, steps=10):
    rows = prompt_rows.shape[0]
    depth, width = key_weight.shape
    return pl.pallas_call(
        functools.partial(project_kernel, steps),
        out_shape=[
            jax.ShapeDtypeStruct((rows, width), BF16),
            jax.ShapeDtypeStruct((depth, width), BF16),
        ],
        in_specs=[VMEM, ANY, ANY],
        out_specs=[VMEM] * 2,
        scratch_shapes=[pltpu.SemaphoreType.DMA((2 * steps,))],
        compiler_params=params(44),
        cost_estimate=cost(2 * rows * depth * width, 2 * depth * width + 2 * rows * depth),
        name="project_own",
    )(prompt_rows, key_weight, value_weight)


def project_other_kernel(x_ref, weights, first_ref, keep_ref, send_ref, second_ref):
    heads, _, _ = place()
    second_ref[...] = dot(x_ref[...], weights[...], 1, 0).astype(BF16)
    part = x_ref.shape[0]
    for out, head in ((keep_ref, heads[0] & 1), (send_ref, heads[2] & 1)):
        for index, source in enumerate((first_ref, second_ref)):
            span = slice(index * part, (index + 1) * part)
            out[span, :E] = source[:, lanes(head, E)]
            out[span, E:] = source[:, lanes(head + 2, E)]


def project_other(other_rows, weights, first):
    rows, depth = other_rows.shape
    return pl.pallas_call(
        project_other_kernel,
        out_shape=[jax.ShapeDtypeStruct((2 * rows, 2 * E), BF16)] * 2,
        in_specs=[VMEM] * 3,
        out_specs=[VMEM] * 2,
        scratch_shapes=[pltpu.VMEM(first.shape, BF16)],
        compiler_params=params(16),
        cost_estimate=cost(2 * rows * depth * first.shape[1], 2 * weights.size),
        name="project_other",
    )(other_rows, weights, first)


def pack_kernel(length_ref, prompts_ref, q_ref, g_ref, k_ref, v_ref, *outs):
    heads, _, _ = place()
    row = lax.broadcasted_iota(jnp.int32, (q_ref.shape[0], E), 0)
    note = jnp.where(
        row < NOTE_ROWS,
        length_ref[0],
        jnp.where(row < 2 * NOTE_ROWS, prompts_ref[0, 0], prompts_ref[0, 1]),
    )
    note = note.astype(F32).astype(BF16)
    for head, out in zip(heads, outs):
        start = 0
        for source in (q_ref, g_ref, k_ref, v_ref):
            width = source.shape[1] // len(outs)
            out[:, start : start + width] = source[:, lanes(head, width)]
            start += width
        out[:, start:] = note


def pack(first_length, resp_prompt, queries, out_grad, own_keys, own_values):
    rows = queries.shape[0]
    n = len(MEMBERS)
    width = (2 * queries.shape[1] + 2 * own_keys.shape[1]) // n + E
    return pl.pallas_call(
        pack_kernel,
        out_shape=[jax.ShapeDtypeStruct((rows, width), BF16)] * n,
        in_specs=[SMEM] * 2 + [VMEM] * 4,
        out_specs=[VMEM] * n,
        compiler_params=params(16),
        cost_estimate=cost(0, 4 * n * rows * width),
        name="pack_rows",
    )(first_length, resp_prompt, queries, out_grad, own_keys, own_values)


def unpack_kernel(n, *rest):
    packets, targets = rest[:n], rest[n:]
    heads, _, _ = place()
    for head, packet in zip(heads, packets):
        start = 0
        for target in targets:
            width = target.shape[1] // n
            target[:, lanes(head, width)] = packet[:, start : start + width]
            start += width


def unpack(packets, q_width, kv_width):
    n = len(packets)
    rows = packets[0].shape[0]
    return pl.pallas_call(
        functools.partial(unpack_kernel, n),
        out_shape=[
            jax.ShapeDtypeStruct((rows, width), BF16) for width in (q_width, kv_width, kv_width)
        ],
        in_specs=[VMEM] * n,
        out_specs=[VMEM] * 3,
        compiler_params=params(16),
        cost_estimate=cost(0, 4 * rows * (q_width + 2 * kv_width)),
        name="unpack_rows",
    )(*packets)


def unstack(near, stacks):
    return near + [stack.at[index] for stack in stacks for index in range(stack.shape[0])]


def open_packet(packet, group, resp_bits):
    _, core, prompt_place = place()
    rows = packet.shape[0]
    boundary, first_at, second_at = (
        jnp.max(packet[at : at + NOTE_ROWS, -E:].astype(F32)).astype(jnp.int32)
        for at in (0, NOTE_ROWS, 2 * NOTE_ROWS)
    )
    first_at, second_at = (
        crossed((prompt ^ prompt_place) << resp_bits, core) >> resp_bits
        for prompt in (first_at, second_at)
    )
    heads = [packet[:, h * E : (h + 1) * E] for h in range(2 * group + 2)]
    query = jnp.concatenate(heads[:group], axis=0)
    grad = jnp.concatenate(heads[group : 2 * group], axis=0)
    row_in_column = lax.broadcasted_iota(jnp.int32, (group * rows, E), 0) & (rows - 1)
    in_first = row_in_column < boundary

    def split(x):
        x = x.astype(F32)
        return jnp.concatenate(
            [jnp.where(in_first, x, 0.0), jnp.where(in_first, 0.0, x)], axis=1
        ).astype(BF16)

    return dict(
        boundary=boundary,
        first_at=first_at,
        second_at=second_at,
        query=query,
        grad=grad,
        own_k=heads[2 * group],
        own_v=heads[2 * group + 1],
        query_pair=split(query),
        grad_pair=split(grad),
    )


def scores_kernel(slots, group, rows, resp_bits, *rest):
    rest = list(rest)

    def take(count):
        taken = rest[:count]
        del rest[:count]
        return taken

    pieces = len(slots)
    n = len(MEMBERS)
    packets = take(n)
    kv_in = unstack(take(pieces // 2), take(2))
    probs_out, dscores_out, keys, far_out, far_key, far_value, values = rest
    blocks, part, _ = kv_in[0].shape

    for index in range(pieces):
        for j in range(blocks):
            prompt, slot = slots[index][j]
            span = slice(slot * part, (slot + 1) * part)
            keys[prompt, span, :] = kv_in[index][j, :, :E]
            values[prompt, span, :] = kv_in[index][j, :, E:]
    far_key[...] = jnp.zeros_like(far_key)
    far_value[...] = jnp.zeros_like(far_value)

    total_rows = group * rows
    row_in_lane = lax.broadcasted_iota(jnp.int32, (rows, total_rows), 1) & (rows - 1)
    own_key = lax.broadcasted_iota(jnp.int32, (rows, total_rows), 0)

    def products(j):
        view = open_packet(packets[j], group, resp_bits)
        boundary, first_at, second_at = view["boundary"], view["first_at"], view["second_at"]
        key_pair = jnp.concatenate([keys[first_at], keys[second_at]], axis=1)
        value_pair = jnp.concatenate([values[first_at], values[second_at]], axis=1)
        visible = (own_key <= row_in_lane) & ((own_key >= boundary) == (row_in_lane >= boundary))
        return dict(
            view,
            scores=dot(key_pair, view["query_pair"], 1, 1),
            own_scores=jnp.where(visible, dot(view["own_k"], view["query"], 1, 1), HIDDEN),
            dprobs=dot(value_pair, view["grad_pair"], 1, 1),
            own_dprobs=dot(view["own_v"], view["grad"], 1, 1),
        )

    def soften(scores, own_scores, dprobs, own_dprobs, **_):
        top = jnp.maximum(
            jnp.max(scores, axis=0, keepdims=True), jnp.max(own_scores, axis=0, keepdims=True)
        )
        weight = jnp.exp2((scores - top) * EXP2_SCALE)
        own_weight = jnp.exp2((own_scores - top) * EXP2_SCALE)
        inverse = 1.0 / (
            jnp.sum(weight, axis=0, keepdims=True) + jnp.sum(own_weight, axis=0, keepdims=True)
        )
        probs = weight * inverse
        own_probs = own_weight * inverse
        probs_low = probs.astype(BF16)
        own_probs_low = own_probs.astype(BF16)
        delta = jnp.sum(probs_low.astype(F32) * dprobs, axis=0, keepdims=True) + jnp.sum(
            own_probs_low.astype(F32) * own_dprobs, axis=0, keepdims=True
        )
        return dict(
            probs_low=probs_low,
            own_probs_low=own_probs_low,
            dscores=(probs * (dprobs - delta)).astype(BF16),
            own_dscores=(own_probs * (own_dprobs - delta)).astype(BF16),
        )

    ahead = products(0)
    for j in range(n):
        now = ahead
        if j + 1 < n:
            ahead = products(j + 1)
        soft = soften(**now)
        probs_out[j, :PLEN, :] = soft["probs_low"]
        probs_out[j, PLEN:, :] = soft["own_probs_low"]
        dscores_out[j, :PLEN, :] = soft["dscores"]
        dscores_out[j, PLEN:, :] = soft["own_dscores"]
        key_part = dot(soft["dscores"][PLEN - E :, :], now["query_pair"], 1, 0)
        value_part = dot(soft["probs_low"][PLEN - E :, :], now["grad_pair"], 1, 0)
        for total, part_sum in ((far_key, key_part), (far_value, value_part)):
            total[now["first_at"]] += part_sum[:, :E]
            total[now["second_at"]] += part_sum[:, E:]

    for j in range(blocks):
        prompt, slot = slots[-1][j]
        span = slice(slot * part - (PLEN - E), (slot + 1) * part - (PLEN - E))
        far_out[0, j, :, :E] = (far_key[prompt, span, :] * SCALE).astype(BF16)
        far_out[0, j, :, E:] = far_value[prompt, span, :].astype(BF16)


def attend_scores(packets, line, stacks, slots, prompts, resp_bits):
    rows, packet_width = packets[0].shape
    group = (packet_width // E - 3) // 2
    operands = [*packets, *line, *stacks]
    low_shape = (len(packets), PLEN + rows, group * rows)
    out_shape = [
        jax.ShapeDtypeStruct(low_shape, BF16),
        jax.ShapeDtypeStruct(low_shape, BF16),
        jax.ShapeDtypeStruct((prompts, PLEN, E), BF16),
        jax.ShapeDtypeStruct((1, *line[0].shape), BF16),
        jax.ShapeDtypeStruct((prompts, E, E), F32),
        jax.ShapeDtypeStruct((prompts, E, E), F32),
    ]
    return pl.pallas_call(
        functools.partial(scores_kernel, slots, group, rows, resp_bits),
        out_shape=out_shape,
        in_specs=[VMEM] * len(operands),
        out_specs=[VMEM] * len(out_shape),
        scratch_shapes=[pltpu.VMEM((prompts, PLEN, E), BF16)],
        compiler_params=params(32),
        cost_estimate=cost(10 * len(packets) * group * rows * (PLEN + rows) * E, 1 << 23),
        name="attend_scores",
    )(*operands)


def prefix_kernel(slots, group, resp_bits, *rest):
    rest = list(rest)
    n = len(MEMBERS)
    packets, rest = rest[:n], rest[n:]
    probs, dscores, far_key, far_value, *outs = rest
    *outs, key_acc, value_acc = outs
    targets = unstack(outs[:-2], outs[-2:])
    blocks, part, _ = targets[0].shape
    start = PLEN - E
    key_acc[...] = jnp.zeros_like(key_acc)
    value_acc[...] = jnp.zeros_like(value_acc)
    for j in range(n):
        view = open_packet(packets[j], group, resp_bits)
        key_part = dot(dscores[j, :start, :], view["query_pair"], 1, 0)
        value_part = dot(probs[j, :start, :], view["grad_pair"], 1, 0)
        for total, part_sum in ((key_acc, key_part), (value_acc, value_part)):
            total[view["first_at"]] += part_sum[:, :E]
            total[view["second_at"]] += part_sum[:, E:]
    for index, target in enumerate(targets):
        for j in range(blocks):
            prompt, slot = slots[index][j]
            at = slot * part
            key_sum, value_sum = (key_acc, value_acc) if at < start else (far_key, far_value)
            at = at if at < start else at - start
            target[j, :, :E] = (key_sum[prompt, at : at + part, :] * SCALE).astype(target.dtype)
            target[j, :, E:] = value_sum[prompt, at : at + part, :].astype(target.dtype)


def attend_prefix(packets, probs, dscores, far_key, far_value, slots, shape, resp_bits):
    rows, packet_width = packets[0].shape
    group = (packet_width // E - 3) // 2
    prompts = far_key.shape[0]
    count = len(slots) // 2
    out_shape = [jax.ShapeDtypeStruct(shape, F32)] * count
    out_shape += [jax.ShapeDtypeStruct((k, *shape), BF16) for k in (1, count - 2)]
    operands = [*packets, probs, dscores, far_key, far_value]
    outs = pl.pallas_call(
        functools.partial(prefix_kernel, slots, group, resp_bits),
        out_shape=out_shape,
        in_specs=[VMEM] * len(operands),
        out_specs=[VMEM] * len(out_shape),
        scratch_shapes=[pltpu.VMEM((prompts, PLEN - E, E), F32)] * 2,
        compiler_params=params(32),
        cost_estimate=cost(6 * len(packets) * group * rows * PLEN * E, 1 << 22),
        name="attend_prefix",
    )(*operands)
    return outs[:-2], outs[-2], outs[-1]


def rows_kernel(group, resp_bits, *rest):
    n = len(MEMBERS)
    packets, (probs, dscores, keys), outs = rest[:n], rest[n : n + 3], rest[n + 3 :]
    rows = packets[0].shape[0]
    lane_row = lax.broadcasted_iota(jnp.int32, (E, group * rows), 1) & (rows - 1)
    for j, (packet, out) in enumerate(zip(packets, outs)):
        view = open_packet(packet, group, resp_bits)
        key_pair = jnp.concatenate([keys[view["first_at"]], keys[view["second_at"]]], axis=1)
        own_dscores = dscores[j, PLEN:, :]
        both = dot(key_pair, dscores[j, :PLEN, :], 0, 0)
        whole = jnp.where(lane_row < view["boundary"], both[:E], both[E:])
        whole = (whole + dot(view["own_k"], own_dscores, 0, 0)) * SCALE
        for h in range(group):
            out[:, h * E : (h + 1) * E] = whole[:, h * rows : (h + 1) * rows].T.astype(BF16)
        key_grad = dot(own_dscores, view["query"], 1, 0) * SCALE
        out[:, group * E : (group + 1) * E] = key_grad.astype(BF16)
        out[:, (group + 1) * E :] = dot(probs[j, PLEN:, :], view["grad"], 1, 0).astype(BF16)


def attend_rows(packets, probs, dscores, keys, resp_bits):
    rows, packet_width = packets[0].shape
    group = (packet_width // E - 3) // 2
    operands = [*packets, probs, dscores, keys]
    return pl.pallas_call(
        functools.partial(rows_kernel, group, resp_bits),
        out_shape=[jax.ShapeDtypeStruct((rows, (group + 2) * E), BF16)] * len(packets),
        in_specs=[VMEM] * len(operands),
        out_specs=[VMEM] * len(packets),
        compiler_params=params(32),
        cost_estimate=cost(6 * len(packets) * group * rows * PLEN * E, 1 << 22),
        name="attend_rows",
    )(*operands)


def total_kernel(keep_ref, *rest):
    parts, outs = rest[: -len(MEMBERS)], rest[-len(MEMBERS) :]
    for j, out in enumerate(outs):
        result = keep_ref[j]
        for part in parts:
            result = result + part[j].astype(F32)
        out[...] = result.astype(BF16)


def total(keep, parts):
    return pl.pallas_call(
        total_kernel,
        out_shape=[jax.ShapeDtypeStruct(keep.shape[1:], BF16)] * len(MEMBERS),
        in_specs=[VMEM] * (1 + len(parts)),
        out_specs=[VMEM] * len(MEMBERS),
        compiler_params=params(16),
        cost_estimate=cost(0, 1 << 25),
        name="total_prefix_grads",
    )(keep, *parts)


def prompt_kernel(chunk, members, first, *rest):
    rest = list(rest)
    shares = [rest.pop(0) for _ in members]
    kw_ref, vw_ref = rest.pop(0), rest.pop(0)
    start_ref = None if first else rest.pop(0)
    out_ref, *scratch = rest
    heads, _, _ = place()
    key_grad, value_grad = (
        jnp.concatenate([share[:, at : at + E] for share in shares], axis=1) for at in (0, E)
    )
    copies = []
    for index in range(kw_ref.shape[0] // chunk):
        span = slice(index * chunk, (index + 1) * chunk)
        key_part, value_part = (
            jnp.concatenate([weight[span, lanes(heads[j], E)] for j in members], axis=1)
            for weight in (kw_ref, vw_ref)
        )
        turned = dot(key_part, key_grad, 1, 1) + dot(value_part, value_grad, 1, 1)
        if first:
            out_ref[span, :] = turned
            continue
        out, sems = scratch
        out[:, span] = (turned + start_ref[span, :]).T.astype(BF16)
        copies.append(pltpu.make_async_copy(out.at[:, span], out_ref.at[:, span], sems.at[index]))
        copies[-1].start()
    for copy in copies:
        copy.wait()


def prompt_gradient(members, shares, key_weight, value_weight, start=None, chunk=1024):
    first = start is None
    rows = shares[0].shape[0]
    depth, width = key_weight.shape
    operands = [*shares, key_weight, value_weight] + ([] if first else [start])
    out = jax.ShapeDtypeStruct((depth, rows), F32)
    if not first:
        out = jax.ShapeDtypeStruct((rows, depth), BF16)
    return pl.pallas_call(
        functools.partial(prompt_kernel, chunk, members, first),
        out_shape=out,
        in_specs=[VMEM] * len(operands),
        out_specs=VMEM if first else ANY,
        scratch_shapes=[]
        if first
        else [pltpu.VMEM((rows, depth), BF16), pltpu.SemaphoreType.DMA((depth // chunk,))],
        compiler_params=params(24),
        cost_estimate=cost(2 * rows * depth * width, 2 * depth * width + 2 * rows * depth),
        name="prompt_gradient",
    )(*operands)


def per_device(
    n_prompt,
    n_resp,
    prompt_rows,
    key_weight,
    value_weight,
    queries,
    own_keys,
    own_values,
    out_grad,
    first_length,
    resp_prompt,
):
    devices = n_prompt * n_resp
    every_bit = range(devices.bit_length() - 1)
    line_bits = [bit for bit in GATHER_BITS if bit in every_bit]
    line_bits += [bit for bit in every_bit if bit not in (CORE, X, Y, *line_bits)]
    part = prompt_rows.shape[0]

    def fetch(x, offset):
        pairs = [(i ^ crossed(offset, i >> CORE & 1), i) for i in range(devices)]
        return lax.ppermute(x, ("prompt", "resp"), pairs)

    def give(x, offset):
        pairs = [(i, i ^ crossed(offset, i >> CORE & 1)) for i in range(devices)]
        return lax.ppermute(x, ("prompt", "resp"), pairs)

    other_rows = fetch(prompt_rows, MEMBERS[1])
    first, weights = project(prompt_rows, key_weight, value_weight)
    keep, send = project_other(other_rows, weights, first)
    send, queries = lax.optimization_barrier((send, queries))
    packed = pack(first_length, resp_prompt, queries, out_grad, own_keys, own_values)
    arriving = fetch(send, MEMBERS[2])
    joined = jnp.concatenate([keep, arriving]).reshape(len(MEMBERS), part, -1)
    joined, packed = lax.optimization_barrier((joined, packed))
    packets = [packed[0]] + [fetch(packed[j], MEMBERS[j]) for j in range(1, len(MEMBERS))]

    pieces = {0: joined}
    for bit in line_bits:
        for offset in list(pieces):
            pieces[offset | 1 << bit] = fetch(pieces[offset], 1 << bit)
            if len(pieces) == 2:
                pieces[1 << bit], packets[2] = lax.optimization_barrier(
                    (pieces[1 << bit], packets[2])
                )
    offsets = list(pieces)
    stacks = [
        jnp.stack([pieces[offset] for offset in some]) for some in (offsets[:-1], offsets[-1:])
    ]
    stacks[1], packets = lax.optimization_barrier((stacks[1], packets))
    stacks = [fetch(x, 1 << Y) for x in stacks]

    filled = [0] * n_prompt
    slots = []
    for offset in offsets + [offset | 1 << Y for offset in offsets]:
        places = []
        for member in MEMBERS:
            at = (offset ^ member) // n_resp
            places.append((at, filled[at]))
            filled[at] += 1
        slots.append(tuple(places))
    resp_bits = n_resp.bit_length() - 1
    line = list(pieces.values())
    slots = tuple(slots)
    probs, dscores, keys, far, far_key, far_value = attend_scores(
        packets, line, stacks, slots, n_prompt, resp_bits
    )
    far = give(far, 1 << Y)
    sums, near, middle = attend_prefix(
        packets, probs, dscores, far_key, far_value, slots, line[0].shape, resp_bits
    )
    sums = dict(zip(offsets, sums))
    middle = give(middle, 1 << Y)
    near = give(near, 1 << Y)
    far, dscores = lax.optimization_barrier((far, dscores))
    grads = attend_rows(packets, probs, dscores, keys, resp_bits)
    back = [grads[0]] + [give(grads[j], MEMBERS[j]) for j in range(1, len(MEMBERS))]
    arrived = {offset: [middle[index]] for index, offset in enumerate(offsets[1:-1])}
    arrived.update({offsets[0]: [near[0]], offsets[-1]: [far[0]]})
    line_ahead = offsets[-1] ^ 1 << line_bits[-1]
    for bit in reversed(line_bits):
        for offset in sorted(sums, reverse=True):
            if offset & 1 << bit:
                piece = sums.pop(offset)
                for x in arrived.pop(offset):
                    piece = piece + x.astype(F32)
                if offset == 1 << bit and bit == line_bits[-1]:
                    ahead = arrived[line_ahead]
                    piece, ahead[-1] = lax.optimization_barrier((piece, ahead[-1]))
                arrived[offset ^ 1 << bit].append(give(piece.astype(BF16), 1 << bit))
    unpacked = unpack(back, queries.shape[1], own_keys.shape[1])
    arrived[0], unpacked = lax.optimization_barrier((arrived[0], unpacked))
    query_grad, key_grad, value_grad = unpacked
    blocks = total(sums[0], arrived[0])
    shares = [blocks[0]] + [give(blocks[j], MEMBERS[j]) for j in range(1, len(MEMBERS))]
    start = prompt_gradient((0, 1), shares[:2], key_weight, value_weight)
    prompt_grad = prompt_gradient((2, 3), shares[2:], key_weight, value_weight, start)
    return (query_grad, key_grad, value_grad, prompt_grad)


def solution(mesh):
    both = P(("prompt", "resp"), None)
    return jax.shard_map(
        functools.partial(per_device, mesh.shape["prompt"], mesh.shape["resp"]),
        mesh=mesh,
        in_specs=(both, P(), P(), both, both, both, both, P(("prompt", "resp")), both),
        out_specs=(both, both, both, both),
        check_vma=False,
    )
```

```python
import functools
import math

import jax
import jax.numpy as jnp
from jax import lax
from jax.experimental import pallas as pl
from jax.experimental.pallas import tpu as pltpu
from jax.sharding import PartitionSpec as P

E = 128
PLEN = 512
SCALE = E ** (-0.5)
EXP2_SCALE = SCALE * math.log2(math.e)
HIDDEN = -1e30
BF16 = jnp.bfloat16
F32 = jnp.float32
NOTE_ROWS = 16
CORE, X, Y = 0, 3, 4
GATHER_BITS = (2, 1)
MEMBERS = (0, 1 << CORE, 1 << X, 1 << X | 1 << CORE)

SMEM = pl.BlockSpec(memory_space=pltpu.SMEM)
ANY = pl.BlockSpec(memory_space=pl.ANY)
VMEM = pl.BlockSpec(memory_space=pltpu.VMEM)


def params(mebibytes=40):
    return pltpu.CompilerParams(vmem_limit_bytes=mebibytes * 1024 * 1024)


def cost(flops, bytes_accessed, transcendentals=0):
    return pl.CostEstimate(
        flops=int(flops), bytes_accessed=int(bytes_accessed), transcendentals=int(transcendentals)
    )


def lanes(index, width):
    return pl.ds(pl.multiple_of(index * width, 128), width)


def dot(a, b, a_dim, b_dim):
    return lax.dot_general(a, b, (((a_dim,), (b_dim,)), ((), ())), preferred_element_type=F32)


def crossed(offset, core):
    change = ((offset >> X) ^ (offset >> Y)) & core
    return offset ^ (change << X | change << Y)


def place():
    prompt = lax.axis_index("prompt")
    device = prompt * lax.axis_size("resp") + lax.axis_index("resp")
    core, x, y = ((device >> bit) & 1 for bit in (CORE, X, Y))
    own, other = jnp.where(core == 0, x, 2 + y), jnp.where(core == 0, 2 + y, x)
    return (own, other, own ^ 1, other ^ 1), core, prompt


def project_kernel(steps, x_ref, kw_ref, vw_ref, out_ref, weights, sems):
    _, core, _ = place()
    width = weights.shape[1] // 2
    chunk = weights.shape[0] // steps
    copies = []
    for step in range(steps):
        span = slice(step * chunk, (step + 1) * chunk)
        for index, source in enumerate((kw_ref, vw_ref)):
            copies.append(
                pltpu.make_async_copy(
                    source.at[span, lanes(core, width)],
                    weights.at[span, index * width : (index + 1) * width],
                    sems.at[len(copies)],
                )
            )
    for copy in copies[:8]:
        copy.start()
    total = None
    for step in range(steps):
        span = slice(step * chunk, (step + 1) * chunk)
        copies[2 * step].wait()
        copies[2 * step + 1].wait()
        for copy in copies[2 * step + 8 : 2 * step + 10]:
            copy.start()
        product = dot(x_ref[:, span], weights[span, :], 1, 0)
        total = product if step == 0 else total + product
    out_ref[...] = total.astype(BF16)


def project(prompt_rows, key_weight, value_weight, steps=10):
    rows = prompt_rows.shape[0]
    depth, width = key_weight.shape
    return pl.pallas_call(
        functools.partial(project_kernel, steps),
        out_shape=[
            jax.ShapeDtypeStruct((rows, width), BF16),
            jax.ShapeDtypeStruct((depth, width), BF16),
        ],
        in_specs=[VMEM, ANY, ANY],
        out_specs=[VMEM] * 2,
        scratch_shapes=[pltpu.SemaphoreType.DMA((2 * steps,))],
        compiler_params=params(44),
        cost_estimate=cost(2 * rows * depth * width, 2 * depth * width + 2 * rows * depth),
        name="project_own",
    )(prompt_rows, key_weight, value_weight)


def project_other_kernel(x_ref, weights, first_ref, keep_ref, send_ref, second_ref):
    heads, _, _ = place()
    second_ref[...] = dot(x_ref[...], weights[...], 1, 0).astype(BF16)
    part = x_ref.shape[0]
    for out, head in ((keep_ref, heads[0] & 1), (send_ref, heads[2] & 1)):
        for index, source in enumerate((first_ref, second_ref)):
            span = slice(index * part, (index + 1) * part)
            out[span, :E] = source[:, lanes(head, E)]
            out[span, E:] = source[:, lanes(head + 2, E)]


def project_other(other_rows, weights, first):
    rows, depth = other_rows.shape
    return pl.pallas_call(
        project_other_kernel,
        out_shape=[jax.ShapeDtypeStruct((2 * rows, 2 * E), BF16)] * 2,
        in_specs=[VMEM] * 3,
        out_specs=[VMEM] * 2,
        scratch_shapes=[pltpu.VMEM(first.shape, BF16)],
        compiler_params=params(16),
        cost_estimate=cost(2 * rows * depth * first.shape[1], 2 * weights.size),
        name="project_other",
    )(other_rows, weights, first)


def pack_kernel(length_ref, prompts_ref, q_ref, g_ref, k_ref, v_ref, *outs):
    heads, _, _ = place()
    row = lax.broadcasted_iota(jnp.int32, (q_ref.shape[0], E), 0)
    note = jnp.where(
        row < NOTE_ROWS,
        length_ref[0],
        jnp.where(row < 2 * NOTE_ROWS, prompts_ref[0, 0], prompts_ref[0, 1]),
    )
    note = note.astype(F32).astype(BF16)
    for head, out in zip(heads, outs):
        start = 0
        for source in (q_ref, g_ref, k_ref, v_ref):
            width = source.shape[1] // len(outs)
            out[:, start : start + width] = source[:, lanes(head, width)]
            start += width
        out[:, start:] = note


def pack(first_length, resp_prompt, queries, out_grad, own_keys, own_values):
    rows = queries.shape[0]
    n = len(MEMBERS)
    width = (2 * queries.shape[1] + 2 * own_keys.shape[1]) // n + E
    return pl.pallas_call(
        pack_kernel,
        out_shape=[jax.ShapeDtypeStruct((rows, width), BF16)] * n,
        in_specs=[SMEM] * 2 + [VMEM] * 4,
        out_specs=[VMEM] * n,
        compiler_params=params(16),
        cost_estimate=cost(0, 4 * n * rows * width),
        name="pack_rows",
    )(first_length, resp_prompt, queries, out_grad, own_keys, own_values)


def unpack_kernel(n, *rest):
    packets, targets = rest[:n], rest[n:]
    heads, _, _ = place()
    for head, packet in zip(heads, packets):
        start = 0
        for target in targets:
            width = target.shape[1] // n
            target[:, lanes(head, width)] = packet[:, start : start + width]
            start += width


def unpack(packets, q_width, kv_width):
    n = len(packets)
    rows = packets[0].shape[0]
    return pl.pallas_call(
        functools.partial(unpack_kernel, n),
        out_shape=[
            jax.ShapeDtypeStruct((rows, width), BF16) for width in (q_width, kv_width, kv_width)
        ],
        in_specs=[VMEM] * n,
        out_specs=[VMEM] * 3,
        compiler_params=params(16),
        cost_estimate=cost(0, 4 * rows * (q_width + 2 * kv_width)),
        name="unpack_rows",
    )(*packets)


def unstack(near, stacks):
    return near + [stack.at[index] for stack in stacks for index in range(stack.shape[0])]


def open_packet(packet, group, resp_bits):
    _, core, prompt_place = place()
    rows = packet.shape[0]
    boundary, first_at, second_at = (
        jnp.max(packet[at : at + NOTE_ROWS, -E:].astype(F32)).astype(jnp.int32)
        for at in (0, NOTE_ROWS, 2 * NOTE_ROWS)
    )
    first_at, second_at = (
        crossed((prompt ^ prompt_place) << resp_bits, core) >> resp_bits
        for prompt in (first_at, second_at)
    )
    heads = [packet[:, h * E : (h + 1) * E] for h in range(2 * group + 2)]
    query = jnp.concatenate(heads[:group], axis=0)
    grad = jnp.concatenate(heads[group : 2 * group], axis=0)
    row_in_column = lax.broadcasted_iota(jnp.int32, (group * rows, E), 0) & (rows - 1)
    in_first = row_in_column < boundary

    def split(x):
        x = x.astype(F32)
        return jnp.concatenate(
            [jnp.where(in_first, x, 0.0), jnp.where(in_first, 0.0, x)], axis=1
        ).astype(BF16)

    return dict(
        boundary=boundary,
        first_at=first_at,
        second_at=second_at,
        query=query,
        grad=grad,
        own_k=heads[2 * group],
        own_v=heads[2 * group + 1],
        query_pair=split(query),
        grad_pair=split(grad),
    )


def scores_kernel(slots, group, rows, resp_bits, *rest):
    rest = list(rest)

    def take(count):
        taken = rest[:count]
        del rest[:count]
        return taken

    pieces = len(slots)
    n = len(MEMBERS)
    packets = take(n)
    kv_in = unstack(take(pieces // 2), take(2))
    probs_out, dscores_out, keys, far_out, far_key, far_value, values = rest
    blocks, part, _ = kv_in[0].shape

    for index in range(pieces):
        for j in range(blocks):
            prompt, slot = slots[index][j]
            span = slice(slot * part, (slot + 1) * part)
            keys[prompt, span, :] = kv_in[index][j, :, :E]
            values[prompt, span, :] = kv_in[index][j, :, E:]
    far_key[...] = jnp.zeros_like(far_key)
    far_value[...] = jnp.zeros_like(far_value)

    total_rows = group * rows
    row_in_lane = lax.broadcasted_iota(jnp.int32, (rows, total_rows), 1) & (rows - 1)
    own_key = lax.broadcasted_iota(jnp.int32, (rows, total_rows), 0)

    def products(j):
        view = open_packet(packets[j], group, resp_bits)
        boundary, first_at, second_at = view["boundary"], view["first_at"], view["second_at"]
        key_pair = jnp.concatenate([keys[first_at], keys[second_at]], axis=1)
        value_pair = jnp.concatenate([values[first_at], values[second_at]], axis=1)
        visible = (own_key <= row_in_lane) & ((own_key >= boundary) == (row_in_lane >= boundary))
        return dict(
            view,
            scores=dot(key_pair, view["query_pair"], 1, 1),
            own_scores=jnp.where(visible, dot(view["own_k"], view["query"], 1, 1), HIDDEN),
            dprobs=dot(value_pair, view["grad_pair"], 1, 1),
            own_dprobs=dot(view["own_v"], view["grad"], 1, 1),
        )

    def soften(scores, own_scores, dprobs, own_dprobs, **_):
        top = jnp.maximum(
            jnp.max(scores, axis=0, keepdims=True), jnp.max(own_scores, axis=0, keepdims=True)
        )
        weight = jnp.exp2((scores - top) * EXP2_SCALE)
        own_weight = jnp.exp2((own_scores - top) * EXP2_SCALE)
        inverse = 1.0 / (
            jnp.sum(weight, axis=0, keepdims=True) + jnp.sum(own_weight, axis=0, keepdims=True)
        )
        probs = weight * inverse
        own_probs = own_weight * inverse
        probs_low = probs.astype(BF16)
        own_probs_low = own_probs.astype(BF16)
        delta = jnp.sum(probs_low.astype(F32) * dprobs, axis=0, keepdims=True) + jnp.sum(
            own_probs_low.astype(F32) * own_dprobs, axis=0, keepdims=True
        )
        return dict(
            probs_low=probs_low,
            own_probs_low=own_probs_low,
            dscores=(probs * (dprobs - delta)).astype(BF16),
            own_dscores=(own_probs * (own_dprobs - delta)).astype(BF16),
        )

    ahead = products(0)
    for j in range(n):
        now = ahead
        if j + 1 < n:
            ahead = products(j + 1)
        soft = soften(**now)
        probs_out[j, :PLEN, :] = soft["probs_low"]
        probs_out[j, PLEN:, :] = soft["own_probs_low"]
        dscores_out[j, :PLEN, :] = soft["dscores"]
        dscores_out[j, PLEN:, :] = soft["own_dscores"]
        key_part = dot(soft["dscores"][PLEN - E :, :], now["query_pair"], 1, 0)
        value_part = dot(soft["probs_low"][PLEN - E :, :], now["grad_pair"], 1, 0)
        for total, part_sum in ((far_key, key_part), (far_value, value_part)):
            total[now["first_at"]] += part_sum[:, :E]
            total[now["second_at"]] += part_sum[:, E:]

    for j in range(blocks):
        prompt, slot = slots[-1][j]
        span = slice(slot * part - (PLEN - E), (slot + 1) * part - (PLEN - E))
        far_out[0, j, :, :E] = (far_key[prompt, span, :] * SCALE).astype(BF16)
        far_out[0, j, :, E:] = far_value[prompt, span, :].astype(BF16)


def attend_scores(packets, line, stacks, slots, prompts, resp_bits):
    rows, packet_width = packets[0].shape
    group = (packet_width // E - 3) // 2
    operands = [*packets, *line, *stacks]
    low_shape = (len(packets), PLEN + rows, group * rows)
    out_shape = [
        jax.ShapeDtypeStruct(low_shape, BF16),
        jax.ShapeDtypeStruct(low_shape, BF16),
        jax.ShapeDtypeStruct((prompts, PLEN, E), BF16),
        jax.ShapeDtypeStruct((1, *line[0].shape), BF16),
        jax.ShapeDtypeStruct((prompts, E, E), F32),
        jax.ShapeDtypeStruct((prompts, E, E), F32),
    ]
    return pl.pallas_call(
        functools.partial(scores_kernel, slots, group, rows, resp_bits),
        out_shape=out_shape,
        in_specs=[VMEM] * len(operands),
        out_specs=[VMEM] * len(out_shape),
        scratch_shapes=[pltpu.VMEM((prompts, PLEN, E), BF16)],
        compiler_params=params(32),
        cost_estimate=cost(10 * len(packets) * group * rows * (PLEN + rows) * E, 1 << 23),
        name="attend_scores",
    )(*operands)


def prefix_kernel(slots, group, resp_bits, *rest):
    rest = list(rest)
    n = len(MEMBERS)
    packets, rest = rest[:n], rest[n:]
    probs, dscores, far_key, far_value, *outs = rest
    *outs, key_acc, value_acc = outs
    targets = unstack(outs[:-2], outs[-2:])
    blocks, part, _ = targets[0].shape
    start = PLEN - E
    key_acc[...] = jnp.zeros_like(key_acc)
    value_acc[...] = jnp.zeros_like(value_acc)
    for j in range(n):
        view = open_packet(packets[j], group, resp_bits)
        key_part = dot(dscores[j, :start, :], view["query_pair"], 1, 0)
        value_part = dot(probs[j, :start, :], view["grad_pair"], 1, 0)
        for total, part_sum in ((key_acc, key_part), (value_acc, value_part)):
            total[view["first_at"]] += part_sum[:, :E]
            total[view["second_at"]] += part_sum[:, E:]
    for index, target in enumerate(targets):
        for j in range(blocks):
            prompt, slot = slots[index][j]
            at = slot * part
            key_sum, value_sum = (key_acc, value_acc) if at < start else (far_key, far_value)
            at = at if at < start else at - start
            target[j, :, :E] = (key_sum[prompt, at : at + part, :] * SCALE).astype(target.dtype)
            target[j, :, E:] = value_sum[prompt, at : at + part, :].astype(target.dtype)


def attend_prefix(packets, probs, dscores, far_key, far_value, slots, shape, resp_bits):
    rows, packet_width = packets[0].shape
    group = (packet_width // E - 3) // 2
    prompts = far_key.shape[0]
    count = len(slots) // 2
    out_shape = [jax.ShapeDtypeStruct(shape, F32)] * count
    out_shape += [jax.ShapeDtypeStruct((k, *shape), BF16) for k in (1, count - 2)]
    operands = [*packets, probs, dscores, far_key, far_value]
    outs = pl.pallas_call(
        functools.partial(prefix_kernel, slots, group, resp_bits),
        out_shape=out_shape,
        in_specs=[VMEM] * len(operands),
        out_specs=[VMEM] * len(out_shape),
        scratch_shapes=[pltpu.VMEM((prompts, PLEN - E, E), F32)] * 2,
        compiler_params=params(32),
        cost_estimate=cost(6 * len(packets) * group * rows * PLEN * E, 1 << 22),
        name="attend_prefix",
    )(*operands)
    return outs[:-2], outs[-2], outs[-1]


def rows_kernel(group, resp_bits, *rest):
    n = len(MEMBERS)
    packets, (probs, dscores, keys), outs = rest[:n], rest[n : n + 3], rest[n + 3 :]
    rows = packets[0].shape[0]
    lane_row = lax.broadcasted_iota(jnp.int32, (E, group * rows), 1) & (rows - 1)
    for j, (packet, out) in enumerate(zip(packets, outs)):
        view = open_packet(packet, group, resp_bits)
        key_pair = jnp.concatenate([keys[view["first_at"]], keys[view["second_at"]]], axis=1)
        own_dscores = dscores[j, PLEN:, :]
        both = dot(key_pair, dscores[j, :PLEN, :], 0, 0)
        whole = jnp.where(lane_row < view["boundary"], both[:E], both[E:])
        whole = (whole + dot(view["own_k"], own_dscores, 0, 0)) * SCALE
        for h in range(group):
            out[:, h * E : (h + 1) * E] = whole[:, h * rows : (h + 1) * rows].T.astype(BF16)
        key_grad = dot(own_dscores, view["query"], 1, 0) * SCALE
        out[:, group * E : (group + 1) * E] = key_grad.astype(BF16)
        out[:, (group + 1) * E :] = dot(probs[j, PLEN:, :], view["grad"], 1, 0).astype(BF16)


def attend_rows(packets, probs, dscores, keys, resp_bits):
    rows, packet_width = packets[0].shape
    group = (packet_width // E - 3) // 2
    operands = [*packets, probs, dscores, keys]
    return pl.pallas_call(
        functools.partial(rows_kernel, group, resp_bits),
        out_shape=[jax.ShapeDtypeStruct((rows, (group + 2) * E), BF16)] * len(packets),
        in_specs=[VMEM] * len(operands),
        out_specs=[VMEM] * len(packets),
        compiler_params=params(32),
        cost_estimate=cost(6 * len(packets) * group * rows * PLEN * E, 1 << 22),
        name="attend_rows",
    )(*operands)


def add_kernel(keep_ref, *rest):
    result = keep_ref[...]
    for part in rest[:-1]:
        result = result + part[...].astype(F32)
    rest[-1][...] = result


def add(keep, parts):
    return pl.pallas_call(
        add_kernel,
        out_shape=jax.ShapeDtypeStruct(keep.shape, F32),
        in_specs=[VMEM] * (1 + len(parts)),
        out_specs=VMEM,
        compiler_params=params(16),
        cost_estimate=cost(keep.size, 8 * keep.size),
        name="add_far_grads",
    )(keep, *parts)


def total_kernel(keep_ref, *rest):
    parts, outs = rest[: -len(MEMBERS)], rest[-len(MEMBERS) :]
    for j, out in enumerate(outs):
        result = keep_ref[j]
        for part in parts:
            result = result + part[j].astype(F32)
        out[...] = result.astype(BF16)


def total(keep, parts):
    return pl.pallas_call(
        total_kernel,
        out_shape=[jax.ShapeDtypeStruct(keep.shape[1:], BF16)] * len(MEMBERS),
        in_specs=[VMEM] * (1 + len(parts)),
        out_specs=[VMEM] * len(MEMBERS),
        compiler_params=params(16),
        cost_estimate=cost(0, 1 << 25),
        name="total_prefix_grads",
    )(keep, *parts)


def prompt_kernel(chunk, members, first, *rest):
    rest = list(rest)
    shares = [rest.pop(0) for _ in members]
    kw_ref, vw_ref = rest.pop(0), rest.pop(0)
    start_ref = None if first else rest.pop(0)
    out_ref, *scratch = rest
    heads, _, _ = place()
    key_grad, value_grad = (
        jnp.concatenate([share[:, at : at + E] for share in shares], axis=1) for at in (0, E)
    )
    copies = []
    for index in range(kw_ref.shape[0] // chunk):
        span = slice(index * chunk, (index + 1) * chunk)
        key_part, value_part = (
            jnp.concatenate([weight[span, lanes(heads[j], E)] for j in members], axis=1)
            for weight in (kw_ref, vw_ref)
        )
        turned = dot(key_part, key_grad, 1, 1) + dot(value_part, value_grad, 1, 1)
        if first:
            out_ref[span, :] = turned
            continue
        out, sems = scratch
        out[:, span] = (turned + start_ref[span, :]).T.astype(BF16)
        copies.append(pltpu.make_async_copy(out.at[:, span], out_ref.at[:, span], sems.at[index]))
        copies[-1].start()
    for copy in copies:
        copy.wait()


def prompt_gradient(members, shares, key_weight, value_weight, start=None, chunk=1024):
    first = start is None
    rows = shares[0].shape[0]
    depth, width = key_weight.shape
    operands = [*shares, key_weight, value_weight] + ([] if first else [start])
    out = jax.ShapeDtypeStruct((depth, rows), F32)
    if not first:
        out = jax.ShapeDtypeStruct((rows, depth), BF16)
    return pl.pallas_call(
        functools.partial(prompt_kernel, chunk, members, first),
        out_shape=out,
        in_specs=[VMEM] * len(operands),
        out_specs=VMEM if first else ANY,
        scratch_shapes=[]
        if first
        else [pltpu.VMEM((rows, depth), BF16), pltpu.SemaphoreType.DMA((depth // chunk,))],
        compiler_params=params(24),
        cost_estimate=cost(2 * rows * depth * width, 2 * depth * width + 2 * rows * depth),
        name="prompt_gradient",
    )(*operands)


def per_device(
    n_prompt,
    n_resp,
    prompt_rows,
    key_weight,
    value_weight,
    queries,
    own_keys,
    own_values,
    out_grad,
    first_length,
    resp_prompt,
):
    devices = n_prompt * n_resp
    every_bit = range(devices.bit_length() - 1)
    line_bits = [bit for bit in GATHER_BITS if bit in every_bit]
    line_bits += [bit for bit in every_bit if bit not in (CORE, X, Y, *line_bits)]
    part = prompt_rows.shape[0]

    def fetch(x, offset):
        pairs = [(i ^ crossed(offset, i >> CORE & 1), i) for i in range(devices)]
        return lax.ppermute(x, ("prompt", "resp"), pairs)

    def give(x, offset):
        pairs = [(i, i ^ crossed(offset, i >> CORE & 1)) for i in range(devices)]
        return lax.ppermute(x, ("prompt", "resp"), pairs)

    other_rows = fetch(prompt_rows, MEMBERS[1])
    first, weights = project(prompt_rows, key_weight, value_weight)
    keep, send = project_other(other_rows, weights, first)
    send, queries = lax.optimization_barrier((send, queries))
    packed = pack(first_length, resp_prompt, queries, out_grad, own_keys, own_values)
    arriving = fetch(send, MEMBERS[2])
    joined = jnp.concatenate([keep, arriving]).reshape(len(MEMBERS), part, -1)
    joined, packed = lax.optimization_barrier((joined, packed))
    packets = [packed[0]] + [fetch(packed[j], MEMBERS[j]) for j in range(1, len(MEMBERS))]

    pieces = {0: joined}
    for bit in line_bits:
        for offset in list(pieces):
            pieces[offset | 1 << bit] = fetch(pieces[offset], 1 << bit)
            if len(pieces) == 2:
                pieces[1 << bit], packets[2] = lax.optimization_barrier(
                    (pieces[1 << bit], packets[2])
                )
    offsets = list(pieces)
    stacks = [
        jnp.stack([pieces[offset] for offset in some]) for some in (offsets[:-1], offsets[-1:])
    ]
    stacks[1], packets = lax.optimization_barrier((stacks[1], packets))
    stacks = [fetch(x, 1 << Y) for x in stacks]

    filled = [0] * n_prompt
    slots = []
    for offset in offsets + [offset | 1 << Y for offset in offsets]:
        places = []
        for member in MEMBERS:
            at = (offset ^ member) // n_resp
            places.append((at, filled[at]))
            filled[at] += 1
        slots.append(tuple(places))
    resp_bits = n_resp.bit_length() - 1
    line = list(pieces.values())
    slots = tuple(slots)
    probs, dscores, keys, far, far_key, far_value = attend_scores(
        packets, line, stacks, slots, n_prompt, resp_bits
    )
    far = give(far, 1 << Y)
    sums, near, middle = attend_prefix(
        packets, probs, dscores, far_key, far_value, slots, line[0].shape, resp_bits
    )
    sums = dict(zip(offsets, sums))
    middle = give(middle, 1 << Y)
    far, dscores = lax.optimization_barrier((far, dscores))
    grads = attend_rows(packets, probs, dscores, keys, resp_bits)
    own, near = lax.optimization_barrier((grads[0], near))
    near = give(near, 1 << Y)[0]
    back = [own, None, give(grads[2], MEMBERS[2]), None]
    arrived = {offset: [middle[index]] for index, offset in enumerate(offsets[1:-1])}
    arrived.update({offsets[0]: [], offsets[-1]: [far[0]]})
    line_ahead = offsets[-1] ^ 1 << line_bits[-1]
    for bit in reversed(line_bits):
        for offset in sorted(sums, reverse=True):
            if offset & 1 << bit:
                piece = sums.pop(offset)
                for x in arrived.pop(offset):
                    piece = piece + x.astype(F32)
                if offset == 1 << bit and bit == line_bits[-1]:
                    ahead = arrived[line_ahead]
                    piece, ahead[-1], later = lax.optimization_barrier(
                        (piece, ahead[-1], [grads[1], grads[3]])
                    )
                    back[1], back[3] = give(later[0], MEMBERS[1]), give(later[1], MEMBERS[3])
                arrived[offset ^ 1 << bit].append(give(piece.astype(BF16), 1 << bit))
    unpacked = unpack(back, queries.shape[1], own_keys.shape[1])
    sums[0], unpacked = lax.optimization_barrier((sums[0], unpacked))
    query_grad, key_grad, value_grad = unpacked
    blocks = total(add(sums[0], arrived[0]), [near])
    shares = [blocks[0]] + [give(blocks[j], MEMBERS[j]) for j in range(1, len(MEMBERS))]
    start = prompt_gradient((0, 1), shares[:2], key_weight, value_weight)
    prompt_grad = prompt_gradient((2, 3), shares[2:], key_weight, value_weight, start)
    return (query_grad, key_grad, value_grad, prompt_grad)


def solution(mesh):
    both = P(("prompt", "resp"), None)
    return jax.shard_map(
        functools.partial(per_device, mesh.shape["prompt"], mesh.shape["resp"]),
        mesh=mesh,
        in_specs=(both, P(), P(), both, both, both, both, P(("prompt", "resp")), both),
        out_specs=(both, both, both, both),
        check_vma=False,
    )
```

```python
import functools
import math

import jax
import jax.numpy as jnp
from jax import lax
from jax.experimental import pallas as pl
from jax.experimental.pallas import tpu as pltpu
from jax.sharding import PartitionSpec as P

E = 128
PLEN = 512
SCALE = E ** (-0.5)
EXP2_SCALE = SCALE * math.log2(math.e)
HIDDEN = -1e30
BF16 = jnp.bfloat16
F32 = jnp.float32
NOTE_ROWS, NOTE_LANES = 16, 32
CORE, X, Y = 0, 3, 4
GATHER_BITS = (2, 1)
MEMBERS = (0, 1 << CORE, 1 << X, 1 << X | 1 << CORE)

SMEM = pl.BlockSpec(memory_space=pltpu.SMEM)
ANY = pl.BlockSpec(memory_space=pl.ANY)
VMEM = pl.BlockSpec(memory_space=pltpu.VMEM)


def params(mebibytes=40):
    return pltpu.CompilerParams(vmem_limit_bytes=mebibytes * 1024 * 1024)


def cost(flops, bytes_accessed, transcendentals=0):
    return pl.CostEstimate(
        flops=int(flops), bytes_accessed=int(bytes_accessed), transcendentals=int(transcendentals)
    )


def lanes(index, width):
    return pl.ds(pl.multiple_of(index * width, 128), width)


def dot(a, b, a_dim, b_dim):
    return lax.dot_general(a, b, (((a_dim,), (b_dim,)), ((), ())), preferred_element_type=F32)


def crossed(offset, core):
    change = ((offset >> X) ^ (offset >> Y)) & core
    return offset ^ (change << X | change << Y)


def place():
    prompt = lax.axis_index("prompt")
    device = prompt * lax.axis_size("resp") + lax.axis_index("resp")
    core, x, y = ((device >> bit) & 1 for bit in (CORE, X, Y))
    own, other = jnp.where(core == 0, x, 2 + y), jnp.where(core == 0, 2 + y, x)
    return (own, other, own ^ 1, other ^ 1), core, prompt


def project_kernel(steps, x_ref, kw_ref, vw_ref, out_ref, weights, sems):
    _, core, _ = place()
    width = weights.shape[1] // 2
    chunk = weights.shape[0] // steps
    copies = []
    for step in range(steps):
        span = slice(step * chunk, (step + 1) * chunk)
        for index, source in enumerate((kw_ref, vw_ref)):
            copies.append(
                pltpu.make_async_copy(
                    source.at[span, lanes(core, width)],
                    weights.at[span, index * width : (index + 1) * width],
                    sems.at[len(copies)],
                )
            )
    for copy in copies[:8]:
        copy.start()
    total = None
    for step in range(steps):
        span = slice(step * chunk, (step + 1) * chunk)
        copies[2 * step].wait()
        copies[2 * step + 1].wait()
        for copy in copies[2 * step + 8 : 2 * step + 10]:
            copy.start()
        product = dot(x_ref[:, span], weights[span, :], 1, 0)
        total = product if step == 0 else total + product
    out_ref[...] = total.astype(BF16)


def project(prompt_rows, key_weight, value_weight, steps=10):
    rows = prompt_rows.shape[0]
    depth, width = key_weight.shape
    return pl.pallas_call(
        functools.partial(project_kernel, steps),
        out_shape=[
            jax.ShapeDtypeStruct((rows, width), BF16),
            jax.ShapeDtypeStruct((depth, width), BF16),
        ],
        in_specs=[VMEM, ANY, ANY],
        out_specs=[VMEM] * 2,
        scratch_shapes=[pltpu.SemaphoreType.DMA((2 * steps,))],
        compiler_params=params(44),
        cost_estimate=cost(2 * rows * depth * width, 2 * depth * width + 2 * rows * depth),
        name="project_own",
    )(prompt_rows, key_weight, value_weight)


def project_other_kernel(x_ref, weights, first_ref, keep_ref, send_ref, second_ref):
    heads, _, _ = place()
    second_ref[...] = dot(x_ref[...], weights[...], 1, 0).astype(BF16)
    part = x_ref.shape[0]
    for out, head in ((keep_ref, heads[0] & 1), (send_ref, heads[2] & 1)):
        for index, source in enumerate((first_ref, second_ref)):
            span = slice(index * part, (index + 1) * part)
            out[span, :E] = source[:, lanes(head, E)]
            out[span, E:] = source[:, lanes(head + 2, E)]


def project_other(other_rows, weights, first):
    rows, depth = other_rows.shape
    return pl.pallas_call(
        project_other_kernel,
        out_shape=[jax.ShapeDtypeStruct((2 * rows, 2 * E), BF16)] * 2,
        in_specs=[VMEM] * 3,
        out_specs=[VMEM] * 2,
        scratch_shapes=[pltpu.VMEM(first.shape, BF16)],
        compiler_params=params(16),
        cost_estimate=cost(2 * rows * depth * first.shape[1], 2 * weights.size),
        name="project_other",
    )(other_rows, weights, first)


def pack_kernel(length_ref, prompts_ref, q_ref, g_ref, k_ref, v_ref, *outs):
    heads, _, _ = place()
    lane = lax.broadcasted_iota(jnp.int32, (NOTE_ROWS, E), 1)
    note = jnp.where(
        lane < NOTE_LANES,
        length_ref[0],
        jnp.where(lane < 2 * NOTE_LANES, prompts_ref[0, 0], prompts_ref[0, 1]),
    )
    note = note.astype(F32).astype(BF16)
    rows = q_ref.shape[0]
    for head, out in zip(heads, outs):
        start = 0
        for source in (q_ref, g_ref, k_ref, v_ref):
            width = source.shape[1] // len(outs)
            part = source[:, lanes(head, width)]
            for at in range(0, width, E):
                out[start : start + rows, :] = part[:, at : at + E]
                start += rows
        out[start:, :] = note


def pack(first_length, resp_prompt, queries, out_grad, own_keys, own_values):
    rows = queries.shape[0]
    n = len(MEMBERS)
    width = (2 * queries.shape[1] + 2 * own_keys.shape[1]) // n
    packet = (rows * width // E + NOTE_ROWS, E)
    return pl.pallas_call(
        pack_kernel,
        out_shape=[jax.ShapeDtypeStruct(packet, BF16)] * n,
        in_specs=[SMEM] * 2 + [VMEM] * 4,
        out_specs=[VMEM] * n,
        compiler_params=params(16),
        cost_estimate=cost(0, 4 * n * rows * width),
        name="pack_rows",
    )(first_length, resp_prompt, queries, out_grad, own_keys, own_values)


def unpack_kernel(n, *rest):
    packets, targets = rest[:n], rest[n:]
    heads, _, _ = place()
    for head, packet in zip(heads, packets):
        start = 0
        for target in targets:
            width = target.shape[1] // n
            target[:, lanes(head, width)] = packet[:, start : start + width]
            start += width


def unpack(packets, q_width, kv_width):
    n = len(packets)
    rows = packets[0].shape[0]
    return pl.pallas_call(
        functools.partial(unpack_kernel, n),
        out_shape=[
            jax.ShapeDtypeStruct((rows, width), BF16) for width in (q_width, kv_width, kv_width)
        ],
        in_specs=[VMEM] * n,
        out_specs=[VMEM] * 3,
        compiler_params=params(16),
        cost_estimate=cost(0, 4 * rows * (q_width + 2 * kv_width)),
        name="unpack_rows",
    )(*packets)


def attend_kernel(slots, group, rows, resp_bits, *rest):
    rest = list(rest)

    def take(count):
        taken = rest[:count]
        del rest[:count]
        return taken

    def unstack(near, stacks):
        return near + [stack.at[index] for stack in stacks for index in range(stack.shape[0])]

    pieces = len(slots)
    n = len(MEMBERS)
    packets = take(n)
    kv_in = unstack(take(pieces // 2), take(2))
    grads_out = take(n)
    prefix_out = unstack(take(pieces // 2), take(3))
    keys, values, key_acc, value_acc = rest
    blocks, part, _ = kv_in[0].shape
    _, core, prompt_place = place()

    for index in range(pieces):
        for j in range(blocks):
            prompt, slot = slots[index][j]
            span = slice(slot * part, (slot + 1) * part)
            keys[prompt, span, :] = kv_in[index][j, :, :E]
            values[prompt, span, :] = kv_in[index][j, :, E:]
    key_acc[...] = jnp.zeros_like(key_acc)
    value_acc[...] = jnp.zeros_like(value_acc)

    total_rows = group * rows
    row_in_column = lax.broadcasted_iota(jnp.int32, (total_rows, E), 0) & (rows - 1)
    row_in_lane = lax.broadcasted_iota(jnp.int32, (rows, total_rows), 1) & (rows - 1)
    own_key = lax.broadcasted_iota(jnp.int32, (rows, total_rows), 0)
    lane_row = lax.broadcasted_iota(jnp.int32, (E, total_rows), 1) & (rows - 1)

    def products(j):
        packet = packets[j]
        note = packet[(2 * group + 2) * rows :, :].astype(F32)
        slot = lax.broadcasted_iota(jnp.int32, note.shape, 1) // NOTE_LANES
        boundary, first_at, second_at = (
            jnp.max(jnp.where(slot == index, note, 0.0)).astype(jnp.int32) for index in range(3)
        )
        first_at, second_at = (
            crossed((prompt ^ prompt_place) << resp_bits, core) >> resp_bits
            for prompt in (first_at, second_at)
        )
        query, grad, own_k, own_v = (
            packet[at * rows : end * rows, :]
            for at, end in (
                (0, group),
                (group, 2 * group),
                (2 * group, 2 * group + 1),
                (2 * group + 1, 2 * group + 2),
            )
        )
        in_first = row_in_column < boundary

        def split(x):
            x = x.astype(F32)
            return jnp.concatenate(
                [jnp.where(in_first, x, 0.0), jnp.where(in_first, 0.0, x)], axis=1
            ).astype(BF16)

        query_pair = split(query)
        grad_pair = split(grad)
        key_pair = jnp.concatenate([keys[first_at], keys[second_at]], axis=1)
        value_pair = jnp.concatenate([values[first_at], values[second_at]], axis=1)

        visible = (own_key <= row_in_lane) & ((own_key >= boundary) == (row_in_lane >= boundary))
        return dict(
            boundary=boundary,
            first_at=first_at,
            second_at=second_at,
            query=query,
            grad=grad,
            own_k=own_k,
            query_pair=query_pair,
            grad_pair=grad_pair,
            key_pair=key_pair,
            scores=dot(key_pair, query_pair, 1, 1),
            own_scores=jnp.where(visible, dot(own_k, query, 1, 1), HIDDEN),
            dprobs=dot(value_pair, grad_pair, 1, 1),
            own_dprobs=dot(own_v, grad, 1, 1),
        )

    def soften(scores, own_scores, dprobs, own_dprobs, **_):
        top = jnp.maximum(
            jnp.max(scores, axis=0, keepdims=True), jnp.max(own_scores, axis=0, keepdims=True)
        )
        weight = jnp.exp2((scores - top) * EXP2_SCALE)
        own_weight = jnp.exp2((own_scores - top) * EXP2_SCALE)
        inverse = 1.0 / (
            jnp.sum(weight, axis=0, keepdims=True) + jnp.sum(own_weight, axis=0, keepdims=True)
        )
        probs = weight * inverse
        own_probs = own_weight * inverse
        probs_low = probs.astype(BF16)
        own_probs_low = own_probs.astype(BF16)
        delta = jnp.sum(probs_low.astype(F32) * dprobs, axis=0, keepdims=True) + jnp.sum(
            own_probs_low.astype(F32) * own_dprobs, axis=0, keepdims=True
        )
        return dict(
            probs_low=probs_low,
            own_probs_low=own_probs_low,
            dscores=(probs * (dprobs - delta)).astype(BF16),
            own_dscores=(own_probs * (own_dprobs - delta)).astype(BF16),
        )

    def gradients(
        grads, boundary, first_at, second_at, query, grad, own_k, query_pair, grad_pair, key_pair,
        probs_low, own_probs_low, dscores, own_dscores, **_
    ):
        key_part = dot(dscores, query_pair, 1, 0)
        value_part = dot(probs_low, grad_pair, 1, 0)
        key_acc[first_at] += key_part[:, :E]
        key_acc[second_at] += key_part[:, E:]
        value_acc[first_at] += value_part[:, :E]
        value_acc[second_at] += value_part[:, E:]

        query_both = dot(key_pair, dscores, 0, 0)
        query_part = jnp.where(lane_row < boundary, query_both[:E], query_both[E:])
        query_part = (query_part + dot(own_k, own_dscores, 0, 0)) * SCALE
        for h in range(group):
            grads[:, h * E : (h + 1) * E] = query_part[:, h * rows : (h + 1) * rows].T.astype(BF16)
        grads[:, group * E : (group + 1) * E] = (dot(own_dscores, query, 1, 0) * SCALE).astype(BF16)
        grads[:, (group + 1) * E :] = dot(own_probs_low, grad, 1, 0).astype(BF16)

    ahead = products(0)
    for j in range(n):
        now = ahead
        if j + 1 < n:
            ahead = products(j + 1)
        gradients(grads_out[j], **now, **soften(**now))

    for index in range(pieces):
        for j in range(blocks):
            prompt, slot = slots[index][j]
            span = slice(slot * part, (slot + 1) * part)
            target = prefix_out[index]
            target[j, :, :E] = (key_acc[prompt, span, :] * SCALE).astype(target.dtype)
            target[j, :, E:] = value_acc[prompt, span, :].astype(target.dtype)


def attend(packets, rows, line, stacks, slots, prompts, resp_bits):
    group = (packets[0].shape[0] - NOTE_ROWS) // (2 * rows) - 1
    sums_shape = (prompts, PLEN, E)
    out_shape = [jax.ShapeDtypeStruct((rows, (group + 2) * E), BF16)] * len(packets)
    out_shape += [jax.ShapeDtypeStruct(x.shape, F32) for x in line]
    out_shape += [
        jax.ShapeDtypeStruct((count, *line[0].shape), BF16) for count in (1, len(line) - 2, 1)
    ]
    operands = [*packets, *line, *stacks]
    outs = pl.pallas_call(
        functools.partial(attend_kernel, slots, group, rows, resp_bits),
        out_shape=out_shape,
        in_specs=[VMEM] * len(operands),
        out_specs=[VMEM] * len(out_shape),
        scratch_shapes=[pltpu.VMEM(sums_shape, BF16)] * 2 + [pltpu.VMEM(sums_shape, F32)] * 2,
        compiler_params=params(32),
        cost_estimate=cost(
            20 * len(packets) * group * rows * (PLEN + rows) * E, 1 << 24
        ),
        name="attend_head",
    )(*operands)
    return outs[: len(packets)], outs[len(packets) : -3], outs[-3:]


def total_kernel(keep_ref, *rest):
    parts, outs = rest[: -len(MEMBERS)], rest[-len(MEMBERS) :]
    for j, out in enumerate(outs):
        result = keep_ref[j]
        for part in parts:
            result = result + part[j].astype(F32)
        out[...] = result.astype(BF16)


def total(keep, parts):
    return pl.pallas_call(
        total_kernel,
        out_shape=[jax.ShapeDtypeStruct(keep.shape[1:], BF16)] * len(MEMBERS),
        in_specs=[VMEM] * (1 + len(parts)),
        out_specs=[VMEM] * len(MEMBERS),
        compiler_params=params(16),
        cost_estimate=cost(0, 1 << 25),
        name="total_prefix_grads",
    )(keep, *parts)


def prompt_kernel(chunk, members, first, *rest):
    rest = list(rest)
    shares = [rest.pop(0) for _ in members]
    kw_ref, vw_ref = rest.pop(0), rest.pop(0)
    start_ref = None if first else rest.pop(0)
    out_ref, *scratch = rest
    heads, _, _ = place()
    key_grad, value_grad = (
        jnp.concatenate([share[:, at : at + E] for share in shares], axis=1) for at in (0, E)
    )
    copies = []
    for index in range(kw_ref.shape[0] // chunk):
        span = slice(index * chunk, (index + 1) * chunk)
        key_part, value_part = (
            jnp.concatenate([weight[span, lanes(heads[j], E)] for j in members], axis=1)
            for weight in (kw_ref, vw_ref)
        )
        turned = dot(key_part, key_grad, 1, 1) + dot(value_part, value_grad, 1, 1)
        if first:
            out_ref[span, :] = turned
            continue
        out, sems = scratch
        out[:, span] = (turned + start_ref[span, :]).T.astype(BF16)
        copies.append(pltpu.make_async_copy(out.at[:, span], out_ref.at[:, span], sems.at[index]))
        copies[-1].start()
    for copy in copies:
        copy.wait()


def prompt_gradient(members, shares, key_weight, value_weight, start=None, chunk=1024):
    first = start is None
    rows = shares[0].shape[0]
    depth, width = key_weight.shape
    operands = [*shares, key_weight, value_weight] + ([] if first else [start])
    out = jax.ShapeDtypeStruct((depth, rows), F32)
    if not first:
        out = jax.ShapeDtypeStruct((rows, depth), BF16)
    return pl.pallas_call(
        functools.partial(prompt_kernel, chunk, members, first),
        out_shape=out,
        in_specs=[VMEM] * len(operands),
        out_specs=VMEM if first else ANY,
        scratch_shapes=[]
        if first
        else [pltpu.VMEM((rows, depth), BF16), pltpu.SemaphoreType.DMA((depth // chunk,))],
        compiler_params=params(24),
        cost_estimate=cost(2 * rows * depth * width, 2 * depth * width + 2 * rows * depth),
        name="prompt_gradient",
    )(*operands)


def per_device(
    n_prompt,
    n_resp,
    prompt_rows,
    key_weight,
    value_weight,
    queries,
    own_keys,
    own_values,
    out_grad,
    first_length,
    resp_prompt,
):
    devices = n_prompt * n_resp
    every_bit = range(devices.bit_length() - 1)
    line_bits = [bit for bit in GATHER_BITS if bit in every_bit]
    line_bits += [bit for bit in every_bit if bit not in (CORE, X, Y, *line_bits)]
    part = prompt_rows.shape[0]

    def fetch(x, offset):
        pairs = [(i ^ crossed(offset, i >> CORE & 1), i) for i in range(devices)]
        return lax.ppermute(x, ("prompt", "resp"), pairs)

    def give(x, offset):
        pairs = [(i, i ^ crossed(offset, i >> CORE & 1)) for i in range(devices)]
        return lax.ppermute(x, ("prompt", "resp"), pairs)

    other_rows = fetch(prompt_rows, MEMBERS[1])
    first, weights = project(prompt_rows, key_weight, value_weight)
    keep, send = project_other(other_rows, weights, first)
    send, queries = lax.optimization_barrier((send, queries))
    packed = pack(first_length, resp_prompt, queries, out_grad, own_keys, own_values)
    arriving = fetch(send, MEMBERS[2])
    joined = jnp.concatenate([keep, arriving]).reshape(len(MEMBERS), part, -1)
    joined, packed = lax.optimization_barrier((joined, packed))
    packets = [packed[0]] + [fetch(packed[j], MEMBERS[j]) for j in range(1, len(MEMBERS))]

    pieces = {0: joined}
    for bit in line_bits:
        for offset in list(pieces):
            pieces[offset | 1 << bit] = fetch(pieces[offset], 1 << bit)
            if len(pieces) == 2:
                pieces[1 << bit], packets[2] = lax.optimization_barrier(
                    (pieces[1 << bit], packets[2])
                )
    offsets = list(pieces)
    stacks = [
        jnp.stack([pieces[offset] for offset in some]) for some in (offsets[:-1], offsets[-1:])
    ]
    stacks[1], packets = lax.optimization_barrier((stacks[1], packets))
    stacks = [fetch(x, 1 << Y) for x in stacks]

    filled = [0] * n_prompt
    slots = []
    for offset in offsets + [offset | 1 << Y for offset in offsets]:
        places = []
        for member in MEMBERS:
            at = (offset ^ member) // n_resp
            places.append((at, filled[at]))
            filled[at] += 1
        slots.append(tuple(places))
    resp_bits = n_resp.bit_length() - 1
    grads, sums, back_stacks = attend(
        packets, queries.shape[0], list(pieces.values()), stacks, tuple(slots), n_prompt, resp_bits
    )

    sums = dict(zip(offsets, sums))
    far = give(back_stacks[2], 1 << Y)
    middle = give(back_stacks[1], 1 << Y)
    near = give(back_stacks[0], 1 << Y)
    middle, grads = lax.optimization_barrier((middle, grads))
    back = [grads[0]] + [give(grads[j], MEMBERS[j]) for j in range(1, len(MEMBERS))]
    arrived = {offset: [middle[index]] for index, offset in enumerate(offsets[1:-1])}
    arrived.update({offsets[0]: [near[0]], offsets[-1]: [far[0]]})
    line_ahead = offsets[-1] ^ 1 << line_bits[-1]
    for bit in reversed(line_bits):
        for offset in sorted(sums, reverse=True):
            if offset & 1 << bit:
                piece = sums.pop(offset)
                for x in arrived.pop(offset):
                    piece = piece + x.astype(F32)
                if offset == 1 << bit and bit == line_bits[-1]:
                    ahead = arrived[line_ahead]
                    piece, ahead[-1] = lax.optimization_barrier((piece, ahead[-1]))
                arrived[offset ^ 1 << bit].append(give(piece.astype(BF16), 1 << bit))
    unpacked = unpack(back, queries.shape[1], own_keys.shape[1])
    arrived[0], unpacked = lax.optimization_barrier((arrived[0], unpacked))
    query_grad, key_grad, value_grad = unpacked
    blocks = total(sums[0], arrived[0])
    shares = [blocks[0]] + [give(blocks[j], MEMBERS[j]) for j in range(1, len(MEMBERS))]
    start = prompt_gradient((0, 1), shares[:2], key_weight, value_weight)
    prompt_grad = prompt_gradient((2, 3), shares[2:], key_weight, value_weight, start)
    return (query_grad, key_grad, value_grad, prompt_grad)


def solution(mesh):
    both = P(("prompt", "resp"), None)
    return jax.shard_map(
        functools.partial(per_device, mesh.shape["prompt"], mesh.shape["resp"]),
        mesh=mesh,
        in_specs=(both, P(), P(), both, both, both, both, P(("prompt", "resp")), both),
        out_specs=(both, both, both, both),
        check_vma=False,
    )
```

```python
import functools
import math

import jax
import jax.numpy as jnp
from jax import lax
from jax.experimental import pallas as pl
from jax.experimental.pallas import tpu as pltpu
from jax.sharding import PartitionSpec as P

E = 128
PLEN = 512
SCALE = E ** (-0.5)
EXP2_SCALE = SCALE * math.log2(math.e)
HIDDEN = -1e30
BF16 = jnp.bfloat16
F32 = jnp.float32
NOTE_ROWS, NOTE_LANES = 16, 32
CORE, X, Y = 0, 3, 4
GATHER_BITS = (2, 1)
MEMBERS = (0, 1 << CORE, 1 << X, 1 << X | 1 << CORE)

SMEM = pl.BlockSpec(memory_space=pltpu.SMEM)
ANY = pl.BlockSpec(memory_space=pl.ANY)
VMEM = pl.BlockSpec(memory_space=pltpu.VMEM)


def params(mebibytes=40):
    return pltpu.CompilerParams(vmem_limit_bytes=mebibytes * 1024 * 1024)


def cost(flops, bytes_accessed, transcendentals=0):
    return pl.CostEstimate(
        flops=int(flops), bytes_accessed=int(bytes_accessed), transcendentals=int(transcendentals)
    )


def lanes(index, width):
    return pl.ds(pl.multiple_of(index * width, 128), width)


def dot(a, b, a_dim, b_dim):
    return lax.dot_general(a, b, (((a_dim,), (b_dim,)), ((), ())), preferred_element_type=F32)


def crossed(offset, core):
    change = ((offset >> X) ^ (offset >> Y)) & core
    return offset ^ (change << X | change << Y)


def place():
    prompt = lax.axis_index("prompt")
    device = prompt * lax.axis_size("resp") + lax.axis_index("resp")
    core, x, y = ((device >> bit) & 1 for bit in (CORE, X, Y))
    own, other = jnp.where(core == 0, x, 2 + y), jnp.where(core == 0, 2 + y, x)
    return (own, other, own ^ 1, other ^ 1), core, prompt


def project_kernel(steps, x_ref, kw_ref, vw_ref, out_ref, weights, sems):
    _, core, _ = place()
    width = weights.shape[1] // 2
    chunk = weights.shape[0] // steps
    copies = []
    for step in range(steps):
        span = slice(step * chunk, (step + 1) * chunk)
        for index, source in enumerate((kw_ref, vw_ref)):
            copies.append(
                pltpu.make_async_copy(
                    source.at[span, lanes(core, width)],
                    weights.at[span, index * width : (index + 1) * width],
                    sems.at[len(copies)],
                )
            )
    for copy in copies[:12]:
        copy.start()
    total = None
    for step in range(steps):
        span = slice(step * chunk, (step + 1) * chunk)
        copies[2 * step].wait()
        copies[2 * step + 1].wait()
        for copy in copies[2 * step + 12 : 2 * step + 14]:
            copy.start()
        product = dot(x_ref[:, span], weights[span, :], 1, 0)
        total = product if step == 0 else total + product
    out_ref[...] = total.astype(BF16)


def project(prompt_rows, key_weight, value_weight, steps=10):
    rows = prompt_rows.shape[0]
    depth, width = key_weight.shape
    return pl.pallas_call(
        functools.partial(project_kernel, steps),
        out_shape=[
            jax.ShapeDtypeStruct((rows, width), BF16),
            jax.ShapeDtypeStruct((depth, width), BF16),
        ],
        in_specs=[VMEM, ANY, ANY],
        out_specs=[VMEM] * 2,
        scratch_shapes=[pltpu.SemaphoreType.DMA((2 * steps,))],
        compiler_params=params(44),
        cost_estimate=cost(2 * rows * depth * width, 2 * depth * width + 2 * rows * depth),
        name="project_own",
    )(prompt_rows, key_weight, value_weight)


def project_other_kernel(x_ref, weights, first_ref, keep_ref, send_ref, second_ref):
    heads, _, _ = place()
    second_ref[...] = dot(x_ref[...], weights[...], 1, 0).astype(BF16)
    part = x_ref.shape[0]
    for out, head in ((keep_ref, heads[0] & 1), (send_ref, heads[2] & 1)):
        for index, source in enumerate((first_ref, second_ref)):
            span = slice(index * part, (index + 1) * part)
            out[span, :E] = source[:, lanes(head, E)]
            out[span, E:] = source[:, lanes(head + 2, E)]


def project_other(other_rows, weights, first):
    rows, depth = other_rows.shape
    return pl.pallas_call(
        project_other_kernel,
        out_shape=[jax.ShapeDtypeStruct((2 * rows, 2 * E), BF16)] * 2,
        in_specs=[VMEM] * 3,
        out_specs=[VMEM] * 2,
        scratch_shapes=[pltpu.VMEM(first.shape, BF16)],
        compiler_params=params(16),
        cost_estimate=cost(2 * rows * depth * first.shape[1], 2 * weights.size),
        name="project_other",
    )(other_rows, weights, first)


def pack_kernel(length_ref, prompts_ref, q_ref, g_ref, k_ref, v_ref, *outs):
    heads, _, _ = place()
    lane = lax.broadcasted_iota(jnp.int32, (NOTE_ROWS, E), 1)
    note = jnp.where(
        lane < NOTE_LANES,
        length_ref[0],
        jnp.where(lane < 2 * NOTE_LANES, prompts_ref[0, 0], prompts_ref[0, 1]),
    )
    note = note.astype(F32).astype(BF16)
    rows = q_ref.shape[0]
    for head, out in zip(heads, outs):
        start = 0
        for source in (q_ref, g_ref, k_ref, v_ref):
            width = source.shape[1] // len(outs)
            part = source[:, lanes(head, width)]
            for at in range(0, width, E):
                out[start : start + rows, :] = part[:, at : at + E]
                start += rows
        out[start:, :] = note


def pack(first_length, resp_prompt, queries, out_grad, own_keys, own_values):
    rows = queries.shape[0]
    n = len(MEMBERS)
    width = (2 * queries.shape[1] + 2 * own_keys.shape[1]) // n
    packet = (rows * width // E + NOTE_ROWS, E)
    return pl.pallas_call(
        pack_kernel,
        out_shape=[jax.ShapeDtypeStruct(packet, BF16)] * n,
        in_specs=[SMEM] * 2 + [VMEM] * 4,
        out_specs=[VMEM] * n,
        compiler_params=params(16),
        cost_estimate=cost(0, 4 * n * rows * width),
        name="pack_rows",
    )(first_length, resp_prompt, queries, out_grad, own_keys, own_values)


def unpack_kernel(n, *rest):
    packets, targets = rest[:n], rest[n:]
    heads, _, _ = place()
    for head, packet in zip(heads, packets):
        start = 0
        for target in targets:
            width = target.shape[1] // n
            target[:, lanes(head, width)] = packet[:, start : start + width]
            start += width


def unpack(packets, q_width, kv_width):
    n = len(packets)
    rows = packets[0].shape[0]
    return pl.pallas_call(
        functools.partial(unpack_kernel, n),
        out_shape=[
            jax.ShapeDtypeStruct((rows, width), BF16) for width in (q_width, kv_width, kv_width)
        ],
        in_specs=[VMEM] * n,
        out_specs=[VMEM] * 3,
        compiler_params=params(16),
        cost_estimate=cost(0, 4 * rows * (q_width + 2 * kv_width)),
        name="unpack_rows",
    )(*packets)


def attend_kernel(slots, group, rows, resp_bits, *rest):
    rest = list(rest)

    def take(count):
        taken = rest[:count]
        del rest[:count]
        return taken

    def unstack(near, stacks):
        return near + [stack.at[index] for stack in stacks for index in range(stack.shape[0])]

    pieces = len(slots)
    n = len(MEMBERS)
    packets = take(n)
    kv_in = unstack(take(pieces // 2), take(2))
    grads_out = take(n)
    prefix_out = unstack(take(pieces // 2), take(3))
    keys, values, key_acc, value_acc = rest
    blocks, part, _ = kv_in[0].shape
    _, core, prompt_place = place()

    for index in range(pieces):
        for j in range(blocks):
            prompt, slot = slots[index][j]
            span = slice(slot * part, (slot + 1) * part)
            keys[prompt, span, :] = kv_in[index][j, :, :E]
            values[prompt, span, :] = kv_in[index][j, :, E:]
    key_acc[...] = jnp.zeros_like(key_acc)
    value_acc[...] = jnp.zeros_like(value_acc)

    total_rows = group * rows
    row_in_column = lax.broadcasted_iota(jnp.int32, (total_rows, E), 0) & (rows - 1)
    row_in_lane = lax.broadcasted_iota(jnp.int32, (rows, total_rows), 1) & (rows - 1)
    own_key = lax.broadcasted_iota(jnp.int32, (rows, total_rows), 0)
    lane_row = lax.broadcasted_iota(jnp.int32, (E, total_rows), 1) & (rows - 1)

    def products(j):
        packet = packets[j]
        note = packet[(2 * group + 2) * rows :, :].astype(F32)
        slot = lax.broadcasted_iota(jnp.int32, note.shape, 1) // NOTE_LANES
        boundary, first_at, second_at = (
            jnp.max(jnp.where(slot == index, note, 0.0)).astype(jnp.int32) for index in range(3)
        )
        first_at, second_at = (
            crossed((prompt ^ prompt_place) << resp_bits, core) >> resp_bits
            for prompt in (first_at, second_at)
        )
        query, grad, own_k, own_v = (
            packet[at * rows : end * rows, :]
            for at, end in (
                (0, group),
                (group, 2 * group),
                (2 * group, 2 * group + 1),
                (2 * group + 1, 2 * group + 2),
            )
        )
        in_first = row_in_column < boundary

        def split(x):
            x = x.astype(F32)
            return jnp.concatenate(
                [jnp.where(in_first, x, 0.0), jnp.where(in_first, 0.0, x)], axis=1
            ).astype(BF16)

        query_pair = split(query)
        grad_pair = split(grad)
        key_pair = jnp.concatenate([keys[first_at], keys[second_at]], axis=1)
        value_pair = jnp.concatenate([values[first_at], values[second_at]], axis=1)

        visible = (own_key <= row_in_lane) & ((own_key >= boundary) == (row_in_lane >= boundary))
        return dict(
            boundary=boundary,
            first_at=first_at,
            second_at=second_at,
            query=query,
            grad=grad,
            own_k=own_k,
            query_pair=query_pair,
            grad_pair=grad_pair,
            key_pair=key_pair,
            scores=dot(key_pair, query_pair, 1, 1),
            own_scores=jnp.where(visible, dot(own_k, query, 1, 1), HIDDEN),
            dprobs=dot(value_pair, grad_pair, 1, 1),
            own_dprobs=dot(own_v, grad, 1, 1),
        )

    def soften(scores, own_scores, dprobs, own_dprobs, **_):
        top = jnp.maximum(
            jnp.max(scores, axis=0, keepdims=True), jnp.max(own_scores, axis=0, keepdims=True)
        )
        weight = jnp.exp2((scores - top) * EXP2_SCALE)
        own_weight = jnp.exp2((own_scores - top) * EXP2_SCALE)
        inverse = 1.0 / (
            jnp.sum(weight, axis=0, keepdims=True) + jnp.sum(own_weight, axis=0, keepdims=True)
        )
        probs = weight * inverse
        own_probs = own_weight * inverse
        probs_low = probs.astype(BF16)
        own_probs_low = own_probs.astype(BF16)
        delta = jnp.sum(probs_low.astype(F32) * dprobs, axis=0, keepdims=True) + jnp.sum(
            own_probs_low.astype(F32) * own_dprobs, axis=0, keepdims=True
        )
        return dict(
            probs_low=probs_low,
            own_probs_low=own_probs_low,
            dscores=(probs * (dprobs - delta)).astype(BF16),
            own_dscores=(own_probs * (own_dprobs - delta)).astype(BF16),
        )

    def gradients(
        grads, boundary, first_at, second_at, query, grad, own_k, query_pair, grad_pair, key_pair,
        probs_low, own_probs_low, dscores, own_dscores, **_
    ):
        key_part = dot(dscores, query_pair, 1, 0)
        value_part = dot(probs_low, grad_pair, 1, 0)
        key_acc[first_at] += key_part[:, :E]
        key_acc[second_at] += key_part[:, E:]
        value_acc[first_at] += value_part[:, :E]
        value_acc[second_at] += value_part[:, E:]

        query_both = dot(key_pair, dscores, 0, 0)
        query_part = jnp.where(lane_row < boundary, query_both[:E], query_both[E:])
        query_part = (query_part + dot(own_k, own_dscores, 0, 0)) * SCALE
        for h in range(group):
            grads[:, h * E : (h + 1) * E] = query_part[:, h * rows : (h + 1) * rows].T.astype(BF16)
        grads[:, group * E : (group + 1) * E] = (dot(own_dscores, query, 1, 0) * SCALE).astype(BF16)
        grads[:, (group + 1) * E :] = dot(own_probs_low, grad, 1, 0).astype(BF16)

    ahead = products(0)
    for j in range(n):
        now = ahead
        if j + 1 < n:
            ahead = products(j + 1)
        gradients(grads_out[j], **now, **soften(**now))

    for index in range(pieces):
        for j in range(blocks):
            prompt, slot = slots[index][j]
            span = slice(slot * part, (slot + 1) * part)
            target = prefix_out[index]
            target[j, :, :E] = (key_acc[prompt, span, :] * SCALE).astype(target.dtype)
            target[j, :, E:] = value_acc[prompt, span, :].astype(target.dtype)


def attend(packets, rows, line, stacks, slots, prompts, resp_bits):
    group = (packets[0].shape[0] - NOTE_ROWS) // (2 * rows) - 1
    sums_shape = (prompts, PLEN, E)
    out_shape = [jax.ShapeDtypeStruct((rows, (group + 2) * E), BF16)] * len(packets)
    out_shape += [jax.ShapeDtypeStruct(x.shape, F32) for x in line]
    out_shape += [
        jax.ShapeDtypeStruct((count, *line[0].shape), BF16) for count in (1, len(line) - 2, 1)
    ]
    operands = [*packets, *line, *stacks]
    outs = pl.pallas_call(
        functools.partial(attend_kernel, slots, group, rows, resp_bits),
        out_shape=out_shape,
        in_specs=[VMEM] * len(operands),
        out_specs=[VMEM] * len(out_shape),
        scratch_shapes=[pltpu.VMEM(sums_shape, BF16)] * 2 + [pltpu.VMEM(sums_shape, F32)] * 2,
        compiler_params=params(32),
        cost_estimate=cost(
            20 * len(packets) * group * rows * (PLEN + rows) * E, 1 << 24
        ),
        name="attend_head",
    )(*operands)
    return outs[: len(packets)], outs[len(packets) : -3], outs[-3:]


def total_kernel(keep_ref, *rest):
    parts, outs = rest[: -len(MEMBERS)], rest[-len(MEMBERS) :]
    for j, out in enumerate(outs):
        result = keep_ref[j]
        for part in parts:
            result = result + part[j].astype(F32)
        out[...] = result.astype(BF16)


def total(keep, parts):
    return pl.pallas_call(
        total_kernel,
        out_shape=[jax.ShapeDtypeStruct(keep.shape[1:], BF16)] * len(MEMBERS),
        in_specs=[VMEM] * (1 + len(parts)),
        out_specs=[VMEM] * len(MEMBERS),
        compiler_params=params(16),
        cost_estimate=cost(0, 1 << 25),
        name="total_prefix_grads",
    )(keep, *parts)


def prompt_kernel(chunk, members, first, *rest):
    rest = list(rest)
    shares = [rest.pop(0) for _ in members]
    kw_ref, vw_ref = rest.pop(0), rest.pop(0)
    start_ref = None if first else rest.pop(0)
    out_ref, *scratch = rest
    heads, _, _ = place()
    key_grad, value_grad = (
        jnp.concatenate([share[:, at : at + E] for share in shares], axis=1) for at in (0, E)
    )
    copies = []
    for index in range(kw_ref.shape[0] // chunk):
        span = slice(index * chunk, (index + 1) * chunk)
        key_part, value_part = (
            jnp.concatenate([weight[span, lanes(heads[j], E)] for j in members], axis=1)
            for weight in (kw_ref, vw_ref)
        )
        turned = dot(key_part, key_grad, 1, 1) + dot(value_part, value_grad, 1, 1)
        if first:
            out_ref[span, :] = turned
            continue
        out, sems = scratch
        out[:, span] = (turned + start_ref[span, :]).T.astype(BF16)
        copies.append(pltpu.make_async_copy(out.at[:, span], out_ref.at[:, span], sems.at[index]))
        copies[-1].start()
    for copy in copies:
        copy.wait()


def prompt_gradient(members, shares, key_weight, value_weight, start=None, chunk=1024):
    first = start is None
    rows = shares[0].shape[0]
    depth, width = key_weight.shape
    operands = [*shares, key_weight, value_weight] + ([] if first else [start])
    out = jax.ShapeDtypeStruct((depth, rows), F32)
    if not first:
        out = jax.ShapeDtypeStruct((rows, depth), BF16)
    return pl.pallas_call(
        functools.partial(prompt_kernel, chunk, members, first),
        out_shape=out,
        in_specs=[VMEM] * len(operands),
        out_specs=VMEM if first else ANY,
        scratch_shapes=[]
        if first
        else [pltpu.VMEM((rows, depth), BF16), pltpu.SemaphoreType.DMA((depth // chunk,))],
        compiler_params=params(24),
        cost_estimate=cost(2 * rows * depth * width, 2 * depth * width + 2 * rows * depth),
        name="prompt_gradient",
    )(*operands)


def per_device(
    n_prompt,
    n_resp,
    prompt_rows,
    key_weight,
    value_weight,
    queries,
    own_keys,
    own_values,
    out_grad,
    first_length,
    resp_prompt,
):
    devices = n_prompt * n_resp
    every_bit = range(devices.bit_length() - 1)
    line_bits = [bit for bit in GATHER_BITS if bit in every_bit]
    line_bits += [bit for bit in every_bit if bit not in (CORE, X, Y, *line_bits)]
    part = prompt_rows.shape[0]

    def fetch(x, offset):
        pairs = [(i ^ crossed(offset, i >> CORE & 1), i) for i in range(devices)]
        return lax.ppermute(x, ("prompt", "resp"), pairs)

    def give(x, offset):
        pairs = [(i, i ^ crossed(offset, i >> CORE & 1)) for i in range(devices)]
        return lax.ppermute(x, ("prompt", "resp"), pairs)

    other_rows = fetch(prompt_rows, MEMBERS[1])
    first, weights = project(prompt_rows, key_weight, value_weight)
    keep, send = project_other(other_rows, weights, first)
    send, queries = lax.optimization_barrier((send, queries))
    packed = pack(first_length, resp_prompt, queries, out_grad, own_keys, own_values)
    arriving = fetch(send, MEMBERS[2])
    joined = jnp.concatenate([keep, arriving]).reshape(len(MEMBERS), part, -1)
    joined, packed = lax.optimization_barrier((joined, packed))
    packets = [packed[0]] + [fetch(packed[j], MEMBERS[j]) for j in range(1, len(MEMBERS))]

    pieces = {0: joined}
    for bit in line_bits:
        for offset in list(pieces):
            pieces[offset | 1 << bit] = fetch(pieces[offset], 1 << bit)
            if len(pieces) == 2:
                pieces[1 << bit], packets[2] = lax.optimization_barrier(
                    (pieces[1 << bit], packets[2])
                )
    offsets = list(pieces)
    stacks = [
        jnp.stack([pieces[offset] for offset in some]) for some in (offsets[:-1], offsets[-1:])
    ]
    stacks[1], packets = lax.optimization_barrier((stacks[1], packets))
    stacks = [fetch(x, 1 << Y) for x in stacks]

    filled = [0] * n_prompt
    slots = []
    for offset in offsets + [offset | 1 << Y for offset in offsets]:
        places = []
        for member in MEMBERS:
            at = (offset ^ member) // n_resp
            places.append((at, filled[at]))
            filled[at] += 1
        slots.append(tuple(places))
    resp_bits = n_resp.bit_length() - 1
    grads, sums, back_stacks = attend(
        packets, queries.shape[0], list(pieces.values()), stacks, tuple(slots), n_prompt, resp_bits
    )

    sums = dict(zip(offsets, sums))
    grads = list(grads)
    far = give(back_stacks[2], 1 << Y)
    middle = give(back_stacks[1], 1 << Y)
    near = give(back_stacks[0], 1 << Y)
    far, grads[1] = lax.optimization_barrier((far, grads[1]))
    middle, grads[2:] = lax.optimization_barrier((middle, grads[2:]))
    back = [grads[0]] + [give(grads[j], MEMBERS[j]) for j in range(1, len(MEMBERS))]
    arrived = {offset: [middle[index]] for index, offset in enumerate(offsets[1:-1])}
    arrived.update({offsets[0]: [near[0]], offsets[-1]: [far[0]]})
    line_ahead = offsets[-1] ^ 1 << line_bits[-1]
    for bit in reversed(line_bits):
        for offset in sorted(sums, reverse=True):
            if offset & 1 << bit:
                piece = sums.pop(offset)
                for x in arrived.pop(offset):
                    piece = piece + x.astype(F32)
                if offset == 1 << bit and bit == line_bits[-1]:
                    ahead = arrived[line_ahead]
                    piece, ahead[-1] = lax.optimization_barrier((piece, ahead[-1]))
                arrived[offset ^ 1 << bit].append(give(piece.astype(BF16), 1 << bit))
    unpacked = unpack(back, queries.shape[1], own_keys.shape[1])
    arrived[0], unpacked = lax.optimization_barrier((arrived[0], unpacked))
    query_grad, key_grad, value_grad = unpacked
    blocks = total(sums[0], arrived[0])
    shares = [blocks[0]] + [give(blocks[j], MEMBERS[j]) for j in range(1, len(MEMBERS))]
    start = prompt_gradient((0, 1), shares[:2], key_weight, value_weight)
    prompt_grad = prompt_gradient((2, 3), shares[2:], key_weight, value_weight, start)
    return (query_grad, key_grad, value_grad, prompt_grad)


def solution(mesh):
    both = P(("prompt", "resp"), None)
    return jax.shard_map(
        functools.partial(per_device, mesh.shape["prompt"], mesh.shape["resp"]),
        mesh=mesh,
        in_specs=(both, P(), P(), both, both, both, both, P(("prompt", "resp")), both),
        out_specs=(both, both, both, both),
        check_vma=False,
    )
```

```python
import functools
import math

import jax
import jax.numpy as jnp
from jax import lax
from jax.experimental import pallas as pl
from jax.experimental.pallas import tpu as pltpu
from jax.sharding import PartitionSpec as P

E = 128
PLEN = 512
SCALE = E ** (-0.5)
EXP2_SCALE = SCALE * math.log2(math.e)
HIDDEN = -1e30
BF16 = jnp.bfloat16
F32 = jnp.float32
NOTE_ROWS, NOTE_LANES = 16, 32
CORE, X, Y = 0, 3, 4
GATHER_BITS = (2, 1)
MEMBERS = (0, 1 << CORE, 1 << X, 1 << X | 1 << CORE)

SMEM = pl.BlockSpec(memory_space=pltpu.SMEM)
ANY = pl.BlockSpec(memory_space=pl.ANY)
VMEM = pl.BlockSpec(memory_space=pltpu.VMEM)


def params(mebibytes=40):
    return pltpu.CompilerParams(vmem_limit_bytes=mebibytes * 1024 * 1024)


def cost(flops, bytes_accessed, transcendentals=0):
    return pl.CostEstimate(
        flops=int(flops), bytes_accessed=int(bytes_accessed), transcendentals=int(transcendentals)
    )


def lanes(index, width):
    return pl.ds(pl.multiple_of(index * width, 128), width)


def dot(a, b, a_dim, b_dim):
    return lax.dot_general(a, b, (((a_dim,), (b_dim,)), ((), ())), preferred_element_type=F32)


def crossed(offset, core):
    change = ((offset >> X) ^ (offset >> Y)) & core
    return offset ^ (change << X | change << Y)


def place():
    prompt = lax.axis_index("prompt")
    device = prompt * lax.axis_size("resp") + lax.axis_index("resp")
    core, x, y = ((device >> bit) & 1 for bit in (CORE, X, Y))
    own, other = jnp.where(core == 0, x, 2 + y), jnp.where(core == 0, 2 + y, x)
    return (own, other, own ^ 1, other ^ 1), core, prompt


def project_kernel(steps, x_ref, kw_ref, vw_ref, out_ref, weights, sems):
    _, core, _ = place()
    width = weights.shape[1] // 2
    chunk = weights.shape[0] // steps
    copies = []
    for step in range(steps):
        span = slice(step * chunk, (step + 1) * chunk)
        for index, source in enumerate((kw_ref, vw_ref)):
            copies.append(
                pltpu.make_async_copy(
                    source.at[span, lanes(core, width)],
                    weights.at[span, index * width : (index + 1) * width],
                    sems.at[len(copies)],
                )
            )
    for copy in copies[:12]:
        copy.start()
    total = None
    for step in range(steps):
        span = slice(step * chunk, (step + 1) * chunk)
        copies[2 * step].wait()
        copies[2 * step + 1].wait()
        for copy in copies[2 * step + 12 : 2 * step + 14]:
            copy.start()
        product = dot(x_ref[:, span], weights[span, :], 1, 0)
        total = product if step == 0 else total + product
    out_ref[...] = total.astype(BF16)


def project(prompt_rows, key_weight, value_weight, steps=10):
    rows = prompt_rows.shape[0]
    depth, width = key_weight.shape
    return pl.pallas_call(
        functools.partial(project_kernel, steps),
        out_shape=[
            jax.ShapeDtypeStruct((rows, width), BF16),
            jax.ShapeDtypeStruct((depth, width), BF16),
        ],
        in_specs=[VMEM, ANY, ANY],
        out_specs=[VMEM] * 2,
        scratch_shapes=[pltpu.SemaphoreType.DMA((2 * steps,))],
        compiler_params=params(44),
        cost_estimate=cost(2 * rows * depth * width, 2 * depth * width + 2 * rows * depth),
        name="project_own",
    )(prompt_rows, key_weight, value_weight)


def project_other_kernel(x_ref, weights, first_ref, keep_ref, send_ref, second_ref):
    heads, _, _ = place()
    second_ref[...] = dot(x_ref[...], weights[...], 1, 0).astype(BF16)
    part = x_ref.shape[0]
    for out, head in ((keep_ref, heads[0] & 1), (send_ref, heads[2] & 1)):
        for index, source in enumerate((first_ref, second_ref)):
            span = slice(index * part, (index + 1) * part)
            out[span, :E] = source[:, lanes(head, E)]
            out[span, E:] = source[:, lanes(head + 2, E)]


def project_other(other_rows, weights, first):
    rows, depth = other_rows.shape
    return pl.pallas_call(
        project_other_kernel,
        out_shape=[jax.ShapeDtypeStruct((2 * rows, 2 * E), BF16)] * 2,
        in_specs=[VMEM] * 3,
        out_specs=[VMEM] * 2,
        scratch_shapes=[pltpu.VMEM(first.shape, BF16)],
        compiler_params=params(16),
        cost_estimate=cost(2 * rows * depth * first.shape[1], 2 * weights.size),
        name="project_other",
    )(other_rows, weights, first)


def pack_kernel(length_ref, prompts_ref, q_ref, g_ref, k_ref, v_ref, *outs):
    heads, _, _ = place()
    lane = lax.broadcasted_iota(jnp.int32, (NOTE_ROWS, E), 1)
    note = jnp.where(
        lane < NOTE_LANES,
        length_ref[0],
        jnp.where(lane < 2 * NOTE_LANES, prompts_ref[0, 0], prompts_ref[0, 1]),
    )
    note = note.astype(F32).astype(BF16)
    rows = q_ref.shape[0]
    for head, out in zip(heads, outs):
        start = 0
        for source in (q_ref, g_ref, k_ref, v_ref):
            width = source.shape[1] // len(outs)
            part = source[:, lanes(head, width)]
            for at in range(0, width, E):
                out[start : start + rows, :] = part[:, at : at + E]
                start += rows
        out[start:, :] = note


def pack(first_length, resp_prompt, queries, out_grad, own_keys, own_values):
    rows = queries.shape[0]
    n = len(MEMBERS)
    width = (2 * queries.shape[1] + 2 * own_keys.shape[1]) // n
    packet = (rows * width // E + NOTE_ROWS, E)
    return pl.pallas_call(
        pack_kernel,
        out_shape=[jax.ShapeDtypeStruct(packet, BF16)] * n,
        in_specs=[SMEM] * 2 + [VMEM] * 4,
        out_specs=[VMEM] * n,
        compiler_params=params(16),
        cost_estimate=cost(0, 4 * n * rows * width),
        name="pack_rows",
    )(first_length, resp_prompt, queries, out_grad, own_keys, own_values)


def unpack_kernel(n, *rest):
    packets, targets = rest[:n], rest[n:]
    heads, _, _ = place()
    for head, packet in zip(heads, packets):
        start = 0
        for target in targets:
            width = target.shape[1] // n
            target[:, lanes(head, width)] = packet[:, start : start + width]
            start += width


def unpack(packets, q_width, kv_width):
    n = len(packets)
    rows = packets[0].shape[0]
    return pl.pallas_call(
        functools.partial(unpack_kernel, n),
        out_shape=[
            jax.ShapeDtypeStruct((rows, width), BF16) for width in (q_width, kv_width, kv_width)
        ],
        in_specs=[VMEM] * n,
        out_specs=[VMEM] * 3,
        compiler_params=params(16),
        cost_estimate=cost(0, 4 * rows * (q_width + 2 * kv_width)),
        name="unpack_rows",
    )(*packets)


def attend_kernel(slots, group, rows, resp_bits, *rest):
    rest = list(rest)

    def take(count):
        taken = rest[:count]
        del rest[:count]
        return taken

    def unstack(near, stacks):
        return near + [stack.at[index] for stack in stacks for index in range(stack.shape[0])]

    pieces = len(slots)
    n = len(MEMBERS)
    packets = take(n)
    kv_in = unstack(take(pieces // 2), take(2))
    grads_out = take(n)
    prefix_out = unstack(take(pieces // 2), take(3))
    keys, values, key_acc, value_acc = rest
    blocks, part, _ = kv_in[0].shape
    _, core, prompt_place = place()

    for index in range(pieces):
        for j in range(blocks):
            prompt, slot = slots[index][j]
            span = slice(slot * part, (slot + 1) * part)
            keys[prompt, span, :] = kv_in[index][j, :, :E]
            values[prompt, span, :] = kv_in[index][j, :, E:]
    key_acc[...] = jnp.zeros_like(key_acc)
    value_acc[...] = jnp.zeros_like(value_acc)

    total_rows = group * rows
    row_in_column = lax.broadcasted_iota(jnp.int32, (total_rows, E), 0) & (rows - 1)
    row_in_lane = lax.broadcasted_iota(jnp.int32, (rows, total_rows), 1) & (rows - 1)
    own_key = lax.broadcasted_iota(jnp.int32, (rows, total_rows), 0)
    lane_row = lax.broadcasted_iota(jnp.int32, (E, total_rows), 1) & (rows - 1)

    def products(j):
        packet = packets[j]
        note = packet[(2 * group + 2) * rows :, :].astype(F32)
        slot = lax.broadcasted_iota(jnp.int32, note.shape, 1) // NOTE_LANES
        boundary, first_at, second_at = (
            jnp.max(jnp.where(slot == index, note, 0.0)).astype(jnp.int32) for index in range(3)
        )
        first_at, second_at = (
            crossed((prompt ^ prompt_place) << resp_bits, core) >> resp_bits
            for prompt in (first_at, second_at)
        )
        query, grad, own_k, own_v = (
            packet[at * rows : end * rows, :]
            for at, end in (
                (0, group),
                (group, 2 * group),
                (2 * group, 2 * group + 1),
                (2 * group + 1, 2 * group + 2),
            )
        )
        in_first = row_in_column < boundary

        def split(x):
            x = x.astype(F32)
            return jnp.concatenate(
                [jnp.where(in_first, x, 0.0), jnp.where(in_first, 0.0, x)], axis=1
            ).astype(BF16)

        query_pair = split(query)
        grad_pair = split(grad)
        key_pair = jnp.concatenate([keys[first_at], keys[second_at]], axis=1)
        value_pair = jnp.concatenate([values[first_at], values[second_at]], axis=1)

        visible = (own_key <= row_in_lane) & ((own_key >= boundary) == (row_in_lane >= boundary))
        return dict(
            boundary=boundary,
            first_at=first_at,
            second_at=second_at,
            query=query,
            grad=grad,
            own_k=own_k,
            query_pair=query_pair,
            grad_pair=grad_pair,
            key_pair=key_pair,
            scores=dot(key_pair, query_pair, 1, 1),
            own_scores=jnp.where(visible, dot(own_k, query, 1, 1), HIDDEN),
            dprobs=dot(value_pair, grad_pair, 1, 1),
            own_dprobs=dot(own_v, grad, 1, 1),
        )

    def soften(scores, own_scores, dprobs, own_dprobs, **_):
        top = jnp.maximum(
            jnp.max(scores, axis=0, keepdims=True), jnp.max(own_scores, axis=0, keepdims=True)
        )
        weight = jnp.exp2((scores - top) * EXP2_SCALE)
        own_weight = jnp.exp2((own_scores - top) * EXP2_SCALE)
        inverse = 1.0 / (
            jnp.sum(weight, axis=0, keepdims=True) + jnp.sum(own_weight, axis=0, keepdims=True)
        )
        probs = weight * inverse
        own_probs = own_weight * inverse
        probs_low = probs.astype(BF16)
        own_probs_low = own_probs.astype(BF16)
        delta = jnp.sum(probs_low.astype(F32) * dprobs, axis=0, keepdims=True) + jnp.sum(
            own_probs_low.astype(F32) * own_dprobs, axis=0, keepdims=True
        )
        return dict(
            probs_low=probs_low,
            own_probs_low=own_probs_low,
            dscores=(probs * (dprobs - delta)).astype(BF16),
            own_dscores=(own_probs * (own_dprobs - delta)).astype(BF16),
        )

    def gradients(
        grads, boundary, first_at, second_at, query, grad, own_k, query_pair, grad_pair, key_pair,
        probs_low, own_probs_low, dscores, own_dscores, **_
    ):
        key_part = dot(dscores, query_pair, 1, 0)
        value_part = dot(probs_low, grad_pair, 1, 0)
        key_acc[first_at] += key_part[:, :E]
        key_acc[second_at] += key_part[:, E:]
        value_acc[first_at] += value_part[:, :E]
        value_acc[second_at] += value_part[:, E:]

        query_both = dot(key_pair, dscores, 0, 0)
        query_part = jnp.where(lane_row < boundary, query_both[:E], query_both[E:])
        query_part = (query_part + dot(own_k, own_dscores, 0, 0)) * SCALE
        for h in range(group):
            grads[:, h * E : (h + 1) * E] = query_part[:, h * rows : (h + 1) * rows].T.astype(BF16)
        grads[:, group * E : (group + 1) * E] = (dot(own_dscores, query, 1, 0) * SCALE).astype(BF16)
        grads[:, (group + 1) * E :] = dot(own_probs_low, grad, 1, 0).astype(BF16)

    ahead = products(0)
    for j in range(n):
        now = ahead
        if j + 1 < n:
            ahead = products(j + 1)
        gradients(grads_out[j], **now, **soften(**now))

    for index in range(pieces):
        for j in range(blocks):
            prompt, slot = slots[index][j]
            span = slice(slot * part, (slot + 1) * part)
            target = prefix_out[index]
            target[j, :, :E] = (key_acc[prompt, span, :] * SCALE).astype(target.dtype)
            target[j, :, E:] = value_acc[prompt, span, :].astype(target.dtype)


def attend(packets, rows, line, stacks, slots, prompts, resp_bits):
    group = (packets[0].shape[0] - NOTE_ROWS) // (2 * rows) - 1
    sums_shape = (prompts, PLEN, E)
    out_shape = [jax.ShapeDtypeStruct((rows, (group + 2) * E), BF16)] * len(packets)
    out_shape += [jax.ShapeDtypeStruct(x.shape, F32) for x in line]
    out_shape += [
        jax.ShapeDtypeStruct((count, *line[0].shape), BF16) for count in (1, len(line) - 2, 1)
    ]
    operands = [*packets, *line, *stacks]
    outs = pl.pallas_call(
        functools.partial(attend_kernel, slots, group, rows, resp_bits),
        out_shape=out_shape,
        in_specs=[VMEM] * len(operands),
        out_specs=[VMEM] * len(out_shape),
        scratch_shapes=[pltpu.VMEM(sums_shape, BF16)] * 2 + [pltpu.VMEM(sums_shape, F32)] * 2,
        compiler_params=params(32),
        cost_estimate=cost(
            20 * len(packets) * group * rows * (PLEN + rows) * E, 1 << 24
        ),
        name="attend_head",
    )(*operands)
    return outs[: len(packets)], outs[len(packets) : -3], outs[-3:]


def total_kernel(keep_ref, *rest):
    parts, outs = rest[: -len(MEMBERS)], rest[-len(MEMBERS) :]
    for j, out in enumerate(outs):
        result = keep_ref[j]
        for part in parts:
            result = result + part[j].astype(F32)
        out[...] = result.astype(BF16)


def total(keep, parts):
    return pl.pallas_call(
        total_kernel,
        out_shape=[jax.ShapeDtypeStruct(keep.shape[1:], BF16)] * len(MEMBERS),
        in_specs=[VMEM] * (1 + len(parts)),
        out_specs=[VMEM] * len(MEMBERS),
        compiler_params=params(16),
        cost_estimate=cost(0, 1 << 25),
        name="total_prefix_grads",
    )(keep, *parts)


def prompt_kernel(chunk, members, first, *rest):
    rest = list(rest)
    shares = [rest.pop(0) for _ in members]
    kw_ref, vw_ref = rest.pop(0), rest.pop(0)
    start_ref = None if first else rest.pop(0)
    out_ref, *scratch = rest
    heads, _, _ = place()
    key_grad, value_grad = (
        jnp.concatenate([share[:, at : at + E] for share in shares], axis=1) for at in (0, E)
    )
    copies = []
    for index in range(kw_ref.shape[0] // chunk):
        span = slice(index * chunk, (index + 1) * chunk)
        key_part, value_part = (
            jnp.concatenate([weight[span, lanes(heads[j], E)] for j in members], axis=1)
            for weight in (kw_ref, vw_ref)
        )
        turned = dot(key_part, key_grad, 1, 1) + dot(value_part, value_grad, 1, 1)
        if first:
            out_ref[span, :] = turned
            continue
        out, sems = scratch
        out[:, span] = (turned + start_ref[span, :]).T.astype(BF16)
        copies.append(pltpu.make_async_copy(out.at[:, span], out_ref.at[:, span], sems.at[index]))
        copies[-1].start()
    for copy in copies:
        copy.wait()


def prompt_gradient(members, shares, key_weight, value_weight, start=None, chunk=1024):
    first = start is None
    rows = shares[0].shape[0]
    depth, width = key_weight.shape
    operands = [*shares, key_weight, value_weight] + ([] if first else [start])
    out = jax.ShapeDtypeStruct((depth, rows), F32)
    if not first:
        out = jax.ShapeDtypeStruct((rows, depth), BF16)
    return pl.pallas_call(
        functools.partial(prompt_kernel, chunk, members, first),
        out_shape=out,
        in_specs=[VMEM] * len(operands),
        out_specs=VMEM if first else ANY,
        scratch_shapes=[]
        if first
        else [pltpu.VMEM((rows, depth), BF16), pltpu.SemaphoreType.DMA((depth // chunk,))],
        compiler_params=params(24),
        cost_estimate=cost(2 * rows * depth * width, 2 * depth * width + 2 * rows * depth),
        name="prompt_gradient",
    )(*operands)


def per_device(
    n_prompt,
    n_resp,
    prompt_rows,
    key_weight,
    value_weight,
    queries,
    own_keys,
    own_values,
    out_grad,
    first_length,
    resp_prompt,
):
    devices = n_prompt * n_resp
    every_bit = range(devices.bit_length() - 1)
    line_bits = [bit for bit in GATHER_BITS if bit in every_bit]
    line_bits += [bit for bit in every_bit if bit not in (CORE, X, Y, *line_bits)]
    part = prompt_rows.shape[0]

    def fetch(x, offset):
        pairs = [(i ^ crossed(offset, i >> CORE & 1), i) for i in range(devices)]
        return lax.ppermute(x, ("prompt", "resp"), pairs)

    def give(x, offset):
        pairs = [(i, i ^ crossed(offset, i >> CORE & 1)) for i in range(devices)]
        return lax.ppermute(x, ("prompt", "resp"), pairs)

    other_rows = fetch(prompt_rows, MEMBERS[1])
    first, weights = project(prompt_rows, key_weight, value_weight)
    keep, send = project_other(other_rows, weights, first)
    send, queries = lax.optimization_barrier((send, queries))
    packed = pack(first_length, resp_prompt, queries, out_grad, own_keys, own_values)
    arriving = fetch(send, MEMBERS[2])
    joined = jnp.concatenate([keep, arriving]).reshape(len(MEMBERS), part, -1)
    joined, packed = lax.optimization_barrier((joined, packed))
    packets = [packed[0]] + [fetch(packed[j], MEMBERS[j]) for j in range(1, len(MEMBERS))]

    pieces = {0: joined}
    for bit in line_bits:
        for offset in list(pieces):
            pieces[offset | 1 << bit] = fetch(pieces[offset], 1 << bit)
            if len(pieces) == 2:
                pieces[1 << bit], packets[2] = lax.optimization_barrier(
                    (pieces[1 << bit], packets[2])
                )
    offsets = list(pieces)
    stacks = [
        jnp.stack([pieces[offset] for offset in some]) for some in (offsets[:-1], offsets[-1:])
    ]
    stacks[1], packets = lax.optimization_barrier((stacks[1], packets))
    stacks = [fetch(x, 1 << Y) for x in stacks]

    filled = [0] * n_prompt
    slots = []
    for offset in offsets + [offset | 1 << Y for offset in offsets]:
        places = []
        for member in MEMBERS:
            at = (offset ^ member) // n_resp
            places.append((at, filled[at]))
            filled[at] += 1
        slots.append(tuple(places))
    resp_bits = n_resp.bit_length() - 1
    grads, sums, back_stacks = attend(
        packets, queries.shape[0], list(pieces.values()), stacks, tuple(slots), n_prompt, resp_bits
    )

    sums = dict(zip(offsets, sums))
    far = give(back_stacks[2], 1 << Y)
    middle = give(back_stacks[1], 1 << Y)
    near = give(back_stacks[0], 1 << Y)
    middle, grads = lax.optimization_barrier((middle, grads))
    back = [grads[0]] + [give(grads[j], MEMBERS[j]) for j in range(1, len(MEMBERS))]
    arrived = {offset: [middle[index]] for index, offset in enumerate(offsets[1:-1])}
    arrived.update({offsets[0]: [near[0]], offsets[-1]: [far[0]]})
    line_ahead = offsets[-1] ^ 1 << line_bits[-1]
    for bit in reversed(line_bits):
        for offset in sorted(sums, reverse=True):
            if offset & 1 << bit:
                piece = sums.pop(offset)
                for x in arrived.pop(offset):
                    piece = piece + x.astype(F32)
                if offset == 1 << bit and bit == line_bits[-1]:
                    ahead = arrived[line_ahead]
                    piece, ahead[-1] = lax.optimization_barrier((piece, ahead[-1]))
                arrived[offset ^ 1 << bit].append(give(piece.astype(BF16), 1 << bit))
    unpacked = unpack(back, queries.shape[1], own_keys.shape[1])
    arrived[0], unpacked = lax.optimization_barrier((arrived[0], unpacked))
    query_grad, key_grad, value_grad = unpacked
    blocks = total(sums[0], arrived[0])
    shares = [blocks[0]] + [give(blocks[j], MEMBERS[j]) for j in range(1, len(MEMBERS))]
    start = prompt_gradient((0, 1), shares[:2], key_weight, value_weight)
    prompt_grad = prompt_gradient((2, 3), shares[2:], key_weight, value_weight, start)
    return (query_grad, key_grad, value_grad, prompt_grad)


def solution(mesh):
    both = P(("prompt", "resp"), None)
    return jax.shard_map(
        functools.partial(per_device, mesh.shape["prompt"], mesh.shape["resp"]),
        mesh=mesh,
        in_specs=(both, P(), P(), both, both, both, both, P(("prompt", "resp")), both),
        out_specs=(both, both, both, both),
        check_vma=False,
    )
```
